256 devices in a mesh: grp: 8 (over x_hi, y), dp: 32 (over x_lo, z, core).
Axes of the slice: x: 4 (x_hi: 2, x_lo: 2; x = x_hi * 2 + x_lo), y: 4, z: 8, core: 2. Of those that a mesh axis runs over, the one named last changes fastest.
Arguments:
- gradient_tiles: bfloat16 [8, 1536, 1536], P('grp', 'dp'), may hold values from -1.5 to 1.5
- qa_basis: bfloat16 [8, 2, 1536, 1536], P('grp', None, 'dp'), may hold values from -0.15625 to 0.15625
- qg_basis: bfloat16 [8, 2, 16, 1536, 1536], P('grp', None, None, None, 'dp'), may hold values from -0.15625 to 0.15625
- qa_values: bfloat16 [8, 2, 1536], P('grp'), may hold values from 0.29882812 to 3
- qg_values: bfloat16 [8, 2, 16, 1536], P('grp'), may hold values from 0.29882812 to 3
- layer_owner: int32 [2], replicated, may hold values from 0 to 7
- block_assign: int32 [2, 4], replicated, may hold values from 0 to 15
Outputs:
- preconditioned: bfloat16 [8, 1536, 1536], P('grp')
The draws below stay inside these ranges and needn't reach their ends.
All inputs are finite; a program needn't handle non-finite values.
Results may differ from the reference program's by a relative error of at most 0.0065.
Values may be sent and summed in bfloat16 or wider, within the bound.
A program may use at most 128 MiB of HBM per device.

```python
import math
import jax
import jax.numpy as jnp

B = 1536
LAYERS = 2
QB = 16
TILES = 8
GB = 4
N_GRP = 8


def touch_ends(drawn, stream_key, least, top_value):
    index_at = [jax.random.randint(jax.random.fold_in(stream_key, axis), (), 0, length) for axis, length in enumerate(drawn.shape)]
    widest = drawn.shape.index(max(drawn.shape))
    next_to = index_at[:widest] + [(index_at[widest] + 1) % drawn.shape[widest]] + index_at[widest + 1:]
    return drawn.at[tuple(index_at)].set(least).at[tuple(next_to)].set(top_value)


def level_of(rng, shape, pieces, low, largest):
    def one(position, parts):
        steps = jax.random.uniform(jax.random.fold_in(jax.random.fold_in(rng, 6), position), (parts,), jnp.float32, low / len(pieces), largest / len(pieces))
        return jnp.repeat(jnp.exp(steps), shape[position] // parts).reshape((-1,) + (1,) * (len(shape) - position - 1))

    gain = one(*pieces[0])
    for cut in pieces[1:]:
        gain = gain * one(*cut)
    return gain


def noise(own_key, extent, spread, bound, pieces=(), dtype=jnp.bfloat16):
    result = jax.random.normal(own_key, extent, jnp.float32) * spread
    if len(pieces) > 0:
        result = level_of(own_key, extent, pieces, -0.22, 0.18) * result
    return jnp.clip(result, min=-bound, max=bound).astype(dtype)


def setup_inputs(seed: int = 0) -> dict:
    splits = jax.random.split(jax.random.key(seed), 8)
    gradient_tiles = noise(splits[0], (TILES, B, B), 0.25, 1.5, ((0, 8), (1, 32)))
    qa_basis = noise(splits[1], (N_GRP, LAYERS, B, B), B ** -0.5, 0.15625, ((0, 8), (2, 32)))
    qg_basis = noise(splits[2], (N_GRP, LAYERS, QB, B, B), B ** -0.5, 0.15625, ((0, 8), (4, 32)))
    qa_values = jnp.clip(jnp.exp(math.log(3.0) - 2.306499 * jax.random.uniform(splits[3], (N_GRP, LAYERS, B), jnp.float32) ** level_of(splits[3], (N_GRP, LAYERS, B), ((0, 8),), -0.2, 0.2)), 0.29882812, 3.0).astype(jnp.bfloat16)
    qg_values = jnp.clip(jnp.exp(math.log(3.0) - 2.306499 * jax.random.uniform(splits[4], (N_GRP, LAYERS, QB, B), jnp.float32) ** level_of(splits[4], (N_GRP, LAYERS, QB, B), ((0, 8),), -0.2, 0.2)), 0.29882812, 3.0).astype(jnp.bfloat16)
    layer_owner = jax.random.randint(splits[5], (LAYERS,), 0, N_GRP).astype(jnp.int32)
    block_assign = touch_ends(jax.random.randint(splits[6], (LAYERS, GB), 0, QB), jax.random.fold_in(splits[6], 1), 0, QB - 1).astype(jnp.int32)
    return {"gradient_tiles": gradient_tiles, "qa_basis": qa_basis, "qg_basis": qg_basis, "qa_values": qa_values, "qg_values": qg_values, "layer_owner": layer_owner, "block_assign": block_assign}


DAMPING = 0.1


def precondition(tile, input_basis, output_basis, input_values, output_values):
    rotated_in = jnp.dot(tile, input_basis, preferred_element_type=jnp.float32).astype(jnp.bfloat16)
    eigen_coords = jnp.dot(output_basis.T, rotated_in, preferred_element_type=jnp.float32)
    denominator = output_values.astype(jnp.float32)[:, None] * input_values.astype(jnp.float32)[None, :] + DAMPING
    scaled = (eigen_coords / denominator).astype(jnp.bfloat16)
    back_in = jnp.dot(scaled, input_basis.T, preferred_element_type=jnp.float32).astype(jnp.bfloat16)
    return jnp.dot(output_basis, back_in, preferred_element_type=jnp.float32).astype(jnp.bfloat16)


def reference(gradient_tiles, qa_basis, qg_basis, qa_values, qg_values, layer_owner, block_assign):
    results = []
    for tile_index in range(TILES):
        layer_index = tile_index // GB
        slot_index = tile_index % GB
        owner_index = layer_owner[layer_index]
        block_index = block_assign[layer_index, slot_index]
        results.append(precondition(gradient_tiles[tile_index], qa_basis[owner_index, layer_index],
                                    qg_basis[owner_index, layer_index, block_index],
                                    qa_values[owner_index, layer_index],
                                    qg_values[owner_index, layer_index, block_index]))
    return jnp.stack(results)
```

```python
import functools

import jax
import jax.numpy as jnp
from jax import lax
from jax.experimental import pallas as pl
from jax.experimental.pallas import tpu as pltpu
from jax.sharding import PartitionSpec as P

MESH = pl.DeviceIdType.MESH
DAMPING = 0.1
NZ = 8
STRIP = 48
PIECE = 16
WIDTH = 1536
LANES = 128
N_DP = 32
HALF = WIDTH // 2
QUARTER = WIDTH // 4
TILE = 256
N_SEM = 256


def works(x, z):
    return (z + 2 * x) % 4 != 3


def rank(x, z):
    return x * 6 + z - (z + 2 * x) // 4


def kernel(
    owner_hbm, assign_hbm, g_hbm, a_hbm, q_hbm, lg_hbm, la_hbm, out_ref,
    owner_ref, assign_ref, lgv, lav, g, a, av, qv, qsel, qr_low, qr_high, qs, qt, qx, qc, ax, ay, vsel, vy, vx, vc, fg, fa, fq, p, lgc, sc, bp, bo, bi, bk, bc, bt,
    ssem, rsem, lsem, b_recv,
):
    member = lax.axis_index("grp")
    dp = lax.axis_index("dp")
    xh, y = member // 4, member % 4
    x, z, c = dp // 16, (dp // 2) % NZ, dp % 2

    load_g = [
        pltpu.make_async_copy(g_hbm.at[:, n * QUARTER:(n + 1) * QUARTER], g.at[n], lsem.at[7 + n]) for n in range(4)
    ]
    load_a = pltpu.make_async_copy(a_hbm, av, lsem.at[1])
    load_q = pltpu.make_async_copy(q_hbm, qv, lsem.at[2])
    loads = [
        pltpu.make_async_copy(src, dst, lsem.at[3 + n])
        for n, (src, dst) in enumerate(
            ((owner_hbm, owner_ref), (assign_hbm, assign_ref), (lg_hbm, lgv), (la_hbm, lav))
        )
    ]
    load_a.start()
    for load in load_g:
        load.start()
    for load in loads:
        load.start()
    load_q.start()
    core0 = c == 0

    def dev(gx, gy, dx, dz, dc):
        return (gx * 4 + gy, dx * 16 + dz * 2 + dc)

    sibling = dev(xh, y, x, z, 1 - c)
    across = dev(xh, y, 1 - x, z, c)
    up = dev(xh, y, x, (z + 1) % NZ, c)
    down = dev(xh, y, x, (z + NZ - 1) % NZ, c)
    across_other = dev(xh, y, 1 - x, z, 1 - c)
    up_other = dev(xh, y, x, (z + 1) % NZ, 1 - c)
    down_other = dev(xh, y, x, (z + NZ - 1) % NZ, 1 - c)
    partner = dev(1 - xh, y, x, z, c)

    barrier = pltpu.get_barrier_semaphore()

    near = [sibling, across, across_other, up, down, up_other, down_other, partner]
    near += [(xh * 4 + (y + k) % 4, dp) for k in range(1, 4)]
    for target in near:
        pl.semaphore_signal(barrier, inc=1, device_id=target, device_id_type=MESH)
    pl.semaphore_wait(barrier, len(near))

    count = [0]
    pending = []

    def number():
        count[0] += 1
        assert count[0] <= N_SEM
        return count[0] - 1

    def copy(m, src, dst, target):
        return pltpu.make_async_remote_copy(
            src_ref=src, dst_ref=dst, send_sem=ssem.at[m], recv_sem=rsem.at[m],
            device_id=target, device_id_type=MESH,
        )

    def send(m, src, dst, target, when=None):
        started = copy(m, src, dst, target)
        pending.append((started, when))
        if when is None:
            started.start()
        else:
            pl.when(when)(started.start)

    def drain(until=None):
        for started, when in pending[:until]:
            if when is None:
                started.wait_send()
            else:
                pl.when(when)(started.wait_send)
        del pending[:until]

    def arrive(m, dst, target, when=None):
        landed = copy(m, dst, dst, target)
        if when is None:
            landed.wait_recv()
        else:
            pl.when(when)(landed.wait_recv)

    class Gather:
        def __init__(self, ref, full, half=None, exists=None):
            self.ref, self.full, self.cut, self.mid = ref, full, full // 2, full // 4
            self.half = half or (lambda bx, bz, bc, to: ref(bx, bz, bc, 0, full))
            self.exists = exists or (lambda bx, bz: None)
            self.sib_waits = []
            self.m = {}

        def key(self, *name):
            if name not in self.m:
                self.m[name] = number()
            return self.m[name]

        def to_sibling(self, bx, bz):
            m = number()
            ref = self.half(bx, bz, c, 1 - c)
            send(m, ref, ref, sibling, self.exists(bx, bz))
            self.sib_waits.append((m, self.half(bx, bz, 1 - c, c), self.exists(bx, bz)))

        def move(self, name, target, bx, bz, first, last):
            ref = self.ref(bx, bz, c, first, last)
            send(self.key(*name), ref, ref, target, self.exists(bx, bz))

        def wait(self, name, bx, bz, first, last, bc=c):
            arrive(self.key(*name), self.ref(bx, bz, bc, first, last), sibling, self.exists(bx, bz))

        def low(self, name, target, bx, bz):
            self.move(name, target, bx, bz, 0, self.cut)

        def high(self, name, target, bx, bz):
            self.move(name, target, bx, bz, self.cut, self.full)

        def wait_low(self, name, bx, bz):
            self.wait(name, bx, bz, 0, self.cut)

        def wait_high(self, name, bx, bz):
            self.wait(name, bx, bz, self.cut, self.full)

        def begin_low(self):
            self.low(("x", 0), across, x, z)
            self.low(("ul", 1), up, x, z)
            self.low(("dl", 1), down, x, z)

        def begin_high(self):
            self.high(("uh", 1), up, x, z)
            self.high(("dh", 1), down, x, z)
            self.high(("xh", 0), across, x, z)
            self.to_sibling(x, z)

        def begin(self):
            self.low(("x", 0), across, x, z)
            self.high(("uh", 1), up, x, z)
            self.high(("dh", 1), down, x, z)
            self.low(("ul", 1), up, x, z)
            self.low(("dl", 1), down, x, z)
            self.high(("xh", 0), across, x, z)
            self.paired = self.whole(x)

        def whole(self, bx):
            m = number()
            ref = self.ref(bx, z, c, 0, self.full)
            send(m, ref, ref, sibling)
            return m, self.ref(bx, z, 1 - c, 0, self.full)

        def swap(self):
            self.wait_low(("x", 0), 1 - x, z)
            self.low(("uq", 1), up, 1 - x, z)
            self.low(("dq", 1), down, 1 - x, z)

        def from_x(self):
            self.wait_high(("xh", 0), 1 - x, z)
            if self is gq:
                self.crossing = self.whole(1 - x)
            else:
                self.to_sibling(1 - x, z)

        def step(self, s):
            lo, hi = (z + NZ - s) % NZ, (z + s) % NZ
            self.wait_high(("uh", s), x, lo)
            self.high(("uh", s + 1), up, x, lo)
            self.high(("xu", s), across, x, lo)
            self.wait_high(("dh", s), x, hi)
            if s < 3:
                self.high(("dh", s + 1), down, x, hi)
            self.high(("xd", s), across, x, hi)
            self.wait_low(("ul", s), x, lo)
            if s < 3:
                self.low(("ul", s + 1), up, x, lo)
            self.wait_low(("dl", s), x, hi)
            self.low(("dl", s + 1), down, x, hi)
            self.wait_low(("uq", s), 1 - x, lo)
            if s < 3:
                self.low(("uq", s + 1), up, 1 - x, lo)
            else:
                self.move(("uq", 4), up, 1 - x, lo, 0, self.mid)
                self.move(("uc", 4), up_other, 1 - x, lo, 0, self.mid)
            self.wait_low(("dq", s), 1 - x, hi)
            if s < 3:
                self.low(("dq", s + 1), down, 1 - x, hi)
            else:
                self.move(("dq", 4), down, 1 - x, hi, self.mid, self.cut)
                self.move(("dc", 4), down_other, 1 - x, hi, self.mid, self.cut)
            self.to_sibling(x, lo)
            self.to_sibling(x, hi)
            if s == 2 and self is not gq:
                self.from_x()
            if s > 1:
                self.crossed(s - 1)

        def crossed(self, s):
            lo, hi = (z + NZ - s) % NZ, (z + s) % NZ
            self.wait_high(("xu", s), 1 - x, lo)
            self.to_sibling(1 - x, lo)
            self.wait_high(("xd", s), 1 - x, hi)
            self.to_sibling(1 - x, hi)

        def last(self):
            far = (z + 4) % NZ
            self.wait_high(("uh", 4), x, far)
            self.high(("xu", 4), across, x, far)
            self.high(("xc", 4), across_other, x, far)
            self.wait_low(("dl", 4), x, far)
            self.to_sibling(x, far)
            self.crossed(3)
            self.wait(("uq", 4), 1 - x, far, 0, self.mid)
            self.wait(("dq", 4), 1 - x, far, self.mid, self.cut)
            self.wait_high(("xu", 4), 1 - x, far)

        def end(self):
            far = (z + 4) % NZ
            for m, ref, when in self.sib_waits:
                arrive(m, ref, sibling, when)
            self.wait(("uc", 4), 1 - x, far, 0, self.mid, 1 - c)
            self.wait(("dc", 4), 1 - x, far, self.mid, self.cut, 1 - c)
            self.wait(("xc", 4), 1 - x, far, self.cut, self.full, 1 - c)

    def strip_at(bz, bc):
        return pl.ds(pl.multiple_of((bz * 2 + bc) * STRIP, PIECE), STRIP)

    def strip_of(bz):
        return pl.ds(pl.multiple_of(bz * STRIP, PIECE), STRIP)

    def at_z(bz):
        return pl.ds(pl.multiple_of(bz * 2 * STRIP, PIECE), 2 * STRIP)

    def half_of(core):
        return pl.ds(pl.multiple_of(core * HALF, LANES), HALF)

    class Ring:
        def __init__(self, f):
            self.f = f
            self.m = {}
            self.m4 = [number() for _ in range(3)]

        def share(self, strip):
            self.f[x, strip_at(z, c), :] = strip[x * 2 + c]
            for n, (dx, dc) in enumerate(((1, 0), (1, 1), (0, 1))):
                bx, bc = (x + dx) % 2, (c + dc) % 2
                send(self.m4[n], strip.at[bx * 2 + bc], self.f.at[x, strip_at(z, c), :], dev(xh, y, bx, z, bc))

        def begin(self):
            for n, (dx, dc) in enumerate(((1, 0), (1, 1), (0, 1))):
                bx, bc = (x + dx) % 2, (c + dc) % 2
                arrive(self.m4[n], self.f.at[bx, strip_at(z, bc), :], sibling)
            for n in range(2):
                self.move("u", 1, n, up, z)
                self.move("d", 1, n, down, z)

        def move(self, way, s, n, target, bz):
            ref = self.f.at[n, at_z(bz), :]
            self.m[way, s, n] = number()
            send(self.m[way, s, n], ref, ref, target)

        def wait(self, way, s, n, bz):
            arrive(self.m[way, s, n], self.f.at[n, at_z(bz), :], sibling)

        def step(self, s):
            lo, hi = (z + NZ - s) % NZ, (z + s) % NZ
            for n in range(2):
                self.wait("u", s, n, lo)
                if s < 3 or n == 0:
                    self.move("u", s + 1, n, up, lo)
                self.wait("d", s, n, hi)
                if s < 3 or n == 1:
                    self.move("d", s + 1, n, down, hi)

        def last(self):
            far = (z + 4) % NZ
            self.wait("u", 4, 0, far)
            self.wait("d", 4, 1, far)

    def by_strips(bx, bz, bc, first, last):
        return fq.at[bc, bx, strip_of(bz), first:last]

    def by_columns(bx, bz, bc, first, last):
        cols = pl.ds(pl.multiple_of(rank(bx, bz) * LANES, LANES), LANES)
        return out_ref.at[pl.ds(pl.multiple_of(bc * HALF + first, PIECE), last - first), cols]

    gg = Ring(fg)
    ga = Ring(fa)
    gq = Gather(
        by_strips, WIDTH, half=lambda bx, bz, bc, to: fq.at[bc, bx, strip_of(bz), half_of(to)]
    )
    go = Gather(by_columns, HALF, exists=lambda bx, bz: works(bx, bz))

    own = pl.ds(pl.multiple_of(dp * STRIP, PIECE), STRIP)

    load_a.wait()
    m_ax = number()
    send(m_ax, av.at[1 - xh], ax.at[1], partner)
    for load in load_g:
        load.wait()
    gg.share(g)
    ax[0] = av[xh]

    for load in loads:
        load.wait()
    owner = owner_ref[xh]
    other = owner_ref[1 - xh]
    is_far = lax.bitwise_xor(lax.shift_right_logical(owner, 2), xh)
    owner_y = lax.bitwise_and(owner, 3)
    other_y = lax.bitwise_and(other, 3)
    load_q.wait()
    for layer in range(2):
        for slot in range(4):
            qsel[layer, slot] = qv[layer, assign_ref[layer, slot]]
    y_up, y_down = (xh * 4 + (y + 1) % 4, dp), (xh * 4 + (y + 3) % 4, dp)
    far, above, below = (y + 2) % 4, (y + 1) % 4, (y + 3) % 4
    m_q1, m_q2 = [number() for _ in range(2)], [number() for _ in range(2)]
    send(m_q1[0], qsel.at[:, far, :, :HALF], qr_low.at[:, 1], y_up)
    send(m_q1[1], qsel.at[:, far, :, HALF:], qr_high.at[:, 1], y_down)
    gg.begin()

    for layer in range(2):
        qr_low[layer, 0] = qsel[layer, above, :, :HALF]
        qr_high[layer, 0] = qsel[layer, below, :, HALF:]
        qt[layer, 0] = qsel[layer, y]
    owners_y = [lax.bitwise_and(owner_ref[layer], 3) for layer in range(2)]

    def one_if(condition):
        return jnp.where(condition, 1, 0)

    arrive(m_q1[0], qr_low.at[:, 1], y_down)
    for layer in range(2):
        qs[0, layer, :, :HALF] = qr_low[layer, one_if(owners_y[layer] == below)]
        qs[0, layer, :, HALF:] = qsel[layer, above, :, HALF:]
    send(m_q2[0], qs.at[0], qt.at[:, 1], y_up)
    arrive(m_q1[1], qr_high.at[:, 1], y_up)
    for layer in range(2):
        qs[1, layer, :, :HALF] = qsel[layer, below, :, :HALF]
        qs[1, layer, :, HALF:] = qr_high[layer, one_if(owners_y[layer] == above)]
    send(m_q2[1], qs.at[1], qt.at[:, 2], y_down)

    arrive(m_ax, ax.at[1], partner)
    ay[y] = ax[is_far]
    m_a1, m_a2 = [number() for _ in range(2)], [number() for _ in range(2)]
    send(m_a1[0], ay.at[y], ay.at[y], y_up)
    send(m_a1[1], ay.at[y], ay.at[y], y_down)

    m_vy = [number() for _ in range(3)]
    for layer in range(2):
        la_all = lav[...].astype(jnp.float32)[layer:layer + 1]
        lg_all = lgv[layer].astype(jnp.float32)
        at_row = lax.broadcasted_iota(jnp.int32, lg_all.shape, 0)
        for slot in range(4):
            lg = jnp.sum(jnp.where(at_row == assign_ref[layer, slot], lg_all, 0.0), axis=0, keepdims=True)
            for n in range(WIDTH // LANES):
                cols = slice(n * LANES, (n + 1) * LANES)
                vsel[slot, layer, 0, n:n + 1] = lg[:, cols]
                vsel[slot, layer, 1, n:n + 1] = la_all[:, cols]
    vy[y] = vsel[y]
    for k in range(1, 4):
        to = (y + k) % 4
        send(m_vy[k - 1], vsel.at[to], vy.at[y], (xh * 4 + to, dp))
    gg.step(1)
    arrive(m_a1[0], ay.at[below], y_down)
    send(m_a2[0], ay.at[below, :, :HALF], ay.at[below, :, :HALF], y_up)
    arrive(m_a1[1], ay.at[above], y_up)
    send(m_a2[1], ay.at[above, :, HALF:], ay.at[above, :, HALF:], y_down)
    gg.step(2)

    arrive(m_q2[0], qt.at[:, 1], y_down)
    arrive(m_q2[1], qt.at[:, 2], y_up)
    for k in range(1, 4):
        arrive(m_vy[k - 1], vy.at[(y + 4 - k) % 4], partner)

    def came(layer, column_half):
        away = lax.bitwise_and(lax.bitwise_and(owner_ref[layer], 3) + 4 - y, 3)
        by_below = (away >= 2) if column_half == 0 else (away == 3)
        return jnp.where(away == 0, 0, jnp.where(by_below, 1, 2))

    m_qx, m_vx = number(), number()
    for n in range(2):
        half = slice(n * HALF, (n + 1) * HALF)
        qc[:, half] = qt[1 - xh, came(1 - xh, n), :, half]
    send(m_qx, qc, qx.at[1], partner)
    vc[...] = vy[other_y, 1 - xh]
    send(m_vx, vc, vx.at[1], partner)
    for n in range(2):
        half = slice(n * HALF, (n + 1) * HALF)
        qx[0, :, half] = qt[xh, came(xh, n), :, half]
    vx[0] = vy[owner_y, xh]

    arrive(m_a2[0], ay.at[far, :, :HALF], y_down)
    arrive(m_a2[1], ay.at[far, :, HALF:], y_up)
    strip_a = ay[owner_y]
    for n in range(4):
        a[n] = strip_a[:, n * QUARTER:(n + 1) * QUARTER]
    ga.share(a)
    gg.step(3)
    arrive(m_qx, qx.at[1], partner)
    fq[c, x, strip_of(z), :] = qx[is_far]
    gq.begin()
    ga.begin()
    gg.last()
    gq.swap()
    arrive(m_vx, vx.at[1], partner)
    for n in range(WIDTH // LANES):
        lg_row = vx[is_far, 0, n:n + 1, :]
        lgc[n * LANES:(n + 1) * LANES, :] = jnp.transpose(jnp.broadcast_to(lg_row, (LANES, LANES)))
    ga.step(1)
    gq.from_x()
    gq.step(1)
    ga.step(2)

    arrive(*gq.paired, sibling)
    arrive(*gq.crossing, sibling)

    def flat(value):
        return value.reshape((-1, value.shape[-1]))

    p[x * 2 + c] = jnp.dot(
        flat(fq[:, :, strip_of(z), :]), flat(fg[...]), preferred_element_type=jnp.float32
    ).astype(jnp.bfloat16)
    m_p = [number() for _ in range(3)]
    p_own, p_far = p.at[x * 2 + c], p.at[(1 - x) * 2 + c]
    send(m_p[0], p_own, p_own, across)
    send(m_p[1], p_own, p_own, sibling)
    ga.step(3)
    arrive(m_p[0], p_far, across)
    send(m_p[2], p_far, p_far, sibling)
    gq.step(2)
    ga.last()

    arrive(m_p[1], p.at[x * 2 + 1 - c], sibling)
    arrive(m_p[2], p.at[(1 - x) * 2 + 1 - c], sibling)
    eigen = sum(
        jnp.dot(p[n], fa[n // 2, n % 2 * QUARTER:(n % 2 + 1) * QUARTER, :], preferred_element_type=jnp.float32)
        for n in range(4)
    )
    lg_col = jnp.concatenate([lgc[pl.ds(pl.multiple_of(bx * HALF + (z * 2 + bc) * STRIP, PIECE), STRIP), :]
                              for bc in range(2) for bx in range(2)])
    for n in range(QUARTER // LANES):
        la_row = vx[is_far, 1, pl.ds((x * 2 + c) * (QUARTER // LANES) + n, 1), :]
        cols = slice(n * LANES, (n + 1) * LANES)
        sc[:, cols] = (eigen[:, cols] / (lg_col * la_row + DAMPING)).astype(jnp.bfloat16)

    for bx in range(2):
        for n in range(2):
            rows = slice(n * QUARTER, (n + 1) * QUARTER)
            part = lax.dot_general(
                sc[...], fa[bx, rows, :], (((1,), (1,)), ((), ())), preferred_element_type=jnp.float32
            ).reshape((2, 2, STRIP, QUARTER))
            cols = slice(bx * HALF + n * QUARTER, bx * HALF + (n + 1) * QUARTER)
            bp[:, :, :, cols] = part
            bo[:, :, :, cols] = part.astype(jnp.bfloat16)
    m_b = number()
    send(m_b, bo.at[1 - c], bi, sibling)
    gq.step(3)
    arrive(m_b, bi, sibling)
    done = (bp[c] + bi[...].astype(jnp.float32)).astype(jnp.bfloat16)
    for j in range(WIDTH // LANES):
        bk[j] = done[:, :, j * LANES:(j + 1) * LANES]

    for wx in range(2):
        for wz in range(NZ):
            if (wz + 2 * wx) % 4 == 3:
                continue
            part = bk.at[wx * 6 + wz - (wz + 2 * wx) // 4]
            to_self = jnp.logical_and(x == wx, z == wz)
            others = jnp.logical_not(to_self)
            started = pltpu.make_async_remote_copy(
                src_ref=part, dst_ref=bc.at[x, :, strip_of(z), :], send_sem=ssem.at[number()],
                recv_sem=b_recv.at[x * NZ + z], device_id=dev(xh, y, wx, wz, c), device_id_type=MESH,
            )
            pl.when(others)(started.start)
            pending.append((started, others))

            @pl.when(to_self)
            def _():
                bc[x, :, strip_of(z), :] = part[...]

    gq.last()
    is_worker = works(x, z)
    m_bt = number()

    @pl.when(is_worker)
    def _():
        def take(k, carry):
            n = (x * NZ + z + k) % 16
            block = bc.at[n // NZ, :, strip_of(n % NZ), :]
            pltpu.make_async_remote_copy(
                src_ref=block, dst_ref=block, send_sem=ssem.at[m_bt], recv_sem=b_recv.at[n],
                device_id=sibling, device_id_type=MESH,
            ).wait_recv()
            return carry

        lax.fori_loop(1, 16, take, 0)
        total = flat(bc[0].astype(jnp.float32) + bc[1].astype(jnp.float32))
        for n in range(HALF // LANES):
            cols = slice(n * LANES, (n + 1) * LANES)
            bt[c, :, cols] = jnp.transpose(total[cols, :]).astype(jnp.bfloat16)

    send(m_bt, bt.at[c], bt.at[c], sibling, is_worker)
    gq.end()
    arrive(m_bt, bt.at[1 - c], sibling, is_worker)

    mine = pl.ds(pl.multiple_of(rank(x, z) * LANES, LANES), LANES)

    def finish(n):
        @pl.when(is_worker)
        def _():
            rows = pl.ds(pl.multiple_of(c * HALF + n * QUARTER, LANES), QUARTER)
            part = sum(
                jnp.dot(bt[k], flat(fq[k, :, :, rows]), preferred_element_type=jnp.float32) for k in range(2)
            )
            out_ref[rows, mine] = jnp.transpose(part).astype(jnp.bfloat16)

    finish(0)
    go.begin_low()
    finish(1)
    go.begin_high()
    drain()
    go.swap()
    go.step(1)
    early = len(pending)
    go.step(2)
    go.step(3)
    drain(early)
    go.last()
    go.end()
    drain()


def local(gradient_tiles, qa_basis, qg_basis, qa_values, qg_values, layer_owner, block_assign):
    strip = (STRIP, WIDTH)
    bf = jnp.bfloat16
    f32 = jnp.float32
    out = pl.pallas_call(
        kernel,
        out_shape=jax.ShapeDtypeStruct((WIDTH, WIDTH), bf),
        in_specs=[pl.BlockSpec(memory_space=pltpu.HBM)] * 7,
        out_specs=pl.BlockSpec(memory_space=pltpu.VMEM),
        scratch_shapes=[
            pltpu.SMEM((2,), jnp.int32),
            pltpu.SMEM((2, 4), jnp.int32),
            pltpu.VMEM((2, 16, WIDTH), bf),
            pltpu.VMEM((2, WIDTH), bf),
            pltpu.VMEM((4, STRIP, QUARTER), bf),
            pltpu.VMEM((4, STRIP, QUARTER), bf),
            pltpu.VMEM((2,) + strip, bf),
            pltpu.VMEM((2, 16) + strip, bf),
            pltpu.VMEM((2, 4) + strip, bf),
            pltpu.VMEM((2, 2, STRIP, HALF), bf),
            pltpu.VMEM((2, 2, STRIP, HALF), bf),
            pltpu.VMEM((2, 2) + strip, bf),
            pltpu.VMEM((2, 3) + strip, bf),
            pltpu.VMEM((2,) + strip, bf),
            pltpu.VMEM(strip, bf),
            pltpu.VMEM((2,) + strip, bf),
            pltpu.VMEM((4,) + strip, bf),
            pltpu.VMEM((4, 2, 2, 16, LANES), f32),
            pltpu.VMEM((4, 2, 2, 16, LANES), f32),
            pltpu.VMEM((2, 2, 16, LANES), f32),
            pltpu.VMEM((2, 16, LANES), f32),
            pltpu.VMEM((2, HALF, QUARTER), bf),
            pltpu.VMEM((2, HALF, QUARTER), bf),
            pltpu.VMEM((2, 2, HALF // 2, WIDTH), bf),
            pltpu.VMEM((4, 4 * STRIP, QUARTER), bf),
            pltpu.VMEM((WIDTH, LANES), f32),
            pltpu.VMEM((4 * STRIP, QUARTER), bf),
            pltpu.VMEM((2, 2) + strip, f32),
            pltpu.VMEM((2, 2) + strip, bf),
            pltpu.VMEM((2,) + strip, bf),
            pltpu.VMEM((12, 2, STRIP, LANES), bf),
            pltpu.VMEM((2, 2, HALF // 2, LANES), bf),
            pltpu.VMEM((2, LANES, HALF), bf),
            pltpu.SemaphoreType.DMA((N_SEM,)),
            pltpu.SemaphoreType.DMA((N_SEM,)),
            pltpu.SemaphoreType.DMA((11,)),
            pltpu.SemaphoreType.DMA((16,)),
        ],
        compiler_params=pltpu.CompilerParams(
            collective_id=0, has_side_effects=True, vmem_limit_bytes=48 * 1024 * 1024
        ),
        cost_estimate=pl.CostEstimate(flops=4 * 2 * 48 * 1536 * 1536, bytes_accessed=10_000_000, transcendentals=0),
    )(
        *(
            pltpu.with_memory_space_constraint(operand, pltpu.HBM)
            for operand in (
                layer_owner, block_assign, gradient_tiles[0], qa_basis[0], jnp.swapaxes(qg_basis[0], -1, -2),
                qg_values[0], qa_values[0],
            )
        )
    )
    return out[None]


def solution(mesh):
    in_specs = (
        P("grp", "dp", None),
        P("grp", None, "dp", None),
        P("grp", None, None, None, "dp"),
        P("grp", None, None),
        P("grp", None, None, None),
        P(),
        P(),
    )
    out_specs = P("grp", None, None)
    return jax.shard_map(local, mesh=mesh, in_specs=in_specs, out_specs=out_specs, check_vma=False)
```

```python
import functools

import jax
import jax.numpy as jnp
from jax import lax
from jax.experimental import pallas as pl
from jax.experimental.pallas import tpu as pltpu
from jax.sharding import PartitionSpec as P

MESH = pl.DeviceIdType.MESH
DAMPING = 0.1
NZ = 8
STRIP = 48
PIECE = 16
WIDTH = 1536
LANES = 128
N_DP = 32
HALF = WIDTH // 2
QUARTER = WIDTH // 4
TILE = 256
N_SEM = 256


def works(x, z):
    return (z + 2 * x) % 4 != 3


def rank(x, z):
    return x * 6 + z - (z + 2 * x) // 4


def kernel(
    owner_hbm, assign_hbm, g_hbm, a_hbm, q_hbm, lg_hbm, la_hbm, out_ref,
    owner_ref, assign_ref, lgv, lav, g, av, qv, qsel, qr_low, qr_high, qs, qt, qx, qc, aq, ac, ax, vsel, vy, vx, vc, fg, fa, fq, p, lgc, sc, bp, bo, bi, bk, bc, bt,
    ssem, rsem, lsem, a_recv, b_recv,
):
    member = lax.axis_index("grp")
    dp = lax.axis_index("dp")
    xh, y = member // 4, member % 4
    x, z, c = dp // 16, (dp // 2) % NZ, dp % 2

    load_g = [
        pltpu.make_async_copy(g_hbm.at[:, n * QUARTER:(n + 1) * QUARTER], g.at[n], lsem.at[7 + n]) for n in range(4)
    ]
    load_a = [
        pltpu.make_async_copy(a_hbm.at[:, :, n * QUARTER:(n + 1) * QUARTER], av.at[n], lsem.at[11 + n])
        for n in range(4)
    ]
    load_q = pltpu.make_async_copy(q_hbm, qv, lsem.at[2])
    loads = [
        pltpu.make_async_copy(src, dst, lsem.at[3 + n])
        for n, (src, dst) in enumerate(
            ((owner_hbm, owner_ref), (assign_hbm, assign_ref), (lg_hbm, lgv), (la_hbm, lav))
        )
    ]
    for load in load_a:
        load.start()
    for load in load_g:
        load.start()
    for load in loads:
        load.start()
    load_q.start()
    core0 = c == 0

    def dp_of(dx, dz, dc):
        return dx * 16 + dz * 2 + dc

    def dev(gx, gy, dx, dz, dc):
        return (gx * 4 + gy, dp_of(dx, dz, dc))

    sibling = dev(xh, y, x, z, 1 - c)
    across = dev(xh, y, 1 - x, z, c)
    up = dev(xh, y, x, (z + 1) % NZ, c)
    down = dev(xh, y, x, (z + NZ - 1) % NZ, c)
    across_other = dev(xh, y, 1 - x, z, 1 - c)
    up_other = dev(xh, y, x, (z + 1) % NZ, 1 - c)
    down_other = dev(xh, y, x, (z + NZ - 1) % NZ, 1 - c)
    partner = dev(1 - xh, y, x, z, c)

    barrier = pltpu.get_barrier_semaphore()

    near = [up, down, up_other, down_other, partner]
    near += [
        dev(xh, (y + k // 4) % 4, (x + k // 2) % 2, z, (c + k) % 2) for k in range(1, 16)
    ]
    for target in near:
        pl.semaphore_signal(barrier, inc=1, device_id=target, device_id_type=MESH)
    pl.semaphore_wait(barrier, len(near))

    count = [0]
    pending = []

    def number():
        count[0] += 1
        assert count[0] <= N_SEM
        return count[0] - 1

    def copy(m, src, dst, target):
        return pltpu.make_async_remote_copy(
            src_ref=src, dst_ref=dst, send_sem=ssem.at[m], recv_sem=rsem.at[m],
            device_id=target, device_id_type=MESH,
        )

    def send(m, src, dst, target, when=None):
        started = copy(m, src, dst, target)
        pending.append((started, when))
        if when is None:
            started.start()
        else:
            pl.when(when)(started.start)

    def drain(until=None):
        for started, when in pending[:until]:
            if when is None:
                started.wait_send()
            else:
                pl.when(when)(started.wait_send)
        del pending[:until]

    def arrive(m, dst, target, when=None):
        landed = copy(m, dst, dst, target)
        if when is None:
            landed.wait_recv()
        else:
            pl.when(when)(landed.wait_recv)

    class Gather:
        def __init__(self, ref, full, half=None, exists=None):
            self.ref, self.full, self.cut, self.mid = ref, full, full // 2, full // 4
            self.half = half or (lambda bx, bz, bc, to: ref(bx, bz, bc, 0, full))
            self.exists = exists or (lambda bx, bz: None)
            self.sib_waits = []
            self.m = {}

        def key(self, *name):
            if name not in self.m:
                self.m[name] = number()
            return self.m[name]

        def to_sibling(self, bx, bz):
            m = number()
            ref = self.half(bx, bz, c, 1 - c)
            send(m, ref, ref, sibling, self.exists(bx, bz))
            self.sib_waits.append((m, self.half(bx, bz, 1 - c, c), self.exists(bx, bz)))

        def move(self, name, target, bx, bz, first, last):
            ref = self.ref(bx, bz, c, first, last)
            send(self.key(*name), ref, ref, target, self.exists(bx, bz))

        def wait(self, name, bx, bz, first, last, bc=c):
            arrive(self.key(*name), self.ref(bx, bz, bc, first, last), sibling, self.exists(bx, bz))

        def low(self, name, target, bx, bz):
            self.move(name, target, bx, bz, 0, self.cut)

        def high(self, name, target, bx, bz):
            self.move(name, target, bx, bz, self.cut, self.full)

        def wait_low(self, name, bx, bz):
            self.wait(name, bx, bz, 0, self.cut)

        def wait_high(self, name, bx, bz):
            self.wait(name, bx, bz, self.cut, self.full)

        def begin_low(self):
            self.low(("x", 0), across, x, z)
            self.low(("ul", 1), up, x, z)
            self.low(("dl", 1), down, x, z)

        def begin_high(self):
            self.high(("uh", 1), up, x, z)
            self.high(("dh", 1), down, x, z)
            self.high(("xh", 0), across, x, z)
            self.to_sibling(x, z)

        def begin(self):
            self.low(("x", 0), across, x, z)
            self.high(("uh", 1), up, x, z)
            self.high(("dh", 1), down, x, z)
            self.low(("ul", 1), up, x, z)
            self.low(("dl", 1), down, x, z)
            self.high(("xh", 0), across, x, z)
            self.paired = self.whole(x)

        def whole(self, bx):
            m = number()
            ref = self.ref(bx, z, c, 0, self.full)
            send(m, ref, ref, sibling)
            return m, self.ref(bx, z, 1 - c, 0, self.full)

        def swap(self):
            self.wait_low(("x", 0), 1 - x, z)
            self.low(("uq", 1), up, 1 - x, z)
            self.low(("dq", 1), down, 1 - x, z)

        def from_x(self):
            self.wait_high(("xh", 0), 1 - x, z)
            if self is gq:
                self.crossing = self.whole(1 - x)
            else:
                self.to_sibling(1 - x, z)

        def step(self, s):
            lo, hi = (z + NZ - s) % NZ, (z + s) % NZ
            self.wait_high(("uh", s), x, lo)
            self.high(("uh", s + 1), up, x, lo)
            self.high(("xu", s), across, x, lo)
            self.wait_high(("dh", s), x, hi)
            if s < 3:
                self.high(("dh", s + 1), down, x, hi)
            self.high(("xd", s), across, x, hi)
            self.wait_low(("ul", s), x, lo)
            if s < 3:
                self.low(("ul", s + 1), up, x, lo)
            self.wait_low(("dl", s), x, hi)
            self.low(("dl", s + 1), down, x, hi)
            self.wait_low(("uq", s), 1 - x, lo)
            if s < 3:
                self.low(("uq", s + 1), up, 1 - x, lo)
            else:
                self.move(("uq", 4), up, 1 - x, lo, 0, self.mid)
                self.move(("uc", 4), up_other, 1 - x, lo, 0, self.mid)
            self.wait_low(("dq", s), 1 - x, hi)
            if s < 3:
                self.low(("dq", s + 1), down, 1 - x, hi)
            else:
                self.move(("dq", 4), down, 1 - x, hi, self.mid, self.cut)
                self.move(("dc", 4), down_other, 1 - x, hi, self.mid, self.cut)
            self.to_sibling(x, lo)
            self.to_sibling(x, hi)
            if s == 2 and self is not gq:
                self.from_x()
            if s > 1:
                self.crossed(s - 1)

        def crossed(self, s):
            lo, hi = (z + NZ - s) % NZ, (z + s) % NZ
            self.wait_high(("xu", s), 1 - x, lo)
            self.to_sibling(1 - x, lo)
            self.wait_high(("xd", s), 1 - x, hi)
            self.to_sibling(1 - x, hi)

        def last(self):
            far = (z + 4) % NZ
            self.wait_high(("uh", 4), x, far)
            self.high(("xu", 4), across, x, far)
            self.high(("xc", 4), across_other, x, far)
            self.wait_low(("dl", 4), x, far)
            self.to_sibling(x, far)
            self.crossed(3)
            self.wait(("uq", 4), 1 - x, far, 0, self.mid)
            self.wait(("dq", 4), 1 - x, far, self.mid, self.cut)
            self.wait_high(("xu", 4), 1 - x, far)

        def end(self):
            far = (z + 4) % NZ
            for m, ref, when in self.sib_waits:
                arrive(m, ref, sibling, when)
            self.wait(("uc", 4), 1 - x, far, 0, self.mid, 1 - c)
            self.wait(("dc", 4), 1 - x, far, self.mid, self.cut, 1 - c)
            self.wait(("xc", 4), 1 - x, far, self.cut, self.full, 1 - c)

    def strip_at(bz, bc):
        return pl.ds(pl.multiple_of((bz * 2 + bc) * STRIP, PIECE), STRIP)

    def strip_of(bz):
        return pl.ds(pl.multiple_of(bz * STRIP, PIECE), STRIP)

    def at_z(bz):
        return pl.ds(pl.multiple_of(bz * 2 * STRIP, PIECE), 2 * STRIP)

    def half_of(core):
        return pl.ds(pl.multiple_of(core * HALF, LANES), HALF)

    class Ring:
        def __init__(self, f):
            self.f = f
            self.m = {}
            self.m4 = [number() for _ in range(3)]

        def share(self, strip):
            self.f[x, strip_at(z, c), :] = strip[x * 2 + c]
            for n, (dx, dc) in enumerate(((1, 0), (1, 1), (0, 1))):
                bx, bc = (x + dx) % 2, (c + dc) % 2
                send(self.m4[n], strip.at[bx * 2 + bc], self.f.at[x, strip_at(z, c), :], dev(xh, y, bx, z, bc))

        def begin(self):
            for n, (dx, dc) in enumerate(((1, 0), (1, 1), (0, 1))):
                bx, bc = (x + dx) % 2, (c + dc) % 2
                arrive(self.m4[n], self.f.at[bx, strip_at(z, bc), :], sibling)
            for n in range(2):
                self.move("u", 1, n, up, z)
                self.move("d", 1, n, down, z)

        def move(self, way, s, n, target, bz):
            ref = self.f.at[n, at_z(bz), :]
            self.m[way, s, n] = number()
            send(self.m[way, s, n], ref, ref, target)

        def wait(self, way, s, n, bz):
            arrive(self.m[way, s, n], self.f.at[n, at_z(bz), :], sibling)

        def step(self, s):
            lo, hi = (z + NZ - s) % NZ, (z + s) % NZ
            for n in range(2):
                self.wait("u", s, n, lo)
                if s < 3 or n == 0:
                    self.move("u", s + 1, n, up, lo)
                self.wait("d", s, n, hi)
                if s < 3 or n == 1:
                    self.move("d", s + 1, n, down, hi)

        def last(self):
            far = (z + 4) % NZ
            self.wait("u", 4, 0, far)
            self.wait("d", 4, 1, far)

    def by_strips(bx, bz, bc, first, last):
        return fq.at[bc, bx, strip_of(bz), first:last]

    def by_columns(bx, bz, bc, first, last):
        cols = pl.ds(pl.multiple_of(rank(bx, bz) * LANES, LANES), LANES)
        return out_ref.at[pl.ds(pl.multiple_of(bc * HALF + first, PIECE), last - first), cols]

    gg = Ring(fg)
    gq = Gather(
        by_strips, WIDTH, half=lambda bx, bz, bc, to: fq.at[bc, bx, strip_of(bz), half_of(to)]
    )
    go = Gather(by_columns, HALF, exists=lambda bx, bz: works(bx, bz))

    own = pl.ds(pl.multiple_of(dp * STRIP, PIECE), STRIP)

    for load in load_a:
        load.wait()
    mine_a = x * 2 + c
    in_place = mine_a == y
    for n in range(4):
        started = pltpu.make_async_remote_copy(
            src_ref=av.at[n], dst_ref=aq.at[y], send_sem=ssem.at[number()], recv_sem=a_recv.at[y],
            device_id=(xh * 4 + mine_a, dp_of(n // 2, z, n % 2)), device_id_type=MESH,
        )
        there = jnp.logical_not(jnp.logical_and(in_place, y == n))
        pl.when(there)(started.start)
        pending.append((started, there))

    @pl.when(in_place)
    def _():
        aq[y] = av[y]

    for load in load_g:
        load.wait()
    gg.share(g)

    for load in loads:
        load.wait()
    owner = owner_ref[xh]
    other = owner_ref[1 - xh]
    is_far = lax.bitwise_xor(lax.shift_right_logical(owner, 2), xh)
    owner_y = lax.bitwise_and(owner, 3)
    other_y = lax.bitwise_and(other, 3)
    load_q.wait()
    for layer in range(2):
        for slot in range(4):
            qsel[layer, slot] = qv[layer, assign_ref[layer, slot]]
    y_up, y_down = (xh * 4 + (y + 1) % 4, dp), (xh * 4 + (y + 3) % 4, dp)
    far, above, below = (y + 2) % 4, (y + 1) % 4, (y + 3) % 4
    m_q1, m_q2 = [number() for _ in range(2)], [number() for _ in range(2)]
    send(m_q1[0], qsel.at[:, far, :, :HALF], qr_low.at[:, 1], y_up)
    send(m_q1[1], qsel.at[:, far, :, HALF:], qr_high.at[:, 1], y_down)
    gg.begin()

    for layer in range(2):
        qr_low[layer, 0] = qsel[layer, above, :, :HALF]
        qr_high[layer, 0] = qsel[layer, below, :, HALF:]
        qt[layer, 0] = qsel[layer, y]
    owners_y = [lax.bitwise_and(owner_ref[layer], 3) for layer in range(2)]

    def one_if(condition):
        return jnp.where(condition, 1, 0)

    arrive(m_q1[0], qr_low.at[:, 1], y_down)
    for layer in range(2):
        qs[0, layer, :, :HALF] = qr_low[layer, one_if(owners_y[layer] == below)]
        qs[0, layer, :, HALF:] = qsel[layer, above, :, HALF:]
    send(m_q2[0], qs.at[0], qt.at[:, 1], y_up)
    arrive(m_q1[1], qr_high.at[:, 1], y_up)
    for layer in range(2):
        qs[1, layer, :, :HALF] = qsel[layer, below, :, :HALF]
        qs[1, layer, :, HALF:] = qr_high[layer, one_if(owners_y[layer] == above)]
    send(m_q2[1], qs.at[1], qt.at[:, 2], y_down)

    for k in range(1, 4):
        m_a = (y + k) % 4
        pltpu.make_async_remote_copy(
            src_ref=aq.at[m_a], dst_ref=aq.at[m_a], send_sem=ssem.at[0], recv_sem=a_recv.at[m_a],
            device_id=sibling, device_id_type=MESH,
        ).wait_recv()

    @pl.when(jnp.logical_not(in_place))
    def _():
        pltpu.make_async_remote_copy(
            src_ref=aq.at[y], dst_ref=aq.at[y], send_sem=ssem.at[0], recv_sem=a_recv.at[y],
            device_id=sibling, device_id_type=MESH,
        ).wait_recv()

    m_ax = number()
    ac[...] = aq[other_y, 1 - xh]
    send(m_ax, ac, ax.at[1], partner)
    ax[0] = aq[owner_y, xh]

    m_vy = [number() for _ in range(3)]
    for layer in range(2):
        la_all = lav[...].astype(jnp.float32)[layer:layer + 1]
        lg_all = lgv[layer].astype(jnp.float32)
        at_row = lax.broadcasted_iota(jnp.int32, lg_all.shape, 0)
        for slot in range(4):
            lg = jnp.sum(jnp.where(at_row == assign_ref[layer, slot], lg_all, 0.0), axis=0, keepdims=True)
            for n in range(WIDTH // LANES):
                cols = slice(n * LANES, (n + 1) * LANES)
                vsel[slot, layer, 0, n:n + 1] = lg[:, cols]
                vsel[slot, layer, 1, n:n + 1] = la_all[:, cols]
    vy[y] = vsel[y]
    for k in range(1, 4):
        to = (y + k) % 4
        send(m_vy[k - 1], vsel.at[to], vy.at[y], (xh * 4 + to, dp))
    gg.step(1)
    arrive(m_ax, ax.at[1], partner)
    fa[y // 2, z, y % 2] = ax[is_far]
    m_a = {}

    def ring_a(way, s, bz):
        ref = fa.at[y // 2, bz, y % 2]
        m_a[way, s] = number()
        send(m_a[way, s], ref, ref, up if way == "u" else down)

    def step_a(s):
        lo, hi = (z + NZ - s) % NZ, (z + s) % NZ
        arrive(m_a["u", s], fa.at[y // 2, lo, y % 2], sibling)
        if s < 4:
            ring_a("u", s + 1, lo)
            arrive(m_a["d", s], fa.at[y // 2, hi, y % 2], sibling)
        if s < 3:
            ring_a("d", s + 1, hi)

    ring_a("u", 1, z)
    ring_a("d", 1, z)
    gg.step(2)

    arrive(m_q2[0], qt.at[:, 1], y_down)
    arrive(m_q2[1], qt.at[:, 2], y_up)
    for k in range(1, 4):
        arrive(m_vy[k - 1], vy.at[(y + 4 - k) % 4], partner)

    def came(layer, column_half):
        away = lax.bitwise_and(lax.bitwise_and(owner_ref[layer], 3) + 4 - y, 3)
        by_below = (away >= 2) if column_half == 0 else (away == 3)
        return jnp.where(away == 0, 0, jnp.where(by_below, 1, 2))

    m_qx, m_vx = number(), number()
    for n in range(2):
        half = slice(n * HALF, (n + 1) * HALF)
        qc[:, half] = qt[1 - xh, came(1 - xh, n), :, half]
    send(m_qx, qc, qx.at[1], partner)
    vc[...] = vy[other_y, 1 - xh]
    send(m_vx, vc, vx.at[1], partner)
    for n in range(2):
        half = slice(n * HALF, (n + 1) * HALF)
        qx[0, :, half] = qt[xh, came(xh, n), :, half]
    vx[0] = vy[owner_y, xh]

    step_a(1)
    gg.step(3)
    step_a(2)
    arrive(m_qx, qx.at[1], partner)
    fq[c, x, strip_of(z), :] = qx[is_far]
    gq.begin()
    step_a(3)
    gg.last()
    step_a(4)
    m_y1, m_y2 = [number() for _ in range(2)], [number() for _ in range(2)]
    plane = fa.at[y // 2, :, y % 2]
    send(m_y1[0], plane, plane, y_up)
    send(m_y1[1], plane, plane, y_down)
    gq.swap()
    arrive(m_vx, vx.at[1], partner)
    for n in range(WIDTH // LANES):
        lg_row = vx[is_far, 0, n:n + 1, :]
        lgc[n * LANES:(n + 1) * LANES, :] = jnp.transpose(jnp.broadcast_to(lg_row, (LANES, LANES)))
    gq.from_x()
    gq.step(1)
    arrive(m_y1[0], fa.at[below // 2, :, below % 2], sibling)
    lower = fa.at[below // 2, 0:4, below % 2]
    send(m_y2[0], lower, lower, y_up)
    arrive(m_y1[1], fa.at[above // 2, :, above % 2], sibling)
    upper = fa.at[above // 2, 4:8, above % 2]
    send(m_y2[1], upper, upper, y_down)

    arrive(*gq.paired, sibling)
    arrive(*gq.crossing, sibling)

    def flat(value):
        return value.reshape((-1, value.shape[-1]))

    p[x * 2 + c] = jnp.dot(
        flat(fq[:, :, strip_of(z), :]), flat(fg[...]), preferred_element_type=jnp.float32
    ).astype(jnp.bfloat16)
    m_p = [number() for _ in range(3)]
    p_own, p_far = p.at[x * 2 + c], p.at[(1 - x) * 2 + c]
    send(m_p[0], p_own, p_own, across)
    send(m_p[1], p_own, p_own, sibling)
    arrive(m_p[0], p_far, across)
    send(m_p[2], p_far, p_far, sibling)
    gq.step(2)
    arrive(m_y2[0], fa.at[far // 2, 0:4, far % 2], sibling)
    arrive(m_y2[1], fa.at[far // 2, 4:8, far % 2], sibling)

    arrive(m_p[1], p.at[x * 2 + 1 - c], sibling)
    arrive(m_p[2], p.at[(1 - x) * 2 + 1 - c], sibling)
    eigen = sum(
        jnp.dot(p[n], flat(fa[n // 2, n % 2 * 4:n % 2 * 4 + 4]), preferred_element_type=jnp.float32)
        for n in range(4)
    )
    lg_col = jnp.concatenate([lgc[pl.ds(pl.multiple_of(bx * HALF + (z * 2 + bc) * STRIP, PIECE), STRIP), :]
                              for bc in range(2) for bx in range(2)])
    for n in range(QUARTER // LANES):
        la_row = vx[is_far, 1, pl.ds((x * 2 + c) * (QUARTER // LANES) + n, 1), :]
        cols = slice(n * LANES, (n + 1) * LANES)
        sc[:, cols] = (eigen[:, cols] / (lg_col * la_row + DAMPING)).astype(jnp.bfloat16)

    for bx in range(2):
        for n in range(2):
            part = lax.dot_general(
                sc[...], flat(fa[bx, n * 4:n * 4 + 4]), (((1,), (1,)), ((), ())), preferred_element_type=jnp.float32
            ).reshape((2, 2, STRIP, QUARTER))
            cols = slice(bx * HALF + n * QUARTER, bx * HALF + (n + 1) * QUARTER)
            bp[:, :, :, cols] = part
            bo[:, :, :, cols] = part.astype(jnp.bfloat16)
    m_b = number()
    send(m_b, bo.at[1 - c], bi, sibling)
    gq.step(3)
    arrive(m_b, bi, sibling)
    done = (bp[c] + bi[...].astype(jnp.float32)).astype(jnp.bfloat16)
    for j in range(WIDTH // LANES):
        bk[j] = done[:, :, j * LANES:(j + 1) * LANES]

    for wx in range(2):
        for wz in range(NZ):
            if (wz + 2 * wx) % 4 == 3:
                continue
            part = bk.at[wx * 6 + wz - (wz + 2 * wx) // 4]
            to_self = jnp.logical_and(x == wx, z == wz)
            others = jnp.logical_not(to_self)
            started = pltpu.make_async_remote_copy(
                src_ref=part, dst_ref=bc.at[x, :, strip_of(z), :], send_sem=ssem.at[number()],
                recv_sem=b_recv.at[x * NZ + z], device_id=dev(xh, y, wx, wz, c), device_id_type=MESH,
            )
            pl.when(others)(started.start)
            pending.append((started, others))

            @pl.when(to_self)
            def _():
                bc[x, :, strip_of(z), :] = part[...]

    gq.last()
    is_worker = works(x, z)
    m_bt = number()

    @pl.when(is_worker)
    def _():
        def take(k, carry):
            n = (x * NZ + z + k) % 16
            block = bc.at[n // NZ, :, strip_of(n % NZ), :]
            pltpu.make_async_remote_copy(
                src_ref=block, dst_ref=block, send_sem=ssem.at[m_bt], recv_sem=b_recv.at[n],
                device_id=sibling, device_id_type=MESH,
            ).wait_recv()
            return carry

        lax.fori_loop(1, 16, take, 0)
        total = flat(bc[0].astype(jnp.float32) + bc[1].astype(jnp.float32))
        for n in range(HALF // LANES):
            cols = slice(n * LANES, (n + 1) * LANES)
            bt[c, :, cols] = jnp.transpose(total[cols, :]).astype(jnp.bfloat16)

    send(m_bt, bt.at[c], bt.at[c], sibling, is_worker)
    gq.end()
    arrive(m_bt, bt.at[1 - c], sibling, is_worker)

    mine = pl.ds(pl.multiple_of(rank(x, z) * LANES, LANES), LANES)

    def finish(n):
        @pl.when(is_worker)
        def _():
            rows = pl.ds(pl.multiple_of(c * HALF + n * QUARTER, LANES), QUARTER)
            part = sum(
                jnp.dot(bt[k], flat(fq[k, :, :, rows]), preferred_element_type=jnp.float32) for k in range(2)
            )
            out_ref[rows, mine] = jnp.transpose(part).astype(jnp.bfloat16)

    finish(0)
    go.begin_low()
    finish(1)
    go.begin_high()
    drain()
    go.swap()
    go.step(1)
    early = len(pending)
    go.step(2)
    go.step(3)
    drain(early)
    go.last()
    go.end()
    drain()


def local(gradient_tiles, qa_basis, qg_basis, qa_values, qg_values, layer_owner, block_assign):
    strip = (STRIP, WIDTH)
    bf = jnp.bfloat16
    f32 = jnp.float32
    out = pl.pallas_call(
        kernel,
        out_shape=jax.ShapeDtypeStruct((WIDTH, WIDTH), bf),
        in_specs=[pl.BlockSpec(memory_space=pltpu.HBM)] * 7,
        out_specs=pl.BlockSpec(memory_space=pltpu.VMEM),
        scratch_shapes=[
            pltpu.SMEM((2,), jnp.int32),
            pltpu.SMEM((2, 4), jnp.int32),
            pltpu.VMEM((2, 16, WIDTH), bf),
            pltpu.VMEM((2, WIDTH), bf),
            pltpu.VMEM((4, STRIP, QUARTER), bf),
            pltpu.VMEM((4, 2, STRIP, QUARTER), bf),
            pltpu.VMEM((2, 16) + strip, bf),
            pltpu.VMEM((2, 4) + strip, bf),
            pltpu.VMEM((2, 2, STRIP, HALF), bf),
            pltpu.VMEM((2, 2, STRIP, HALF), bf),
            pltpu.VMEM((2, 2) + strip, bf),
            pltpu.VMEM((2, 3) + strip, bf),
            pltpu.VMEM((2,) + strip, bf),
            pltpu.VMEM(strip, bf),
            pltpu.VMEM((4, 2, STRIP, QUARTER), bf),
            pltpu.VMEM((STRIP, QUARTER), bf),
            pltpu.VMEM((2, STRIP, QUARTER), bf),
            pltpu.VMEM((4, 2, 2, 16, LANES), f32),
            pltpu.VMEM((4, 2, 2, 16, LANES), f32),
            pltpu.VMEM((2, 2, 16, LANES), f32),
            pltpu.VMEM((2, 16, LANES), f32),
            pltpu.VMEM((2, HALF, QUARTER), bf),
            pltpu.VMEM((2, NZ, 2, STRIP, QUARTER), bf),
            pltpu.VMEM((2, 2, HALF // 2, WIDTH), bf),
            pltpu.VMEM((4, 4 * STRIP, QUARTER), bf),
            pltpu.VMEM((WIDTH, LANES), f32),
            pltpu.VMEM((4 * STRIP, QUARTER), bf),
            pltpu.VMEM((2, 2) + strip, f32),
            pltpu.VMEM((2, 2) + strip, bf),
            pltpu.VMEM((2,) + strip, bf),
            pltpu.VMEM((12, 2, STRIP, LANES), bf),
            pltpu.VMEM((2, 2, HALF // 2, LANES), bf),
            pltpu.VMEM((2, LANES, HALF), bf),
            pltpu.SemaphoreType.DMA((N_SEM,)),
            pltpu.SemaphoreType.DMA((N_SEM,)),
            pltpu.SemaphoreType.DMA((15,)),
            pltpu.SemaphoreType.DMA((4,)),
            pltpu.SemaphoreType.DMA((16,)),
        ],
        compiler_params=pltpu.CompilerParams(
            collective_id=0, has_side_effects=True, vmem_limit_bytes=48 * 1024 * 1024
        ),
        cost_estimate=pl.CostEstimate(flops=4 * 2 * 48 * 1536 * 1536, bytes_accessed=10_000_000, transcendentals=0),
    )(
        *(
            pltpu.with_memory_space_constraint(operand, pltpu.HBM)
            for operand in (
                layer_owner, block_assign, gradient_tiles[0], qa_basis[0], jnp.swapaxes(qg_basis[0], -1, -2),
                qg_values[0], qa_values[0],
            )
        )
    )
    return out[None]


def solution(mesh):
    in_specs = (
        P("grp", "dp", None),
        P("grp", None, "dp", None),
        P("grp", None, None, None, "dp"),
        P("grp", None, None),
        P("grp", None, None, None),
        P(),
        P(),
    )
    out_specs = P("grp", None, None)
    return jax.shard_map(local, mesh=mesh, in_specs=in_specs, out_specs=out_specs, check_vma=False)
```

```python
import functools

import jax
import jax.numpy as jnp
from jax import lax
from jax.experimental import pallas as pl
from jax.experimental.pallas import tpu as pltpu
from jax.sharding import PartitionSpec as P

MESH = pl.DeviceIdType.MESH
DAMPING = 0.1
NZ = 8
STRIP = 48
PIECE = 16
WIDTH = 1536
LANES = 128
N_DP = 32
HALF = WIDTH // 2
QUARTER = WIDTH // 4
TILE = 256
N_SEM = 256


def works(x, z):
    return (z + 2 * x) % 4 != 3


def rank(x, z):
    return x * 6 + z - (z + 2 * x) // 4


def kernel(
    owner_hbm, assign_hbm, g_hbm, a_hbm, q_hbm, lg_hbm, la_hbm, out_ref,
    owner_ref, assign_ref, lgv, lav, g, av, qv, qsel, qr_low, qr_high, qs, qt, qx_low, qx_high, qc, aq, ac, ax, vsel, vy, vx, vc, fg, fa, fq, p, lgc, sc, bp, bo, bi, bk, bc, bt,
    ssem, rsem, lsem, a_recv, b_recv,
):
    member = lax.axis_index("grp")
    dp = lax.axis_index("dp")
    xh, y = member // 4, member % 4
    x, z, c = dp // 16, (dp // 2) % NZ, dp % 2

    load_g = [
        pltpu.make_async_copy(g_hbm.at[:, n * QUARTER:(n + 1) * QUARTER], g.at[n], lsem.at[7 + n]) for n in range(4)
    ]
    load_a = [
        pltpu.make_async_copy(a_hbm.at[:, :, n * QUARTER:(n + 1) * QUARTER], av.at[n], lsem.at[11 + n])
        for n in range(4)
    ]
    load_q = pltpu.make_async_copy(q_hbm, qv, lsem.at[2])
    loads = [
        pltpu.make_async_copy(src, dst, lsem.at[3 + n])
        for n, (src, dst) in enumerate(
            ((owner_hbm, owner_ref), (assign_hbm, assign_ref), (lg_hbm, lgv), (la_hbm, lav))
        )
    ]
    for load in load_a:
        load.start()
    for load in load_g:
        load.start()
    for load in loads:
        load.start()
    load_q.start()
    core0 = c == 0

    def dp_of(dx, dz, dc):
        return dx * 16 + dz * 2 + dc

    def dev(gx, gy, dx, dz, dc):
        return (gx * 4 + gy, dp_of(dx, dz, dc))

    sibling = dev(xh, y, x, z, 1 - c)
    across = dev(xh, y, 1 - x, z, c)
    up = dev(xh, y, x, (z + 1) % NZ, c)
    down = dev(xh, y, x, (z + NZ - 1) % NZ, c)
    across_other = dev(xh, y, 1 - x, z, 1 - c)
    up_other = dev(xh, y, x, (z + 1) % NZ, 1 - c)
    down_other = dev(xh, y, x, (z + NZ - 1) % NZ, 1 - c)
    partner = dev(1 - xh, y, x, z, c)

    barrier = pltpu.get_barrier_semaphore()

    near = [up, down, up_other, down_other, partner]
    near += [
        dev(xh, (y + k // 4) % 4, (x + k // 2) % 2, z, (c + k) % 2) for k in range(1, 16)
    ]
    for target in near:
        pl.semaphore_signal(barrier, inc=1, device_id=target, device_id_type=MESH)
    pl.semaphore_wait(barrier, len(near))

    count = [0]
    pending = []

    def number():
        count[0] += 1
        assert count[0] <= N_SEM
        return count[0] - 1

    def copy(m, src, dst, target):
        return pltpu.make_async_remote_copy(
            src_ref=src, dst_ref=dst, send_sem=ssem.at[m], recv_sem=rsem.at[m],
            device_id=target, device_id_type=MESH,
        )

    def send(m, src, dst, target, when=None):
        started = copy(m, src, dst, target)
        pending.append((started, when))
        if when is None:
            started.start()
        else:
            pl.when(when)(started.start)

    def drain(until=None):
        for started, when in pending[:until]:
            if when is None:
                started.wait_send()
            else:
                pl.when(when)(started.wait_send)
        del pending[:until]

    def arrive(m, dst, target, when=None):
        landed = copy(m, dst, dst, target)
        if when is None:
            landed.wait_recv()
        else:
            pl.when(when)(landed.wait_recv)

    class Gather:
        def __init__(self, ref, full, half=None, exists=None):
            self.ref, self.full, self.cut, self.mid = ref, full, full // 2, full // 4
            self.half = half or (lambda bx, bz, bc, to: ref(bx, bz, bc, 0, full))
            self.exists = exists or (lambda bx, bz: None)
            self.sib_waits = []
            self.m = {}

        def key(self, *name):
            if name not in self.m:
                self.m[name] = number()
            return self.m[name]

        def to_sibling(self, bx, bz):
            m = number()
            ref = self.half(bx, bz, c, 1 - c)
            send(m, ref, ref, sibling, self.exists(bx, bz))
            self.sib_waits.append((m, self.half(bx, bz, 1 - c, c), self.exists(bx, bz)))

        def move(self, name, target, bx, bz, first, last):
            ref = self.ref(bx, bz, c, first, last)
            send(self.key(*name), ref, ref, target, self.exists(bx, bz))

        def wait(self, name, bx, bz, first, last, bc=c):
            arrive(self.key(*name), self.ref(bx, bz, bc, first, last), sibling, self.exists(bx, bz))

        def low(self, name, target, bx, bz):
            self.move(name, target, bx, bz, 0, self.cut)

        def high(self, name, target, bx, bz):
            self.move(name, target, bx, bz, self.cut, self.full)

        def wait_low(self, name, bx, bz):
            self.wait(name, bx, bz, 0, self.cut)

        def wait_high(self, name, bx, bz):
            self.wait(name, bx, bz, self.cut, self.full)

        def begin_low(self):
            self.low(("x", 0), across, x, z)
            self.low(("ul", 1), up, x, z)
            self.low(("dl", 1), down, x, z)

        def begin_high(self):
            self.high(("xh", 0), across, x, z)
            if self is gq:
                self.paired = self.whole(x)
            self.high(("uh", 1), up, x, z)
            self.high(("dh", 1), down, x, z)
            if self is not gq:
                self.to_sibling(x, z)

        def whole(self, bx):
            m = number()
            ref = self.ref(bx, z, c, 0, self.full)
            send(m, ref, ref, sibling)
            return m, self.ref(bx, z, 1 - c, 0, self.full)

        def swap(self):
            self.wait_low(("x", 0), 1 - x, z)
            self.low(("uq", 1), up, 1 - x, z)
            self.low(("dq", 1), down, 1 - x, z)

        def from_x(self):
            self.wait_high(("xh", 0), 1 - x, z)
            if self is gq:
                self.crossing = self.whole(1 - x)
            else:
                self.to_sibling(1 - x, z)

        def step(self, s):
            lo, hi = (z + NZ - s) % NZ, (z + s) % NZ
            self.wait_high(("uh", s), x, lo)
            self.high(("uh", s + 1), up, x, lo)
            self.high(("xu", s), across, x, lo)
            self.wait_high(("dh", s), x, hi)
            if s < 3:
                self.high(("dh", s + 1), down, x, hi)
            self.high(("xd", s), across, x, hi)
            self.wait_low(("ul", s), x, lo)
            if s < 3:
                self.low(("ul", s + 1), up, x, lo)
            self.wait_low(("dl", s), x, hi)
            self.low(("dl", s + 1), down, x, hi)
            self.wait_low(("uq", s), 1 - x, lo)
            if s < 3:
                self.low(("uq", s + 1), up, 1 - x, lo)
            else:
                self.move(("uq", 4), up, 1 - x, lo, 0, self.mid)
                self.move(("uc", 4), up_other, 1 - x, lo, 0, self.mid)
            self.wait_low(("dq", s), 1 - x, hi)
            if s < 3:
                self.low(("dq", s + 1), down, 1 - x, hi)
            else:
                self.move(("dq", 4), down, 1 - x, hi, self.mid, self.cut)
                self.move(("dc", 4), down_other, 1 - x, hi, self.mid, self.cut)
            self.to_sibling(x, lo)
            self.to_sibling(x, hi)
            if s == 2 and self is not gq:
                self.from_x()
            if s > 1:
                self.crossed(s - 1)

        def crossed(self, s):
            lo, hi = (z + NZ - s) % NZ, (z + s) % NZ
            self.wait_high(("xu", s), 1 - x, lo)
            self.to_sibling(1 - x, lo)
            self.wait_high(("xd", s), 1 - x, hi)
            self.to_sibling(1 - x, hi)

        def last(self):
            far = (z + 4) % NZ
            self.wait_high(("uh", 4), x, far)
            self.high(("xu", 4), across, x, far)
            self.high(("xc", 4), across_other, x, far)
            self.wait_low(("dl", 4), x, far)
            self.to_sibling(x, far)
            self.crossed(3)
            self.wait(("uq", 4), 1 - x, far, 0, self.mid)
            self.wait(("dq", 4), 1 - x, far, self.mid, self.cut)
            self.wait_high(("xu", 4), 1 - x, far)

        def end(self):
            far = (z + 4) % NZ
            for m, ref, when in self.sib_waits:
                arrive(m, ref, sibling, when)
            self.wait(("uc", 4), 1 - x, far, 0, self.mid, 1 - c)
            self.wait(("dc", 4), 1 - x, far, self.mid, self.cut, 1 - c)
            self.wait(("xc", 4), 1 - x, far, self.cut, self.full, 1 - c)

    def strip_at(bz, bc):
        return pl.ds(pl.multiple_of((bz * 2 + bc) * STRIP, PIECE), STRIP)

    def strip_of(bz):
        return pl.ds(pl.multiple_of(bz * STRIP, PIECE), STRIP)

    def at_z(bz):
        return pl.ds(pl.multiple_of(bz * 2 * STRIP, PIECE), 2 * STRIP)

    def half_of(core):
        return pl.ds(pl.multiple_of(core * HALF, LANES), HALF)

    class Ring:
        def __init__(self, f):
            self.f = f
            self.m = {}
            self.m4 = [number() for _ in range(3)]

        def share(self, strip):
            self.f[x, strip_at(z, c), :] = strip[x * 2 + c]
            for n, (dx, dc) in enumerate(((1, 0), (1, 1), (0, 1))):
                bx, bc = (x + dx) % 2, (c + dc) % 2
                send(self.m4[n], strip.at[bx * 2 + bc], self.f.at[x, strip_at(z, c), :], dev(xh, y, bx, z, bc))

        def begin(self):
            for n, (dx, dc) in enumerate(((1, 0), (1, 1), (0, 1))):
                bx, bc = (x + dx) % 2, (c + dc) % 2
                arrive(self.m4[n], self.f.at[bx, strip_at(z, bc), :], sibling)
            for n in range(2):
                self.move("u", 1, n, up, z)
                self.move("d", 1, n, down, z)

        def move(self, way, s, n, target, bz):
            ref = self.f.at[n, at_z(bz), :]
            self.m[way, s, n] = number()
            send(self.m[way, s, n], ref, ref, target)

        def wait(self, way, s, n, bz):
            arrive(self.m[way, s, n], self.f.at[n, at_z(bz), :], sibling)

        def step(self, s):
            lo, hi = (z + NZ - s) % NZ, (z + s) % NZ
            for n in range(2):
                self.wait("u", s, n, lo)
                if s < 3 or n == 0:
                    self.move("u", s + 1, n, up, lo)
                self.wait("d", s, n, hi)
                if s < 3 or n == 1:
                    self.move("d", s + 1, n, down, hi)

        def last(self):
            far = (z + 4) % NZ
            self.wait("u", 4, 0, far)
            self.wait("d", 4, 1, far)

    def by_strips(bx, bz, bc, first, last):
        return fq.at[bc, bx, strip_of(bz), first:last]

    def by_columns(bx, bz, bc, first, last):
        cols = pl.ds(pl.multiple_of(rank(bx, bz) * LANES, LANES), LANES)
        return out_ref.at[pl.ds(pl.multiple_of(bc * HALF + first, PIECE), last - first), cols]

    gg = Ring(fg)
    gq = Gather(
        by_strips, WIDTH, half=lambda bx, bz, bc, to: fq.at[bc, bx, strip_of(bz), half_of(to)]
    )
    go = Gather(by_columns, HALF, exists=lambda bx, bz: works(bx, bz))

    own = pl.ds(pl.multiple_of(dp * STRIP, PIECE), STRIP)

    for load in load_a:
        load.wait()
    mine_a = x * 2 + c
    in_place = mine_a == y
    for n in range(4):
        started = pltpu.make_async_remote_copy(
            src_ref=av.at[n], dst_ref=aq.at[y], send_sem=ssem.at[number()], recv_sem=a_recv.at[y],
            device_id=(xh * 4 + mine_a, dp_of(n // 2, z, n % 2)), device_id_type=MESH,
        )
        there = jnp.logical_not(jnp.logical_and(in_place, y == n))
        pl.when(there)(started.start)
        pending.append((started, there))

    @pl.when(in_place)
    def _():
        aq[y] = av[y]

    for load in load_g:
        load.wait()
    gg.share(g)

    for load in loads:
        load.wait()
    owner = owner_ref[xh]
    other = owner_ref[1 - xh]
    is_far = lax.bitwise_xor(lax.shift_right_logical(owner, 2), xh)
    owner_y = lax.bitwise_and(owner, 3)
    other_y = lax.bitwise_and(other, 3)
    load_q.wait()
    for layer in range(2):
        for slot in range(4):
            qsel[layer, slot] = qv[layer, assign_ref[layer, slot]]
    y_up, y_down = (xh * 4 + (y + 1) % 4, dp), (xh * 4 + (y + 3) % 4, dp)
    far, above, below = (y + 2) % 4, (y + 1) % 4, (y + 3) % 4
    m_q1, m_q2, m_q3 = ([number() for _ in range(2)] for _ in range(3))
    send(m_q1[0], qsel.at[:, far, :, :HALF], qr_low.at[:, 1], y_up)
    send(m_q1[1], qsel.at[:, far, :, HALF:], qr_high.at[:, 1], y_down)
    send(m_q3[0], qsel.at[:, above, :, HALF:], qt.at[:, 1, :, HALF:], y_up)
    send(m_q3[1], qsel.at[:, below, :, :HALF], qt.at[:, 2, :, :HALF], y_down)
    gg.begin()

    for layer in range(2):
        qr_low[layer, 0] = qsel[layer, above, :, :HALF]
        qr_high[layer, 0] = qsel[layer, below, :, HALF:]
        qt[layer, 0] = qsel[layer, y]
    owners_y = [lax.bitwise_and(owner_ref[layer], 3) for layer in range(2)]

    def one_if(condition):
        return jnp.where(condition, 1, 0)

    arrive(m_q1[0], qr_low.at[:, 1], y_down)
    for layer in range(2):
        qs[0, layer] = qr_low[layer, one_if(owners_y[layer] == below)]
    send(m_q2[0], qs.at[0], qt.at[:, 1, :, :HALF], y_up)
    arrive(m_q1[1], qr_high.at[:, 1], y_up)
    for layer in range(2):
        qs[1, layer] = qr_high[layer, one_if(owners_y[layer] == above)]
    send(m_q2[1], qs.at[1], qt.at[:, 2, :, HALF:], y_down)

    for k in range(1, 4):
        m_a = (y + k) % 4
        pltpu.make_async_remote_copy(
            src_ref=aq.at[m_a], dst_ref=aq.at[m_a], send_sem=ssem.at[0], recv_sem=a_recv.at[m_a],
            device_id=sibling, device_id_type=MESH,
        ).wait_recv()

    @pl.when(jnp.logical_not(in_place))
    def _():
        pltpu.make_async_remote_copy(
            src_ref=aq.at[y], dst_ref=aq.at[y], send_sem=ssem.at[0], recv_sem=a_recv.at[y],
            device_id=sibling, device_id_type=MESH,
        ).wait_recv()

    m_ax = number()
    ac[...] = aq[other_y, 1 - xh]
    send(m_ax, ac, ax.at[1], partner)
    ax[0] = aq[owner_y, xh]

    m_vy = [number() for _ in range(3)]
    for layer in range(2):
        la_all = lav[...].astype(jnp.float32)[layer:layer + 1]
        lg_all = lgv[layer].astype(jnp.float32)
        at_row = lax.broadcasted_iota(jnp.int32, lg_all.shape, 0)
        for slot in range(4):
            lg = jnp.sum(jnp.where(at_row == assign_ref[layer, slot], lg_all, 0.0), axis=0, keepdims=True)
            for n in range(WIDTH // LANES):
                cols = slice(n * LANES, (n + 1) * LANES)
                vsel[slot, layer, 0, n:n + 1] = lg[:, cols]
                vsel[slot, layer, 1, n:n + 1] = la_all[:, cols]
    vy[y] = vsel[y]
    for k in range(1, 4):
        to = (y + k) % 4
        send(m_vy[k - 1], vsel.at[to], vy.at[y], (xh * 4 + to, dp))
    gg.step(1)
    arrive(m_ax, ax.at[1], partner)
    fa[y // 2, z, y % 2] = ax[is_far]
    m_a = {}

    def ring_a(way, s, bz):
        ref = fa.at[y // 2, bz, y % 2]
        m_a[way, s] = number()
        send(m_a[way, s], ref, ref, up if way == "u" else down)

    def step_a(s):
        lo, hi = (z + NZ - s) % NZ, (z + s) % NZ
        arrive(m_a["u", s], fa.at[y // 2, lo, y % 2], sibling)
        if s < 4:
            ring_a("u", s + 1, lo)
            arrive(m_a["d", s], fa.at[y // 2, hi, y % 2], sibling)
        if s < 3:
            ring_a("d", s + 1, hi)

    ring_a("u", 1, z)
    ring_a("d", 1, z)

    arrive(m_q3[0], qt.at[:, 1, :, HALF:], y_down)
    arrive(m_q3[1], qt.at[:, 2, :, :HALF], y_up)
    arrive(m_q2[0], qt.at[:, 1, :, :HALF], y_down)
    arrive(m_q2[1], qt.at[:, 2, :, HALF:], y_up)
    for k in range(1, 4):
        arrive(m_vy[k - 1], vy.at[(y + 4 - k) % 4], partner)

    def came(layer, column_half):
        away = lax.bitwise_and(lax.bitwise_and(owner_ref[layer], 3) + 4 - y, 3)
        by_below = (away >= 2) if column_half == 0 else (away == 3)
        return jnp.where(away == 0, 0, jnp.where(by_below, 1, 2))

    m_qx, m_vx = [number() for _ in range(2)], number()
    for n in range(2):
        half = slice(n * HALF, (n + 1) * HALF)
        qc[n] = qt[1 - xh, came(1 - xh, n), :, half]
        send(m_qx[n], qc.at[n], (qx_low, qx_high)[n].at[1], partner)
    vc[...] = vy[other_y, 1 - xh]
    send(m_vx, vc, vx.at[1], partner)
    for n in range(2):
        half = slice(n * HALF, (n + 1) * HALF)
        (qx_low, qx_high)[n][0] = qt[xh, came(xh, n), :, half]
    vx[0] = vy[owner_y, xh]
    gg.step(2)

    step_a(1)
    gg.step(3)
    step_a(2)
    arrive(m_qx[0], qx_low.at[1], partner)
    fq[c, x, strip_of(z), :HALF] = qx_low[is_far]
    gq.begin_low()
    arrive(m_qx[1], qx_high.at[1], partner)
    fq[c, x, strip_of(z), HALF:] = qx_high[is_far]
    gq.begin_high()
    step_a(3)
    gg.last()
    step_a(4)
    m_y1, m_y2 = [number() for _ in range(2)], [number() for _ in range(2)]
    plane = fa.at[y // 2, :, y % 2]
    send(m_y1[0], plane, plane, y_up)
    send(m_y1[1], plane, plane, y_down)
    gq.swap()
    arrive(m_vx, vx.at[1], partner)
    for n in range(WIDTH // LANES):
        lg_row = vx[is_far, 0, n:n + 1, :]
        lgc[n * LANES:(n + 1) * LANES, :] = jnp.transpose(jnp.broadcast_to(lg_row, (LANES, LANES)))
    gq.from_x()
    gq.step(1)
    arrive(m_y1[0], fa.at[below // 2, :, below % 2], sibling)
    lower = fa.at[below // 2, 0:4, below % 2]
    send(m_y2[0], lower, lower, y_up)
    arrive(m_y1[1], fa.at[above // 2, :, above % 2], sibling)
    upper = fa.at[above // 2, 4:8, above % 2]
    send(m_y2[1], upper, upper, y_down)

    arrive(*gq.paired, sibling)
    arrive(*gq.crossing, sibling)

    def flat(value):
        return value.reshape((-1, value.shape[-1]))

    p[x * 2 + c] = jnp.dot(
        flat(fq[:, :, strip_of(z), :]), flat(fg[...]), preferred_element_type=jnp.float32
    ).astype(jnp.bfloat16)
    m_p = [number() for _ in range(3)]
    p_own, p_far = p.at[x * 2 + c], p.at[(1 - x) * 2 + c]
    send(m_p[0], p_own, p_own, across)
    send(m_p[1], p_own, p_own, sibling)
    arrive(m_p[0], p_far, across)
    send(m_p[2], p_far, p_far, sibling)
    gq.step(2)
    arrive(m_y2[0], fa.at[far // 2, 0:4, far % 2], sibling)
    arrive(m_y2[1], fa.at[far // 2, 4:8, far % 2], sibling)

    arrive(m_p[1], p.at[x * 2 + 1 - c], sibling)
    arrive(m_p[2], p.at[(1 - x) * 2 + 1 - c], sibling)
    eigen = sum(
        jnp.dot(p[n], flat(fa[n // 2, n % 2 * 4:n % 2 * 4 + 4]), preferred_element_type=jnp.float32)
        for n in range(4)
    )
    lg_col = jnp.concatenate([lgc[pl.ds(pl.multiple_of(bx * HALF + (z * 2 + bc) * STRIP, PIECE), STRIP), :]
                              for bc in range(2) for bx in range(2)])
    for n in range(QUARTER // LANES):
        la_row = vx[is_far, 1, pl.ds((x * 2 + c) * (QUARTER // LANES) + n, 1), :]
        cols = slice(n * LANES, (n + 1) * LANES)
        sc[:, cols] = (eigen[:, cols] / (lg_col * la_row + DAMPING)).astype(jnp.bfloat16)

    for bx in range(2):
        for n in range(2):
            part = lax.dot_general(
                sc[...], flat(fa[bx, n * 4:n * 4 + 4]), (((1,), (1,)), ((), ())), preferred_element_type=jnp.float32
            ).reshape((2, 2, STRIP, QUARTER))
            cols = slice(bx * HALF + n * QUARTER, bx * HALF + (n + 1) * QUARTER)
            bp[:, :, :, cols] = part
            bo[:, :, :, cols] = part.astype(jnp.bfloat16)
    m_b = number()
    send(m_b, bo.at[1 - c], bi, sibling)
    gq.step(3)
    arrive(m_b, bi, sibling)
    done = (bp[c] + bi[...].astype(jnp.float32)).astype(jnp.bfloat16)
    for j in range(WIDTH // LANES):
        bk[j] = done[:, :, j * LANES:(j + 1) * LANES]

    for wx in range(2):
        for wz in range(NZ):
            if (wz + 2 * wx) % 4 == 3:
                continue
            part = bk.at[wx * 6 + wz - (wz + 2 * wx) // 4]
            to_self = jnp.logical_and(x == wx, z == wz)
            others = jnp.logical_not(to_self)
            started = pltpu.make_async_remote_copy(
                src_ref=part, dst_ref=bc.at[x, :, strip_of(z), :], send_sem=ssem.at[number()],
                recv_sem=b_recv.at[x * NZ + z], device_id=dev(xh, y, wx, wz, c), device_id_type=MESH,
            )
            pl.when(others)(started.start)
            pending.append((started, others))

            @pl.when(to_self)
            def _():
                bc[x, :, strip_of(z), :] = part[...]

    gq.last()
    is_worker = works(x, z)
    m_bt = number()

    @pl.when(is_worker)
    def _():
        def take(k, carry):
            n = (x * NZ + z + k) % 16
            block = bc.at[n // NZ, :, strip_of(n % NZ), :]
            pltpu.make_async_remote_copy(
                src_ref=block, dst_ref=block, send_sem=ssem.at[m_bt], recv_sem=b_recv.at[n],
                device_id=sibling, device_id_type=MESH,
            ).wait_recv()
            return carry

        lax.fori_loop(1, 16, take, 0)
        total = flat(bc[0].astype(jnp.float32) + bc[1].astype(jnp.float32))
        for n in range(HALF // LANES):
            cols = slice(n * LANES, (n + 1) * LANES)
            bt[c, :, cols] = jnp.transpose(total[cols, :]).astype(jnp.bfloat16)

    send(m_bt, bt.at[c], bt.at[c], sibling, is_worker)
    gq.end()
    arrive(m_bt, bt.at[1 - c], sibling, is_worker)

    mine = pl.ds(pl.multiple_of(rank(x, z) * LANES, LANES), LANES)

    def finish(n):
        @pl.when(is_worker)
        def _():
            rows = pl.ds(pl.multiple_of(c * HALF + n * QUARTER, LANES), QUARTER)
            part = sum(
                jnp.dot(bt[k], flat(fq[k, :, :, rows]), preferred_element_type=jnp.float32) for k in range(2)
            )
            out_ref[rows, mine] = jnp.transpose(part).astype(jnp.bfloat16)

    finish(0)
    go.begin_low()
    finish(1)
    go.begin_high()
    drain()
    go.swap()
    go.step(1)
    early = len(pending)
    go.step(2)
    go.step(3)
    drain(early)
    go.last()
    go.end()
    drain()


def local(gradient_tiles, qa_basis, qg_basis, qa_values, qg_values, layer_owner, block_assign):
    strip = (STRIP, WIDTH)
    bf = jnp.bfloat16
    f32 = jnp.float32
    out = pl.pallas_call(
        kernel,
        out_shape=jax.ShapeDtypeStruct((WIDTH, WIDTH), bf),
        in_specs=[pl.BlockSpec(memory_space=pltpu.HBM)] * 7,
        out_specs=pl.BlockSpec(memory_space=pltpu.VMEM),
        scratch_shapes=[
            pltpu.SMEM((2,), jnp.int32),
            pltpu.SMEM((2, 4), jnp.int32),
            pltpu.VMEM((2, 16, WIDTH), bf),
            pltpu.VMEM((2, WIDTH), bf),
            pltpu.VMEM((4, STRIP, QUARTER), bf),
            pltpu.VMEM((4, 2, STRIP, QUARTER), bf),
            pltpu.VMEM((2, 16) + strip, bf),
            pltpu.VMEM((2, 4) + strip, bf),
            pltpu.VMEM((2, 2, STRIP, HALF), bf),
            pltpu.VMEM((2, 2, STRIP, HALF), bf),
            pltpu.VMEM((2, 2, STRIP, HALF), bf),
            pltpu.VMEM((2, 3) + strip, bf),
            pltpu.VMEM((2, STRIP, HALF), bf),
            pltpu.VMEM((2, STRIP, HALF), bf),
            pltpu.VMEM((2, STRIP, HALF), bf),
            pltpu.VMEM((4, 2, STRIP, QUARTER), bf),
            pltpu.VMEM((STRIP, QUARTER), bf),
            pltpu.VMEM((2, STRIP, QUARTER), bf),
            pltpu.VMEM((4, 2, 2, 16, LANES), f32),
            pltpu.VMEM((4, 2, 2, 16, LANES), f32),
            pltpu.VMEM((2, 2, 16, LANES), f32),
            pltpu.VMEM((2, 16, LANES), f32),
            pltpu.VMEM((2, HALF, QUARTER), bf),
            pltpu.VMEM((2, NZ, 2, STRIP, QUARTER), bf),
            pltpu.VMEM((2, 2, HALF // 2, WIDTH), bf),
            pltpu.VMEM((4, 4 * STRIP, QUARTER), bf),
            pltpu.VMEM((WIDTH, LANES), f32),
            pltpu.VMEM((4 * STRIP, QUARTER), bf),
            pltpu.VMEM((2, 2) + strip, f32),
            pltpu.VMEM((2, 2) + strip, bf),
            pltpu.VMEM((2,) + strip, bf),
            pltpu.VMEM((12, 2, STRIP, LANES), bf),
            pltpu.VMEM((2, 2, HALF // 2, LANES), bf),
            pltpu.VMEM((2, LANES, HALF), bf),
            pltpu.SemaphoreType.DMA((N_SEM,)),
            pltpu.SemaphoreType.DMA((N_SEM,)),
            pltpu.SemaphoreType.DMA((15,)),
            pltpu.SemaphoreType.DMA((4,)),
            pltpu.SemaphoreType.DMA((16,)),
        ],
        compiler_params=pltpu.CompilerParams(
            collective_id=0, has_side_effects=True, vmem_limit_bytes=48 * 1024 * 1024
        ),
        cost_estimate=pl.CostEstimate(flops=4 * 2 * 48 * 1536 * 1536, bytes_accessed=10_000_000, transcendentals=0),
    )(
        *(
            pltpu.with_memory_space_constraint(operand, pltpu.HBM)
            for operand in (
                layer_owner, block_assign, gradient_tiles[0], qa_basis[0], jnp.swapaxes(qg_basis[0], -1, -2),
                qg_values[0], qa_values[0],
            )
        )
    )
    return out[None]


def solution(mesh):
    in_specs = (
        P("grp", "dp", None),
        P("grp", None, "dp", None),
        P("grp", None, None, None, "dp"),
        P("grp", None, None),
        P("grp", None, None, None),
        P(),
        P(),
    )
    out_specs = P("grp", None, None)
    return jax.shard_map(local, mesh=mesh, in_specs=in_specs, out_specs=out_specs, check_vma=False)
```

```python
import functools

import jax
import jax.numpy as jnp
from jax import lax
from jax.experimental import pallas as pl
from jax.experimental.pallas import tpu as pltpu
from jax.sharding import PartitionSpec as P

MESH = pl.DeviceIdType.MESH
DAMPING = 0.1
NZ = 8
STRIP = 48
PIECE = 16
WIDTH = 1536
LANES = 128
N_DP = 32
HALF = WIDTH // 2
QUARTER = WIDTH // 4
TILE = 256
N_SEM = 320


def works(x, z):
    return (z + 2 * x) % 4 != 3


def rank(x, z):
    return x * 6 + z - (z + 2 * x) // 4


def kernel(
    owner_hbm, assign_hbm, g_hbm, a_hbm, q_hbm, lg_hbm, la_hbm, out_ref,
    owner_ref, assign_ref, lgv, lav, g, av, qv, qsel, qr_low, qr_high, qs, qt, qx_low, qx_high, qc, aq, ac, ax, vsel, vy, vx, vc, fg, fa, fq, p, lgc, sc, bp, bo, bi, bk, bc, bt,
    ssem, rsem, lsem, a_recv, b_recv,
):
    member = lax.axis_index("grp")
    dp = lax.axis_index("dp")
    xh, y = member // 4, member % 4
    x, z, c = dp // 16, (dp // 2) % NZ, dp % 2

    load_g = [
        pltpu.make_async_copy(g_hbm.at[:, n * QUARTER:(n + 1) * QUARTER], g.at[n], lsem.at[7 + n]) for n in range(4)
    ]
    load_a = [
        pltpu.make_async_copy(a_hbm.at[:, :, n * QUARTER:(n + 1) * QUARTER], av.at[n], lsem.at[11 + n])
        for n in range(4)
    ]
    load_q = pltpu.make_async_copy(q_hbm, qv, lsem.at[2])
    loads = [
        pltpu.make_async_copy(src, dst, lsem.at[3 + n])
        for n, (src, dst) in enumerate(
            ((owner_hbm, owner_ref), (assign_hbm, assign_ref), (lg_hbm, lgv), (la_hbm, lav))
        )
    ]
    for load in load_a:
        load.start()
    for load in load_g:
        load.start()
    for load in loads:
        load.start()
    load_q.start()
    core0 = c == 0

    def dp_of(dx, dz, dc):
        return dx * 16 + dz * 2 + dc

    def dev(gx, gy, dx, dz, dc):
        return (gx * 4 + gy, dp_of(dx, dz, dc))

    sibling = dev(xh, y, x, z, 1 - c)
    across = dev(xh, y, 1 - x, z, c)
    up = dev(xh, y, x, (z + 1) % NZ, c)
    down = dev(xh, y, x, (z + NZ - 1) % NZ, c)
    across_other = dev(xh, y, 1 - x, z, 1 - c)
    up_other = dev(xh, y, x, (z + 1) % NZ, 1 - c)
    down_other = dev(xh, y, x, (z + NZ - 1) % NZ, 1 - c)
    partner = dev(1 - xh, y, x, z, c)

    barrier = pltpu.get_barrier_semaphore()

    near = [up, down, up_other, down_other, partner]
    near += [
        dev(xh, (y + k // 4) % 4, (x + k // 2) % 2, z, (c + k) % 2) for k in range(1, 16)
    ]
    for target in near:
        pl.semaphore_signal(barrier, inc=1, device_id=target, device_id_type=MESH)
    pl.semaphore_wait(barrier, len(near))

    count = [0]
    pending = []

    def number():
        count[0] += 1
        assert count[0] <= N_SEM
        return count[0] - 1

    def copy(m, src, dst, target):
        return pltpu.make_async_remote_copy(
            src_ref=src, dst_ref=dst, send_sem=ssem.at[m], recv_sem=rsem.at[m],
            device_id=target, device_id_type=MESH,
        )

    def send(m, src, dst, target, when=None):
        started = copy(m, src, dst, target)
        pending.append((started, when))
        if when is None:
            started.start()
        else:
            pl.when(when)(started.start)

    def drain(until=None):
        for started, when in pending[:until]:
            if when is None:
                started.wait_send()
            else:
                pl.when(when)(started.wait_send)
        del pending[:until]

    def arrive(m, dst, target, when=None):
        landed = copy(m, dst, dst, target)
        if when is None:
            landed.wait_recv()
        else:
            pl.when(when)(landed.wait_recv)

    class Gather:
        def __init__(self, ref, full, half=None, exists=None):
            self.ref, self.full, self.cut, self.mid = ref, full, full // 2, full // 4
            self.half = half or (lambda bx, bz, bc, to: ref(bx, bz, bc, 0, full))
            self.exists = exists or (lambda bx, bz: None)
            self.sib_waits = []
            self.m = {}

        def key(self, *name):
            if name not in self.m:
                self.m[name] = number()
            return self.m[name]

        def to_sibling(self, bx, bz):
            m = number()
            ref = self.half(bx, bz, c, 1 - c)
            send(m, ref, ref, sibling, self.exists(bx, bz))
            self.sib_waits.append((m, self.half(bx, bz, 1 - c, c), self.exists(bx, bz)))

        def move(self, name, target, bx, bz, first, last):
            ref = self.ref(bx, bz, c, first, last)
            send(self.key(*name), ref, ref, target, self.exists(bx, bz))

        def wait(self, name, bx, bz, first, last, bc=c):
            arrive(self.key(*name), self.ref(bx, bz, bc, first, last), sibling, self.exists(bx, bz))

        def low(self, name, target, bx, bz):
            self.move(name, target, bx, bz, 0, self.cut)

        def high(self, name, target, bx, bz):
            self.move(name, target, bx, bz, self.cut, self.full)

        def wait_low(self, name, bx, bz):
            self.wait(name, bx, bz, 0, self.cut)

        def wait_high(self, name, bx, bz):
            self.wait(name, bx, bz, self.cut, self.full)

        def begin_low(self):
            self.low(("x", 0), across, x, z)
            self.low(("ul", 1), up, x, z)
            self.low(("dl", 1), down, x, z)

        def begin_high(self):
            self.high(("xh", 0), across, x, z)
            if self is gq:
                self.paired = self.whole(x)
            self.high(("uh", 1), up, x, z)
            self.high(("dh", 1), down, x, z)
            if self is not gq:
                self.to_sibling(x, z)

        def whole(self, bx):
            m = number()
            ref = self.ref(bx, z, c, 0, self.full)
            send(m, ref, ref, sibling)
            return m, self.ref(bx, z, 1 - c, 0, self.full)

        def swap(self):
            self.wait_low(("x", 0), 1 - x, z)
            self.low(("uq", 1), up, 1 - x, z)
            self.low(("dq", 1), down, 1 - x, z)

        def from_x(self):
            self.wait_high(("xh", 0), 1 - x, z)
            if self is gq:
                self.crossing = self.whole(1 - x)
            else:
                self.to_sibling(1 - x, z)

        def step(self, s):
            lo, hi = (z + NZ - s) % NZ, (z + s) % NZ
            self.wait_high(("uh", s), x, lo)
            self.high(("uh", s + 1), up, x, lo)
            self.high(("xu", s), across, x, lo)
            self.wait_high(("dh", s), x, hi)
            if s < 3:
                self.high(("dh", s + 1), down, x, hi)
            self.high(("xd", s), across, x, hi)
            self.wait_low(("ul", s), x, lo)
            if s < 3:
                self.low(("ul", s + 1), up, x, lo)
            self.wait_low(("dl", s), x, hi)
            self.low(("dl", s + 1), down, x, hi)
            self.wait_low(("uq", s), 1 - x, lo)
            if s < 3:
                self.low(("uq", s + 1), up, 1 - x, lo)
            else:
                self.move(("uq", 4), up, 1 - x, lo, 0, self.mid)
                self.move(("uc", 4), up_other, 1 - x, lo, 0, self.mid)
            self.wait_low(("dq", s), 1 - x, hi)
            if s < 3:
                self.low(("dq", s + 1), down, 1 - x, hi)
            else:
                self.move(("dq", 4), down, 1 - x, hi, self.mid, self.cut)
                self.move(("dc", 4), down_other, 1 - x, hi, self.mid, self.cut)
            self.to_sibling(x, lo)
            self.to_sibling(x, hi)
            if s == 2 and self is not gq:
                self.from_x()
            if s > 1:
                self.crossed(s - 1)

        def crossed(self, s):
            lo, hi = (z + NZ - s) % NZ, (z + s) % NZ
            self.wait_high(("xu", s), 1 - x, lo)
            self.to_sibling(1 - x, lo)
            self.wait_high(("xd", s), 1 - x, hi)
            self.to_sibling(1 - x, hi)

        def last(self):
            far = (z + 4) % NZ
            self.wait_high(("uh", 4), x, far)
            self.high(("xu", 4), across, x, far)
            self.high(("xc", 4), across_other, x, far)
            self.wait_low(("dl", 4), x, far)
            self.to_sibling(x, far)
            self.crossed(3)
            self.wait(("uq", 4), 1 - x, far, 0, self.mid)
            self.wait(("dq", 4), 1 - x, far, self.mid, self.cut)
            self.wait_high(("xu", 4), 1 - x, far)

        def end(self):
            far = (z + 4) % NZ
            for m, ref, when in self.sib_waits:
                arrive(m, ref, sibling, when)
            self.wait(("uc", 4), 1 - x, far, 0, self.mid, 1 - c)
            self.wait(("dc", 4), 1 - x, far, self.mid, self.cut, 1 - c)
            self.wait(("xc", 4), 1 - x, far, self.cut, self.full, 1 - c)

    def strip_at(bz, bc):
        return pl.ds(pl.multiple_of((bz * 2 + bc) * STRIP, PIECE), STRIP)

    def strip_of(bz):
        return pl.ds(pl.multiple_of(bz * STRIP, PIECE), STRIP)

    def at_z(bz):
        return pl.ds(pl.multiple_of(bz * 2 * STRIP, PIECE), 2 * STRIP)

    def half_of(core):
        return pl.ds(pl.multiple_of(core * HALF, LANES), HALF)

    class Ring:
        def __init__(self, f):
            self.f = f
            self.m = {}
            self.m4 = [number() for _ in range(3)]

        def share(self, strip):
            self.f[x, strip_at(z, c), :] = strip[x * 2 + c]
            for n, (dx, dc) in enumerate(((1, 0), (1, 1), (0, 1))):
                bx, bc = (x + dx) % 2, (c + dc) % 2
                send(self.m4[n], strip.at[bx * 2 + bc], self.f.at[x, strip_at(z, c), :], dev(xh, y, bx, z, bc))

        def begin(self):
            for n, (dx, dc) in enumerate(((1, 0), (1, 1), (0, 1))):
                bx, bc = (x + dx) % 2, (c + dc) % 2
                arrive(self.m4[n], self.f.at[bx, strip_at(z, bc), :], sibling)
            for n in range(2):
                self.move("u", 1, n, up, z)
                self.move("d", 1, n, down, z)

        def move(self, way, s, n, target, bz):
            ref = self.f.at[n, at_z(bz), :]
            self.m[way, s, n] = number()
            send(self.m[way, s, n], ref, ref, target)

        def wait(self, way, s, n, bz):
            arrive(self.m[way, s, n], self.f.at[n, at_z(bz), :], sibling)

        def step(self, s):
            lo, hi = (z + NZ - s) % NZ, (z + s) % NZ
            for n in range(2):
                self.wait("u", s, n, lo)
                if s < 3 or n == 0:
                    self.move("u", s + 1, n, up, lo)
                self.wait("d", s, n, hi)
                if s < 3 or n == 1:
                    self.move("d", s + 1, n, down, hi)

        def last(self):
            far = (z + 4) % NZ
            self.wait("u", 4, 0, far)
            self.wait("d", 4, 1, far)

    def by_strips(bx, bz, bc, first, last):
        return fq.at[bc, bx, strip_of(bz), first:last]

    def by_columns(bx, bz, bc, first, last):
        cols = pl.ds(pl.multiple_of(rank(bx, bz) * LANES, LANES), LANES)
        return out_ref.at[pl.ds(pl.multiple_of(bc * HALF + first, PIECE), last - first), cols]

    gg = Ring(fg)
    gq = Gather(
        by_strips, WIDTH, half=lambda bx, bz, bc, to: fq.at[bc, bx, strip_of(bz), half_of(to)]
    )
    go = Gather(by_columns, HALF, exists=lambda bx, bz: works(bx, bz))

    own = pl.ds(pl.multiple_of(dp * STRIP, PIECE), STRIP)

    for load in load_a:
        load.wait()
    mine_a = x * 2 + c
    in_place = mine_a == y
    for n in range(4):
        started = pltpu.make_async_remote_copy(
            src_ref=av.at[n], dst_ref=aq.at[y], send_sem=ssem.at[number()], recv_sem=a_recv.at[y],
            device_id=(xh * 4 + mine_a, dp_of(n // 2, z, n % 2)), device_id_type=MESH,
        )
        there = jnp.logical_not(jnp.logical_and(in_place, y == n))
        pl.when(there)(started.start)
        pending.append((started, there))

    @pl.when(in_place)
    def _():
        aq[y] = av[y]

    for load in load_g:
        load.wait()
    gg.share(g)

    for load in loads:
        load.wait()
    owner = owner_ref[xh]
    other = owner_ref[1 - xh]
    is_far = lax.bitwise_xor(lax.shift_right_logical(owner, 2), xh)
    owner_y = lax.bitwise_and(owner, 3)
    other_y = lax.bitwise_and(other, 3)
    load_q.wait()
    for layer in range(2):
        for slot in range(4):
            qsel[layer, slot] = qv[layer, assign_ref[layer, slot]]
    y_up, y_down = (xh * 4 + (y + 1) % 4, dp), (xh * 4 + (y + 3) % 4, dp)
    far, above, below = (y + 2) % 4, (y + 1) % 4, (y + 3) % 4
    m_q1, m_q2, m_q3 = ([number() for _ in range(2)] for _ in range(3))
    send(m_q1[0], qsel.at[:, far, :, :HALF], qr_low.at[:, 1], y_up)
    send(m_q1[1], qsel.at[:, far, :, HALF:], qr_high.at[:, 1], y_down)
    send(m_q3[0], qsel.at[:, above, :, HALF:], qt.at[:, 1, :, HALF:], y_up)
    send(m_q3[1], qsel.at[:, below, :, :HALF], qt.at[:, 2, :, :HALF], y_down)
    gg.begin()

    for layer in range(2):
        qr_low[layer, 0] = qsel[layer, above, :, :HALF]
        qr_high[layer, 0] = qsel[layer, below, :, HALF:]
        qt[layer, 0] = qsel[layer, y]
    owners_y = [lax.bitwise_and(owner_ref[layer], 3) for layer in range(2)]

    def one_if(condition):
        return jnp.where(condition, 1, 0)

    arrive(m_q1[0], qr_low.at[:, 1], y_down)
    for layer in range(2):
        qs[0, layer] = qr_low[layer, one_if(owners_y[layer] == below)]
    send(m_q2[0], qs.at[0], qt.at[:, 1, :, :HALF], y_up)
    arrive(m_q1[1], qr_high.at[:, 1], y_up)
    for layer in range(2):
        qs[1, layer] = qr_high[layer, one_if(owners_y[layer] == above)]
    send(m_q2[1], qs.at[1], qt.at[:, 2, :, HALF:], y_down)

    for k in range(1, 4):
        m_a = (y + k) % 4
        pltpu.make_async_remote_copy(
            src_ref=aq.at[m_a], dst_ref=aq.at[m_a], send_sem=ssem.at[0], recv_sem=a_recv.at[m_a],
            device_id=sibling, device_id_type=MESH,
        ).wait_recv()

    @pl.when(jnp.logical_not(in_place))
    def _():
        pltpu.make_async_remote_copy(
            src_ref=aq.at[y], dst_ref=aq.at[y], send_sem=ssem.at[0], recv_sem=a_recv.at[y],
            device_id=sibling, device_id_type=MESH,
        ).wait_recv()

    m_ax = number()
    ac[...] = aq[other_y, 1 - xh]
    send(m_ax, ac, ax.at[1], partner)
    ax[0] = aq[owner_y, xh]

    m_vy = [number() for _ in range(3)]
    for layer in range(2):
        la_all = lav[...].astype(jnp.float32)[layer:layer + 1]
        lg_all = lgv[layer].astype(jnp.float32)
        at_row = lax.broadcasted_iota(jnp.int32, lg_all.shape, 0)
        for slot in range(4):
            lg = jnp.sum(jnp.where(at_row == assign_ref[layer, slot], lg_all, 0.0), axis=0, keepdims=True)
            for n in range(WIDTH // LANES):
                cols = slice(n * LANES, (n + 1) * LANES)
                vsel[slot, layer, 0, n:n + 1] = lg[:, cols]
                vsel[slot, layer, 1, n:n + 1] = la_all[:, cols]
    vy[y] = vsel[y]
    for k in range(1, 4):
        to = (y + k) % 4
        send(m_vy[k - 1], vsel.at[to], vy.at[y], (xh * 4 + to, dp))
    gg.step(1)
    arrive(m_ax, ax.at[1], partner)
    fa[y // 2, z, y % 2] = ax[is_far]
    m_a = {}

    def ring_a(way, s, bz):
        ref = fa.at[y // 2, bz, y % 2]
        m_a[way, s] = number()
        send(m_a[way, s], ref, ref, up if way == "u" else down)

    def step_a(s):
        lo, hi = (z + NZ - s) % NZ, (z + s) % NZ
        arrive(m_a["u", s], fa.at[y // 2, lo, y % 2], sibling)
        if s < 4:
            ring_a("u", s + 1, lo)
            arrive(m_a["d", s], fa.at[y // 2, hi, y % 2], sibling)
        if s < 3:
            ring_a("d", s + 1, hi)

    def blocks_a(s):
        lo, hi = (z + NZ - s) % NZ, (z + s) % NZ
        return (lo,) if s in (0, 4) else (lo, hi)

    m_y = {}

    def move_y(name, s, n, target, ref):
        m_y[name, s, n] = number()
        send(m_y[name, s, n], ref, ref, target)

    def cross_y(s):
        for n, bz in enumerate(blocks_a(s)):
            ref = fa.at[y // 2, bz, y % 2]
            move_y("u", s, n, y_up, ref)
            move_y("d", s, n, y_down, ref)

    def relay_y(s):
        for n, bz in enumerate(blocks_a(s)):
            from_below, from_above = fa.at[below // 2, bz, below % 2], fa.at[above // 2, bz, above % 2]
            arrive(m_y["u", s, n], from_below, sibling)
            if n == 0:
                move_y("f", s, n, y_up, from_below)
            arrive(m_y["d", s, n], from_above, sibling)
            if n == 1:
                move_y("f", s, n, y_down, from_above)

    def finish_y(s):
        for n, bz in enumerate(blocks_a(s)):
            arrive(m_y["f", s, n], fa.at[far // 2, bz, far % 2], sibling)

    ring_a("u", 1, z)
    ring_a("d", 1, z)
    cross_y(0)

    arrive(m_q3[0], qt.at[:, 1, :, HALF:], y_down)
    arrive(m_q3[1], qt.at[:, 2, :, :HALF], y_up)
    arrive(m_q2[0], qt.at[:, 1, :, :HALF], y_down)
    arrive(m_q2[1], qt.at[:, 2, :, HALF:], y_up)
    for k in range(1, 4):
        arrive(m_vy[k - 1], vy.at[(y + 4 - k) % 4], partner)

    def came(layer, column_half):
        away = lax.bitwise_and(lax.bitwise_and(owner_ref[layer], 3) + 4 - y, 3)
        by_below = (away >= 2) if column_half == 0 else (away == 3)
        return jnp.where(away == 0, 0, jnp.where(by_below, 1, 2))

    m_qx, m_vx = [number() for _ in range(2)], number()
    for n in range(2):
        half = slice(n * HALF, (n + 1) * HALF)
        qc[n] = qt[1 - xh, came(1 - xh, n), :, half]
        send(m_qx[n], qc.at[n], (qx_low, qx_high)[n].at[1], partner)
    vc[...] = vy[other_y, 1 - xh]
    send(m_vx, vc, vx.at[1], partner)
    for n in range(2):
        half = slice(n * HALF, (n + 1) * HALF)
        (qx_low, qx_high)[n][0] = qt[xh, came(xh, n), :, half]
    vx[0] = vy[owner_y, xh]
    gg.step(2)

    step_a(1)
    cross_y(1)
    gg.step(3)
    relay_y(0)
    step_a(2)
    cross_y(2)
    relay_y(1)
    arrive(m_qx[0], qx_low.at[1], partner)
    fq[c, x, strip_of(z), :HALF] = qx_low[is_far]
    gq.begin_low()
    arrive(m_qx[1], qx_high.at[1], partner)
    fq[c, x, strip_of(z), HALF:] = qx_high[is_far]
    gq.begin_high()
    step_a(3)
    cross_y(3)
    gq.swap()
    step_a(4)
    cross_y(4)
    relay_y(2)
    gq.from_x()
    gg.last()
    relay_y(3)

    arrive(*gq.paired, sibling)
    arrive(*gq.crossing, sibling)

    def flat(value):
        return value.reshape((-1, value.shape[-1]))

    p[x * 2 + c] = jnp.dot(
        flat(fq[:, :, strip_of(z), :]), flat(fg[...]), preferred_element_type=jnp.float32
    ).astype(jnp.bfloat16)
    m_p = [number() for _ in range(3)]
    p_own, p_far = p.at[x * 2 + c], p.at[(1 - x) * 2 + c]
    send(m_p[0], p_own, p_own, across)
    send(m_p[1], p_own, p_own, sibling)
    gq.step(1)
    arrive(m_vx, vx.at[1], partner)
    for n in range(WIDTH // LANES):
        lg_row = vx[is_far, 0, n:n + 1, :]
        lgc[n * LANES:(n + 1) * LANES, :] = jnp.transpose(jnp.broadcast_to(lg_row, (LANES, LANES)))
    relay_y(4)
    arrive(m_p[0], p_far, across)
    send(m_p[2], p_far, p_far, sibling)
    gq.step(2)
    for s in range(5):
        finish_y(s)

    arrive(m_p[1], p.at[x * 2 + 1 - c], sibling)
    arrive(m_p[2], p.at[(1 - x) * 2 + 1 - c], sibling)
    eigen = sum(
        jnp.dot(p[n], flat(fa[n // 2, n % 2 * 4:n % 2 * 4 + 4]), preferred_element_type=jnp.float32)
        for n in range(4)
    )
    lg_col = jnp.concatenate([lgc[pl.ds(pl.multiple_of(bx * HALF + (z * 2 + bc) * STRIP, PIECE), STRIP), :]
                              for bc in range(2) for bx in range(2)])
    for n in range(QUARTER // LANES):
        la_row = vx[is_far, 1, pl.ds((x * 2 + c) * (QUARTER // LANES) + n, 1), :]
        cols = slice(n * LANES, (n + 1) * LANES)
        sc[:, cols] = (eigen[:, cols] / (lg_col * la_row + DAMPING)).astype(jnp.bfloat16)

    for bx in range(2):
        for n in range(2):
            part = lax.dot_general(
                sc[...], flat(fa[bx, n * 4:n * 4 + 4]), (((1,), (1,)), ((), ())), preferred_element_type=jnp.float32
            ).reshape((2, 2, STRIP, QUARTER))
            cols = slice(bx * HALF + n * QUARTER, bx * HALF + (n + 1) * QUARTER)
            bp[:, :, :, cols] = part
            bo[:, :, :, cols] = part.astype(jnp.bfloat16)
    m_b = number()
    send(m_b, bo.at[1 - c], bi, sibling)
    gq.step(3)
    arrive(m_b, bi, sibling)
    done = (bp[c] + bi[...].astype(jnp.float32)).astype(jnp.bfloat16)
    for j in range(WIDTH // LANES):
        bk[j] = done[:, :, j * LANES:(j + 1) * LANES]

    for wx in range(2):
        for wz in range(NZ):
            if (wz + 2 * wx) % 4 == 3:
                continue
            part = bk.at[wx * 6 + wz - (wz + 2 * wx) // 4]
            to_self = jnp.logical_and(x == wx, z == wz)
            others = jnp.logical_not(to_self)
            started = pltpu.make_async_remote_copy(
                src_ref=part, dst_ref=bc.at[x, :, strip_of(z), :], send_sem=ssem.at[number()],
                recv_sem=b_recv.at[x * NZ + z], device_id=dev(xh, y, wx, wz, c), device_id_type=MESH,
            )
            pl.when(others)(started.start)
            pending.append((started, others))

            @pl.when(to_self)
            def _():
                bc[x, :, strip_of(z), :] = part[...]

    gq.last()
    is_worker = works(x, z)
    m_bt = number()

    @pl.when(is_worker)
    def _():
        def take(k, carry):
            n = (x * NZ + z + k) % 16
            block = bc.at[n // NZ, :, strip_of(n % NZ), :]
            pltpu.make_async_remote_copy(
                src_ref=block, dst_ref=block, send_sem=ssem.at[m_bt], recv_sem=b_recv.at[n],
                device_id=sibling, device_id_type=MESH,
            ).wait_recv()
            return carry

        lax.fori_loop(1, 16, take, 0)
        total = flat(bc[0].astype(jnp.float32) + bc[1].astype(jnp.float32))
        for n in range(HALF // LANES):
            cols = slice(n * LANES, (n + 1) * LANES)
            bt[c, :, cols] = jnp.transpose(total[cols, :]).astype(jnp.bfloat16)

    send(m_bt, bt.at[c], bt.at[c], sibling, is_worker)
    gq.end()
    arrive(m_bt, bt.at[1 - c], sibling, is_worker)

    mine = pl.ds(pl.multiple_of(rank(x, z) * LANES, LANES), LANES)

    def finish(n):
        @pl.when(is_worker)
        def _():
            rows = pl.ds(pl.multiple_of(c * HALF + n * QUARTER, LANES), QUARTER)
            part = sum(
                jnp.dot(bt[k], flat(fq[k, :, :, rows]), preferred_element_type=jnp.float32) for k in range(2)
            )
            out_ref[rows, mine] = jnp.transpose(part).astype(jnp.bfloat16)

    finish(0)
    go.begin_low()
    finish(1)
    go.begin_high()
    drain()
    go.swap()
    go.step(1)
    early = len(pending)
    go.step(2)
    go.step(3)
    drain(early)
    go.last()
    go.end()
    drain()


def local(gradient_tiles, qa_basis, qg_basis, qa_values, qg_values, layer_owner, block_assign):
    strip = (STRIP, WIDTH)
    bf = jnp.bfloat16
    f32 = jnp.float32
    out = pl.pallas_call(
        kernel,
        out_shape=jax.ShapeDtypeStruct((WIDTH, WIDTH), bf),
        in_specs=[pl.BlockSpec(memory_space=pltpu.HBM)] * 7,
        out_specs=pl.BlockSpec(memory_space=pltpu.VMEM),
        scratch_shapes=[
            pltpu.SMEM((2,), jnp.int32),
            pltpu.SMEM((2, 4), jnp.int32),
            pltpu.VMEM((2, 16, WIDTH), bf),
            pltpu.VMEM((2, WIDTH), bf),
            pltpu.VMEM((4, STRIP, QUARTER), bf),
            pltpu.VMEM((4, 2, STRIP, QUARTER), bf),
            pltpu.VMEM((2, 16) + strip, bf),
            pltpu.VMEM((2, 4) + strip, bf),
            pltpu.VMEM((2, 2, STRIP, HALF), bf),
            pltpu.VMEM((2, 2, STRIP, HALF), bf),
            pltpu.VMEM((2, 2, STRIP, HALF), bf),
            pltpu.VMEM((2, 3) + strip, bf),
            pltpu.VMEM((2, STRIP, HALF), bf),
            pltpu.VMEM((2, STRIP, HALF), bf),
            pltpu.VMEM((2, STRIP, HALF), bf),
            pltpu.VMEM((4, 2, STRIP, QUARTER), bf),
            pltpu.VMEM((STRIP, QUARTER), bf),
            pltpu.VMEM((2, STRIP, QUARTER), bf),
            pltpu.VMEM((4, 2, 2, 16, LANES), f32),
            pltpu.VMEM((4, 2, 2, 16, LANES), f32),
            pltpu.VMEM((2, 2, 16, LANES), f32),
            pltpu.VMEM((2, 16, LANES), f32),
            pltpu.VMEM((2, HALF, QUARTER), bf),
            pltpu.VMEM((2, NZ, 2, STRIP, QUARTER), bf),
            pltpu.VMEM((2, 2, HALF // 2, WIDTH), bf),
            pltpu.VMEM((4, 4 * STRIP, QUARTER), bf),
            pltpu.VMEM((WIDTH, LANES), f32),
            pltpu.VMEM((4 * STRIP, QUARTER), bf),
            pltpu.VMEM((2, 2) + strip, f32),
            pltpu.VMEM((2, 2) + strip, bf),
            pltpu.VMEM((2,) + strip, bf),
            pltpu.VMEM((12, 2, STRIP, LANES), bf),
            pltpu.VMEM((2, 2, HALF // 2, LANES), bf),
            pltpu.VMEM((2, LANES, HALF), bf),
            pltpu.SemaphoreType.DMA((N_SEM,)),
            pltpu.SemaphoreType.DMA((N_SEM,)),
            pltpu.SemaphoreType.DMA((15,)),
            pltpu.SemaphoreType.DMA((4,)),
            pltpu.SemaphoreType.DMA((16,)),
        ],
        compiler_params=pltpu.CompilerParams(
            collective_id=0, has_side_effects=True, vmem_limit_bytes=48 * 1024 * 1024
        ),
        cost_estimate=pl.CostEstimate(flops=4 * 2 * 48 * 1536 * 1536, bytes_accessed=10_000_000, transcendentals=0),
    )(
        *(
            pltpu.with_memory_space_constraint(operand, pltpu.HBM)
            for operand in (
                layer_owner, block_assign, gradient_tiles[0], qa_basis[0], jnp.swapaxes(qg_basis[0], -1, -2),
                qg_values[0], qa_values[0],
            )
        )
    )
    return out[None]


def solution(mesh):
    in_specs = (
        P("grp", "dp", None),
        P("grp", None, "dp", None),
        P("grp", None, None, None, "dp"),
        P("grp", None, None),
        P("grp", None, None, None),
        P(),
        P(),
    )
    out_specs = P("grp", None, None)
    return jax.shard_map(local, mesh=mesh, in_specs=in_specs, out_specs=out_specs, check_vma=False)
```

```python
import functools

import jax
import jax.numpy as jnp
from jax import lax
from jax.experimental import pallas as pl
from jax.experimental.pallas import tpu as pltpu
from jax.sharding import PartitionSpec as P

MESH = pl.DeviceIdType.MESH
DAMPING = 0.1
NZ = 8
STRIP = 48
PIECE = 16
WIDTH = 1536
LANES = 128
N_DP = 32
HALF = WIDTH // 2
QUARTER = WIDTH // 4
TILE = 256
N_SEM = 320


def works(x, z):
    return (z + 2 * x) % 4 != 3


def rank(x, z):
    return x * 6 + z - (z + 2 * x) // 4


def kernel(
    owner_hbm, assign_hbm, g_hbm, a_hbm, q_hbm, lg_hbm, la_hbm, out_ref,
    owner_ref, assign_ref, lgv, lav, g, av, qv, qsel, qr_low, qr_high, qs, qt, qx_low, qx_high, qc, aq, ac, ax, vsel, vsb, vy, vx, vc, vf, fg, fa, fq, p, lgc, sc, bp, bo, bi, bk, bc, bt,
    ssem, rsem, lsem, a_recv, b_recv,
):
    member = lax.axis_index("grp")
    dp = lax.axis_index("dp")
    xh, y = member // 4, member % 4
    x, z, c = dp // 16, (dp // 2) % NZ, dp % 2

    load_g = [
        pltpu.make_async_copy(g_hbm.at[:, n * QUARTER:(n + 1) * QUARTER], g.at[n], lsem.at[7 + n]) for n in range(4)
    ]
    load_a = [
        pltpu.make_async_copy(a_hbm.at[:, :, n * QUARTER:(n + 1) * QUARTER], av.at[n], lsem.at[11 + n])
        for n in range(4)
    ]
    load_q = pltpu.make_async_copy(q_hbm, qv, lsem.at[2])
    loads = [
        pltpu.make_async_copy(src, dst, lsem.at[3 + n])
        for n, (src, dst) in enumerate(
            ((owner_hbm, owner_ref), (assign_hbm, assign_ref), (lg_hbm, lgv), (la_hbm, lav))
        )
    ]
    for load in load_a:
        load.start()
    for load in load_g:
        load.start()
    for load in loads:
        load.start()
    load_q.start()
    core0 = c == 0

    def dp_of(dx, dz, dc):
        return dx * 16 + dz * 2 + dc

    def dev(gx, gy, dx, dz, dc):
        return (gx * 4 + gy, dp_of(dx, dz, dc))

    sibling = dev(xh, y, x, z, 1 - c)
    across = dev(xh, y, 1 - x, z, c)
    up = dev(xh, y, x, (z + 1) % NZ, c)
    down = dev(xh, y, x, (z + NZ - 1) % NZ, c)
    partner = dev(1 - xh, y, x, z, c)

    barrier = pltpu.get_barrier_semaphore()

    near = [up, down, partner]
    near += [
        dev(xh, (y + k // 4) % 4, (x + k // 2) % 2, z, (c + k) % 2) for k in range(1, 16)
    ]
    for target in near:
        pl.semaphore_signal(barrier, inc=1, device_id=target, device_id_type=MESH)
    pl.semaphore_wait(barrier, len(near))

    count = [0]
    pending = []

    def number():
        count[0] += 1
        assert count[0] <= N_SEM
        return count[0] - 1

    def copy(m, src, dst, target):
        return pltpu.make_async_remote_copy(
            src_ref=src, dst_ref=dst, send_sem=ssem.at[m], recv_sem=rsem.at[m],
            device_id=target, device_id_type=MESH,
        )

    def send(m, src, dst, target, when=None):
        started = copy(m, src, dst, target)
        pending.append((started, when))
        if when is None:
            started.start()
        else:
            pl.when(when)(started.start)

    def drain(until=None):
        for started, when in pending[:until]:
            if when is None:
                started.wait_send()
            else:
                pl.when(when)(started.wait_send)
        del pending[:until]

    def arrive(m, dst, target, when=None):
        landed = copy(m, dst, dst, target)
        if when is None:
            landed.wait_recv()
        else:
            pl.when(when)(landed.wait_recv)

    class Gather:
        def __init__(self, ref, full, exists=None, alone=False):
            self.ref, self.full, self.cut, self.mid = ref, full, full // 2, 2 * LANES if alone else full // 4
            self.alone = alone
            self.exists = exists or (lambda bx, bz: None)
            self.sib_waits = []
            self.m = {}

        def key(self, *name):
            if name not in self.m:
                self.m[name] = number()
            return self.m[name]

        def to_sibling(self, bx, bz):
            if self.alone:
                return
            m = number()
            ref = self.ref(bx, bz, c, 0, self.full)
            send(m, ref, ref, sibling, self.exists(bx, bz))
            self.sib_waits.append((m, self.ref(bx, bz, 1 - c, 0, self.full), self.exists(bx, bz)))

        def move(self, name, target, bx, bz, first, last):
            ref = self.ref(bx, bz, c, first, last)
            send(self.key(*name), ref, ref, target, self.exists(bx, bz))

        def wait(self, name, bx, bz, first, last, bc=c):
            arrive(self.key(*name), self.ref(bx, bz, bc, first, last), sibling, self.exists(bx, bz))

        def low(self, name, target, bx, bz):
            self.move(name, target, bx, bz, 0, self.cut)

        def high(self, name, target, bx, bz):
            self.move(name, target, bx, bz, self.cut, self.full)

        def wait_low(self, name, bx, bz):
            self.wait(name, bx, bz, 0, self.cut)

        def wait_high(self, name, bx, bz):
            self.wait(name, bx, bz, self.cut, self.full)

        def begin_low(self):
            self.low(("x", 0), across, x, z)
            self.low(("ul", 1), up, x, z)
            self.low(("dl", 1), down, x, z)

        def begin_high(self):
            self.high(("xh", 0), across, x, z)
            self.high(("uh", 1), up, x, z)
            self.high(("dh", 1), down, x, z)
            self.to_sibling(x, z)

        def swap(self):
            self.wait_low(("x", 0), 1 - x, z)
            self.low(("uq", 1), up, 1 - x, z)
            self.low(("dq", 1), down, 1 - x, z)

        def from_x(self):
            self.wait_high(("xh", 0), 1 - x, z)
            self.to_sibling(1 - x, z)

        def step(self, s):
            lo, hi = (z + NZ - s) % NZ, (z + s) % NZ
            self.wait_high(("uh", s), x, lo)
            self.high(("uh", s + 1), up, x, lo)
            self.high(("xu", s), across, x, lo)
            self.wait_high(("dh", s), x, hi)
            if s < 3:
                self.high(("dh", s + 1), down, x, hi)
            self.high(("xd", s), across, x, hi)
            self.wait_low(("ul", s), x, lo)
            if s < 3:
                self.low(("ul", s + 1), up, x, lo)
            self.wait_low(("dl", s), x, hi)
            self.low(("dl", s + 1), down, x, hi)
            self.wait_low(("uq", s), 1 - x, lo)
            if s < 3:
                self.low(("uq", s + 1), up, 1 - x, lo)
            else:
                self.move(("uq", 4), up, 1 - x, lo, 0, self.mid)
            self.wait_low(("dq", s), 1 - x, hi)
            if s < 3:
                self.low(("dq", s + 1), down, 1 - x, hi)
            else:
                self.move(("dq", 4), down, 1 - x, hi, self.mid, self.cut)
            self.to_sibling(x, lo)
            self.to_sibling(x, hi)
            if s == 2 and not self.alone:
                self.from_x()
            if s > 1:
                self.crossed(s - 1)

        def crossed(self, s):
            lo, hi = (z + NZ - s) % NZ, (z + s) % NZ
            self.wait_high(("xu", s), 1 - x, lo)
            self.to_sibling(1 - x, lo)
            self.wait_high(("xd", s), 1 - x, hi)
            self.to_sibling(1 - x, hi)

        def last(self):
            far = (z + 4) % NZ
            self.wait_high(("uh", 4), x, far)
            self.high(("xu", 4), across, x, far)
            self.wait_low(("dl", 4), x, far)
            self.to_sibling(x, far)
            self.crossed(3)
            self.wait(("uq", 4), 1 - x, far, 0, self.mid)
            self.wait(("dq", 4), 1 - x, far, self.mid, self.cut)
            self.wait_high(("xu", 4), 1 - x, far)
            self.to_sibling(1 - x, far)

        def end(self):
            for m, ref, when in self.sib_waits:
                arrive(m, ref, sibling, when)

    def strip_at(bz, bc):
        return pl.ds(pl.multiple_of((bz * 2 + bc) * STRIP, PIECE), STRIP)

    def strip_of(bz):
        return pl.ds(pl.multiple_of(bz * STRIP, PIECE), STRIP)

    def at_z(bz):
        return pl.ds(pl.multiple_of(bz * 2 * STRIP, PIECE), 2 * STRIP)

    class Ring:
        def __init__(self, f):
            self.f = f
            self.m = {}
            self.m4 = [number() for _ in range(3)]

        def share(self, strip):
            self.f[x, strip_at(z, c), :] = strip[x * 2 + c]
            for n, (dx, dc) in enumerate(((1, 0), (1, 1), (0, 1))):
                bx, bc = (x + dx) % 2, (c + dc) % 2
                send(self.m4[n], strip.at[bx * 2 + bc], self.f.at[x, strip_at(z, c), :], dev(xh, y, bx, z, bc))

        def begin(self):
            for n, (dx, dc) in enumerate(((1, 0), (1, 1), (0, 1))):
                bx, bc = (x + dx) % 2, (c + dc) % 2
                arrive(self.m4[n], self.f.at[bx, strip_at(z, bc), :], sibling)
            for n in range(2):
                self.move("u", 1, n, up, z)
                self.move("d", 1, n, down, z)

        def move(self, way, s, n, target, bz):
            ref = self.f.at[n, at_z(bz), :]
            self.m[way, s, n] = number()
            send(self.m[way, s, n], ref, ref, target)

        def wait(self, way, s, n, bz):
            arrive(self.m[way, s, n], self.f.at[n, at_z(bz), :], sibling)

        def step(self, s):
            lo, hi = (z + NZ - s) % NZ, (z + s) % NZ
            for n in range(2):
                self.wait("u", s, n, lo)
                if s < 3 or n == 0:
                    self.move("u", s + 1, n, up, lo)
                self.wait("d", s, n, hi)
                if s < 3 or n == 1:
                    self.move("d", s + 1, n, down, hi)

        def last(self):
            far = (z + 4) % NZ
            self.wait("u", 4, 0, far)
            self.wait("d", 4, 1, far)

    def by_strips(bx, bz, bc, first, last):
        cols = pl.ds(pl.multiple_of(bc * HALF + first, LANES), last - first)
        return fq.at[:, bx, strip_of(bz), cols]

    def by_columns(bx, bz, bc, first, last):
        cols = pl.ds(pl.multiple_of(rank(bx, bz) * LANES, LANES), LANES)
        return out_ref.at[pl.ds(pl.multiple_of(bc * HALF + first, PIECE), last - first), cols]

    gg = Ring(fg)
    gq = Gather(by_strips, HALF, alone=True)
    go = Gather(by_columns, HALF, exists=lambda bx, bz: works(bx, bz))

    own = pl.ds(pl.multiple_of(dp * STRIP, PIECE), STRIP)

    for load in load_a:
        load.wait()
    mine_a = x * 2 + c
    in_place = mine_a == y
    for n in range(4):
        started = pltpu.make_async_remote_copy(
            src_ref=av.at[n], dst_ref=aq.at[y], send_sem=ssem.at[number()], recv_sem=a_recv.at[y],
            device_id=(xh * 4 + mine_a, dp_of(n // 2, z, n % 2)), device_id_type=MESH,
        )
        there = jnp.logical_not(jnp.logical_and(in_place, y == n))
        pl.when(there)(started.start)
        pending.append((started, there))

    @pl.when(in_place)
    def _():
        aq[y] = av[y]

    for load in load_g:
        load.wait()
    gg.share(g)

    for load in loads:
        load.wait()
    owner = owner_ref[xh]
    other = owner_ref[1 - xh]
    is_far = lax.bitwise_xor(lax.shift_right_logical(owner, 2), xh)
    owner_y = lax.bitwise_and(owner, 3)
    other_y = lax.bitwise_and(other, 3)
    load_q.wait()
    for layer in range(2):
        for slot in range(4):
            qsel[layer, slot] = qv[layer, assign_ref[layer, slot]]
    y_up, y_down = (xh * 4 + (y + 1) % 4, dp), (xh * 4 + (y + 3) % 4, dp)
    far, above, below = (y + 2) % 4, (y + 1) % 4, (y + 3) % 4
    m_q1, m_q2, m_q3 = ([number() for _ in range(2)] for _ in range(3))
    send(m_q1[0], qsel.at[:, far, :, :HALF], qr_low.at[:, 1], y_up)
    send(m_q1[1], qsel.at[:, far, :, HALF:], qr_high.at[:, 1], y_down)
    send(m_q3[0], qsel.at[:, above, :, HALF:], qt.at[:, 1, :, HALF:], y_up)
    send(m_q3[1], qsel.at[:, below, :, :HALF], qt.at[:, 2, :, :HALF], y_down)
    gg.begin()

    for layer in range(2):
        qr_low[layer, 0] = qsel[layer, above, :, :HALF]
        qr_high[layer, 0] = qsel[layer, below, :, HALF:]
        qt[layer, 0] = qsel[layer, y]
    owners_y = [lax.bitwise_and(owner_ref[layer], 3) for layer in range(2)]

    def one_if(condition):
        return jnp.where(condition, 1, 0)

    arrive(m_q1[0], qr_low.at[:, 1], y_down)
    for layer in range(2):
        qs[0, layer] = qr_low[layer, one_if(owners_y[layer] == below)]
    send(m_q2[0], qs.at[0], qt.at[:, 1, :, :HALF], y_up)
    arrive(m_q1[1], qr_high.at[:, 1], y_up)
    for layer in range(2):
        qs[1, layer] = qr_high[layer, one_if(owners_y[layer] == above)]
    send(m_q2[1], qs.at[1], qt.at[:, 2, :, HALF:], y_down)

    for k in range(1, 4):
        m_a = (y + k) % 4
        pltpu.make_async_remote_copy(
            src_ref=aq.at[m_a], dst_ref=aq.at[m_a], send_sem=ssem.at[0], recv_sem=a_recv.at[m_a],
            device_id=sibling, device_id_type=MESH,
        ).wait_recv()

    @pl.when(jnp.logical_not(in_place))
    def _():
        pltpu.make_async_remote_copy(
            src_ref=aq.at[y], dst_ref=aq.at[y], send_sem=ssem.at[0], recv_sem=a_recv.at[y],
            device_id=sibling, device_id_type=MESH,
        ).wait_recv()

    m_ax = number()
    ac[...] = aq[other_y, 1 - xh]
    send(m_ax, ac, ax.at[1], partner)
    ax[0] = aq[owner_y, xh]

    m_vy = [number() for _ in range(3)]
    for layer in range(2):
        la_all = lav[...].astype(jnp.float32)[layer:layer + 1]
        lg_all = lgv[layer].astype(jnp.float32)
        at_row = lax.broadcasted_iota(jnp.int32, lg_all.shape, 0)
        for slot in range(4):
            lg = jnp.sum(jnp.where(at_row == assign_ref[layer, slot], lg_all, 0.0), axis=0, keepdims=True)
            for n in range(WIDTH // LANES):
                cols = slice(n * LANES, (n + 1) * LANES)
                vsel[slot, layer, 0, n:n + 1] = lg[:, cols]
                vsel[slot, layer, 1, n:n + 1] = la_all[:, cols]
    vsb[...] = vsel[...].astype(jnp.bfloat16)
    vy[y] = vsb[y]
    for k in range(1, 4):
        to = (y + k) % 4
        send(m_vy[k - 1], vsb.at[to], vy.at[y], (xh * 4 + to, dp))
    gg.step(1)
    arrive(m_ax, ax.at[1], partner)
    fa[y // 2, z, y % 2] = ax[is_far]
    m_a = {}

    def ring_a(way, s, bz):
        ref = fa.at[y // 2, bz, y % 2]
        m_a[way, s] = number()
        send(m_a[way, s], ref, ref, up if way == "u" else down)

    def step_a(s):
        lo, hi = (z + NZ - s) % NZ, (z + s) % NZ
        arrive(m_a["u", s], fa.at[y // 2, lo, y % 2], sibling)
        if s < 4:
            ring_a("u", s + 1, lo)
            arrive(m_a["d", s], fa.at[y // 2, hi, y % 2], sibling)
        if s < 3:
            ring_a("d", s + 1, hi)

    def blocks_a(s):
        lo, hi = (z + NZ - s) % NZ, (z + s) % NZ
        return (lo,) if s in (0, 4) else (lo, hi)

    m_y = {}

    def move_y(name, s, n, target, ref):
        m_y[name, s, n] = number()
        send(m_y[name, s, n], ref, ref, target)

    def cross_y(s):
        for n, bz in enumerate(blocks_a(s)):
            ref = fa.at[y // 2, bz, y % 2]
            move_y("u", s, n, y_up, ref)
            move_y("d", s, n, y_down, ref)

    def relay_y(s):
        for n, bz in enumerate(blocks_a(s)):
            from_below, from_above = fa.at[below // 2, bz, below % 2], fa.at[above // 2, bz, above % 2]
            arrive(m_y["u", s, n], from_below, sibling)
            if n == 0:
                move_y("f", s, n, y_up, from_below)
            arrive(m_y["d", s, n], from_above, sibling)
            if n == 1:
                move_y("f", s, n, y_down, from_above)

    def finish_y(s):
        for n, bz in enumerate(blocks_a(s)):
            arrive(m_y["f", s, n], fa.at[far // 2, bz, far % 2], sibling)

    ring_a("u", 1, z)
    ring_a("d", 1, z)
    cross_y(0)

    arrive(m_q3[0], qt.at[:, 1, :, HALF:], y_down)
    arrive(m_q3[1], qt.at[:, 2, :, :HALF], y_up)
    arrive(m_q2[0], qt.at[:, 1, :, :HALF], y_down)
    arrive(m_q2[1], qt.at[:, 2, :, HALF:], y_up)
    for k in range(1, 4):
        arrive(m_vy[k - 1], vy.at[(y + 4 - k) % 4], partner)

    def came(layer, column_half):
        away = lax.bitwise_and(lax.bitwise_and(owner_ref[layer], 3) + 4 - y, 3)
        by_below = (away >= 2) if column_half == 0 else (away == 3)
        return jnp.where(away == 0, 0, jnp.where(by_below, 1, 2))

    m_qx, m_vx = [number() for _ in range(2)], number()
    for n in range(2):
        half = slice(n * HALF, (n + 1) * HALF)
        qc[n] = qt[1 - xh, came(1 - xh, n), :, half]
        send(m_qx[n], qc.at[n], (qx_low, qx_high)[n].at[1], partner)
    vc[...] = vy[other_y, 1 - xh]
    send(m_vx, vc, vx.at[1], partner)
    for n in range(2):
        half = slice(n * HALF, (n + 1) * HALF)
        (qx_low, qx_high)[n][0] = qt[xh, came(xh, n), :, half]
    vx[0] = vy[owner_y, xh]
    gg.step(2)

    step_a(1)
    cross_y(1)
    gg.step(3)
    relay_y(0)
    step_a(2)
    cross_y(2)
    relay_y(1)
    m_s = [number() for _ in range(3)]
    for n, strip_half in enumerate((qx_low, qx_high)):
        arrive(m_qx[n], strip_half.at[1], partner)
        cols = slice(n * HALF, (n + 1) * HALF)
        fq[c, x, strip_of(z), cols] = strip_half[is_far]
        part = fq.at[c, x, strip_of(z), cols]
        send(m_s[n], part, part, sibling)
    for n in range(2):
        arrive(m_s[n], fq.at[1 - c, x, strip_of(z), n * HALF:(n + 1) * HALF], sibling)
    gq.begin_low()
    gq.begin_high()
    step_a(3)
    cross_y(3)
    gq.swap()
    step_a(4)
    cross_y(4)
    relay_y(2)
    gq.from_x()
    came_over = by_strips(1 - x, z, c, 0, HALF)
    send(m_s[2], came_over, came_over, sibling)
    gg.last()
    relay_y(3)

    arrive(m_s[2], by_strips(1 - x, z, 1 - c, 0, HALF), sibling)

    def flat(value):
        return value.reshape((-1, value.shape[-1]))

    p[x * 2 + c] = jnp.dot(
        flat(fq[:, :, strip_of(z), :]), flat(fg[...]), preferred_element_type=jnp.float32
    ).astype(jnp.bfloat16)
    m_p = [number() for _ in range(3)]
    p_own, p_far = p.at[x * 2 + c], p.at[(1 - x) * 2 + c]
    send(m_p[0], p_own, p_own, across)
    send(m_p[1], p_own, p_own, sibling)
    gq.step(1)
    arrive(m_vx, vx.at[1], partner)
    vf[...] = vx[is_far].astype(jnp.float32)
    for n in range(WIDTH // LANES):
        lg_row = vf[0, n:n + 1, :]
        lgc[n * LANES:(n + 1) * LANES, :] = jnp.transpose(jnp.broadcast_to(lg_row, (LANES, LANES)))
    relay_y(4)
    arrive(m_p[0], p_far, across)
    send(m_p[2], p_far, p_far, sibling)
    gq.step(2)
    for s in range(5):
        finish_y(s)

    arrive(m_p[1], p.at[x * 2 + 1 - c], sibling)
    arrive(m_p[2], p.at[(1 - x) * 2 + 1 - c], sibling)
    eigen = sum(
        jnp.dot(p[n], flat(fa[n // 2, n % 2 * 4:n % 2 * 4 + 4]), preferred_element_type=jnp.float32)
        for n in range(4)
    )
    lg_col = jnp.concatenate([lgc[pl.ds(pl.multiple_of(bx * HALF + (z * 2 + bc) * STRIP, PIECE), STRIP), :]
                              for bc in range(2) for bx in range(2)])
    for n in range(QUARTER // LANES):
        la_row = vf[1, pl.ds((x * 2 + c) * (QUARTER // LANES) + n, 1), :]
        cols = slice(n * LANES, (n + 1) * LANES)
        sc[:, cols] = (eigen[:, cols] / (lg_col * la_row + DAMPING)).astype(jnp.bfloat16)

    for bx in range(2):
        for n in range(2):
            part = lax.dot_general(
                sc[...], flat(fa[bx, n * 4:n * 4 + 4]), (((1,), (1,)), ((), ())), preferred_element_type=jnp.float32
            ).reshape((2, 2, STRIP, QUARTER))
            cols = slice(bx * HALF + n * QUARTER, bx * HALF + (n + 1) * QUARTER)
            bp[:, :, :, cols] = part
            bo[:, :, :, cols] = part.astype(jnp.bfloat16)
    m_b = number()
    send(m_b, bo.at[1 - c], bi, sibling)
    gq.step(3)
    arrive(m_b, bi, sibling)
    done = (bp[c] + bi[...].astype(jnp.float32)).astype(jnp.bfloat16)
    for j in range(WIDTH // LANES):
        bk[j] = done[:, :, j * LANES:(j + 1) * LANES]

    for wx in range(2):
        for wz in range(NZ):
            if (wz + 2 * wx) % 4 == 3:
                continue
            part = bk.at[wx * 6 + wz - (wz + 2 * wx) // 4]
            to_self = jnp.logical_and(x == wx, z == wz)
            others = jnp.logical_not(to_self)
            started = pltpu.make_async_remote_copy(
                src_ref=part, dst_ref=bc.at[x, :, strip_of(z), :], send_sem=ssem.at[number()],
                recv_sem=b_recv.at[x * NZ + z], device_id=dev(xh, y, wx, wz, c), device_id_type=MESH,
            )
            pl.when(others)(started.start)
            pending.append((started, others))

            @pl.when(to_self)
            def _():
                bc[x, :, strip_of(z), :] = part[...]

    gq.last()
    is_worker = works(x, z)
    m_bt = number()

    @pl.when(is_worker)
    def _():
        def take(k, carry):
            n = (x * NZ + z + k) % 16
            block = bc.at[n // NZ, :, strip_of(n % NZ), :]
            pltpu.make_async_remote_copy(
                src_ref=block, dst_ref=block, send_sem=ssem.at[m_bt], recv_sem=b_recv.at[n],
                device_id=sibling, device_id_type=MESH,
            ).wait_recv()
            return carry

        lax.fori_loop(1, 16, take, 0)
        total = flat(bc[0].astype(jnp.float32) + bc[1].astype(jnp.float32))
        for n in range(HALF // LANES):
            cols = slice(n * LANES, (n + 1) * LANES)
            bt[c, :, cols] = jnp.transpose(total[cols, :]).astype(jnp.bfloat16)

    send(m_bt, bt.at[c], bt.at[c], sibling, is_worker)
    arrive(m_bt, bt.at[1 - c], sibling, is_worker)

    mine = pl.ds(pl.multiple_of(rank(x, z) * LANES, LANES), LANES)

    def finish(n):
        @pl.when(is_worker)
        def _():
            rows = pl.ds(pl.multiple_of(c * HALF + n * QUARTER, LANES), QUARTER)
            part = sum(
                jnp.dot(bt[k], flat(fq[k, :, :, rows]), preferred_element_type=jnp.float32) for k in range(2)
            )
            out_ref[rows, mine] = jnp.transpose(part).astype(jnp.bfloat16)

    finish(0)
    go.begin_low()
    finish(1)
    go.begin_high()
    drain()
    go.swap()
    go.step(1)
    early = len(pending)
    go.step(2)
    go.step(3)
    drain(early)
    go.last()
    go.end()
    drain()


def local(gradient_tiles, qa_basis, qg_basis, qa_values, qg_values, layer_owner, block_assign):
    strip = (STRIP, WIDTH)
    bf = jnp.bfloat16
    f32 = jnp.float32
    out = pl.pallas_call(
        kernel,
        out_shape=jax.ShapeDtypeStruct((WIDTH, WIDTH), bf),
        in_specs=[pl.BlockSpec(memory_space=pltpu.HBM)] * 7,
        out_specs=pl.BlockSpec(memory_space=pltpu.VMEM),
        scratch_shapes=[
            pltpu.SMEM((2,), jnp.int32),
            pltpu.SMEM((2, 4), jnp.int32),
            pltpu.VMEM((2, 16, WIDTH), bf),
            pltpu.VMEM((2, WIDTH), bf),
            pltpu.VMEM((4, STRIP, QUARTER), bf),
            pltpu.VMEM((4, 2, STRIP, QUARTER), bf),
            pltpu.VMEM((2, 16) + strip, bf),
            pltpu.VMEM((2, 4) + strip, bf),
            pltpu.VMEM((2, 2, STRIP, HALF), bf),
            pltpu.VMEM((2, 2, STRIP, HALF), bf),
            pltpu.VMEM((2, 2, STRIP, HALF), bf),
            pltpu.VMEM((2, 3) + strip, bf),
            pltpu.VMEM((2, STRIP, HALF), bf),
            pltpu.VMEM((2, STRIP, HALF), bf),
            pltpu.VMEM((2, STRIP, HALF), bf),
            pltpu.VMEM((4, 2, STRIP, QUARTER), bf),
            pltpu.VMEM((STRIP, QUARTER), bf),
            pltpu.VMEM((2, STRIP, QUARTER), bf),
            pltpu.VMEM((4, 2, 2, 16, LANES), f32),
            pltpu.VMEM((4, 2, 2, 16, LANES), bf),
            pltpu.VMEM((4, 2, 2, 16, LANES), bf),
            pltpu.VMEM((2, 2, 16, LANES), bf),
            pltpu.VMEM((2, 16, LANES), bf),
            pltpu.VMEM((2, 16, LANES), f32),
            pltpu.VMEM((2, HALF, QUARTER), bf),
            pltpu.VMEM((2, NZ, 2, STRIP, QUARTER), bf),
            pltpu.VMEM((2, 2, HALF // 2, WIDTH), bf),
            pltpu.VMEM((4, 4 * STRIP, QUARTER), bf),
            pltpu.VMEM((WIDTH, LANES), f32),
            pltpu.VMEM((4 * STRIP, QUARTER), bf),
            pltpu.VMEM((2, 2) + strip, f32),
            pltpu.VMEM((2, 2) + strip, bf),
            pltpu.VMEM((2,) + strip, bf),
            pltpu.VMEM((12, 2, STRIP, LANES), bf),
            pltpu.VMEM((2, 2, HALF // 2, LANES), bf),
            pltpu.VMEM((2, LANES, HALF), bf),
            pltpu.SemaphoreType.DMA((N_SEM,)),
            pltpu.SemaphoreType.DMA((N_SEM,)),
            pltpu.SemaphoreType.DMA((15,)),
            pltpu.SemaphoreType.DMA((4,)),
            pltpu.SemaphoreType.DMA((16,)),
        ],
        compiler_params=pltpu.CompilerParams(
            collective_id=0, has_side_effects=True, vmem_limit_bytes=48 * 1024 * 1024
        ),
        cost_estimate=pl.CostEstimate(flops=4 * 2 * 48 * 1536 * 1536, bytes_accessed=10_000_000, transcendentals=0),
    )(
        *(
            pltpu.with_memory_space_constraint(operand, pltpu.HBM)
            for operand in (
                layer_owner, block_assign, gradient_tiles[0], qa_basis[0], jnp.swapaxes(qg_basis[0], -1, -2),
                qg_values[0], qa_values[0],
            )
        )
    )
    return out[None]


def solution(mesh):
    in_specs = (
        P("grp", "dp", None),
        P("grp", None, "dp", None),
        P("grp", None, None, None, "dp"),
        P("grp", None, None),
        P("grp", None, None, None),
        P(),
        P(),
    )
    out_specs = P("grp", None, None)
    return jax.shard_map(local, mesh=mesh, in_specs=in_specs, out_specs=out_specs, check_vma=False)
```

```python
import functools

import jax
import jax.numpy as jnp
from jax import lax
from jax.experimental import pallas as pl
from jax.experimental.pallas import tpu as pltpu
from jax.sharding import PartitionSpec as P

MESH = pl.DeviceIdType.MESH
DAMPING = 0.1
NZ = 8
STRIP = 48
PIECE = 16
WIDTH = 1536
LANES = 128
N_DP = 32
HALF = WIDTH // 2
QUARTER = WIDTH // 4
TILE = 256
N_SEM = 320


def works(x, z):
    return (z + 2 * x) % 4 != 3


def rank(x, z):
    return x * 6 + z - (z + 2 * x) // 4


def kernel(
    owner_hbm, assign_hbm, g_hbm, a_hbm, q_hbm, lg_hbm, la_hbm, out_ref,
    owner_ref, assign_ref, lgv, lav, g, av, qv, qsel, qr_low, qr_high, qs, qt, qx_low, qx_high, qc, aq, ac, ax, vsel, vsb, vy, vx, vc, vf, fg, fa, fq, p, lgc, sc, bp, bo, bi, bk, bc, bt,
    ssem, rsem, lsem, a_recv, b_recv,
):
    member = lax.axis_index("grp")
    dp = lax.axis_index("dp")
    xh, y = member // 4, member % 4
    x, z, c = dp // 16, (dp // 2) % NZ, dp % 2

    load_g = [
        pltpu.make_async_copy(g_hbm.at[:, n * QUARTER:(n + 1) * QUARTER], g.at[n], lsem.at[7 + n]) for n in range(4)
    ]
    load_a = [
        pltpu.make_async_copy(a_hbm.at[:, :, n * QUARTER:(n + 1) * QUARTER], av.at[n], lsem.at[11 + n])
        for n in range(4)
    ]
    load_q = pltpu.make_async_copy(q_hbm, qv, lsem.at[2])
    loads = [
        pltpu.make_async_copy(src, dst, lsem.at[3 + n])
        for n, (src, dst) in enumerate(
            ((owner_hbm, owner_ref), (assign_hbm, assign_ref), (lg_hbm, lgv), (la_hbm, lav))
        )
    ]
    for load in load_a:
        load.start()
    for load in load_g:
        load.start()
    for load in loads:
        load.start()
    load_q.start()
    core0 = c == 0

    def dp_of(dx, dz, dc):
        return dx * 16 + dz * 2 + dc

    def dev(gx, gy, dx, dz, dc):
        return (gx * 4 + gy, dp_of(dx, dz, dc))

    sibling = dev(xh, y, x, z, 1 - c)
    across = dev(xh, y, 1 - x, z, c)
    up = dev(xh, y, x, (z + 1) % NZ, c)
    down = dev(xh, y, x, (z + NZ - 1) % NZ, c)
    partner = dev(1 - xh, y, x, z, c)

    barrier = pltpu.get_barrier_semaphore()

    near = [up, down, partner]
    near += [
        dev(xh, (y + k // 4) % 4, (x + k // 2) % 2, z, (c + k) % 2) for k in range(1, 16)
    ]
    for target in near:
        pl.semaphore_signal(barrier, inc=1, device_id=target, device_id_type=MESH)
    pl.semaphore_wait(barrier, len(near))

    count = [0]
    pending = []

    def number():
        count[0] += 1
        assert count[0] <= N_SEM
        return count[0] - 1

    def copy(m, src, dst, target):
        return pltpu.make_async_remote_copy(
            src_ref=src, dst_ref=dst, send_sem=ssem.at[m], recv_sem=rsem.at[m],
            device_id=target, device_id_type=MESH,
        )

    def send(m, src, dst, target, when=None):
        started = copy(m, src, dst, target)
        pending.append((started, when))
        if when is None:
            started.start()
        else:
            pl.when(when)(started.start)

    def drain(until=None):
        for started, when in pending[:until]:
            if when is None:
                started.wait_send()
            else:
                pl.when(when)(started.wait_send)
        del pending[:until]

    def arrive(m, dst, target, when=None):
        landed = copy(m, dst, dst, target)
        if when is None:
            landed.wait_recv()
        else:
            pl.when(when)(landed.wait_recv)

    class Gather:
        def __init__(self, ref, full, exists=None, alone=False):
            self.ref, self.full, self.cut, self.mid = ref, full, full // 2, 2 * LANES if alone else full // 4
            self.alone = alone
            self.exists = exists or (lambda bx, bz: None)
            self.sib_waits = []
            self.m = {}

        def key(self, *name):
            if name not in self.m:
                self.m[name] = number()
            return self.m[name]

        def to_sibling(self, bx, bz):
            if self.alone:
                return
            m = number()
            ref = self.ref(bx, bz, c, 0, self.full)
            send(m, ref, ref, sibling, self.exists(bx, bz))
            self.sib_waits.append((m, self.ref(bx, bz, 1 - c, 0, self.full), self.exists(bx, bz)))

        def move(self, name, target, bx, bz, first, last):
            ref = self.ref(bx, bz, c, first, last)
            send(self.key(*name), ref, ref, target, self.exists(bx, bz))

        def wait(self, name, bx, bz, first, last, bc=c):
            arrive(self.key(*name), self.ref(bx, bz, bc, first, last), sibling, self.exists(bx, bz))

        def low(self, name, target, bx, bz):
            self.move(name, target, bx, bz, 0, self.cut)

        def high(self, name, target, bx, bz):
            self.move(name, target, bx, bz, self.cut, self.full)

        def wait_low(self, name, bx, bz):
            self.wait(name, bx, bz, 0, self.cut)

        def wait_high(self, name, bx, bz):
            self.wait(name, bx, bz, self.cut, self.full)

        def begin_low(self):
            self.low(("x", 0), across, x, z)
            self.low(("ul", 1), up, x, z)
            self.low(("dl", 1), down, x, z)

        def begin_high(self):
            self.high(("xh", 0), across, x, z)
            self.high(("uh", 1), up, x, z)
            self.high(("dh", 1), down, x, z)
            self.to_sibling(x, z)

        def swap(self):
            self.wait_low(("x", 0), 1 - x, z)
            self.low(("uq", 1), up, 1 - x, z)
            self.low(("dq", 1), down, 1 - x, z)

        def from_x(self):
            self.wait_high(("xh", 0), 1 - x, z)
            self.to_sibling(1 - x, z)

        def step(self, s):
            lo, hi = (z + NZ - s) % NZ, (z + s) % NZ
            self.wait_high(("uh", s), x, lo)
            self.high(("uh", s + 1), up, x, lo)
            self.high(("xu", s), across, x, lo)
            self.wait_high(("dh", s), x, hi)
            if s < 3:
                self.high(("dh", s + 1), down, x, hi)
            self.high(("xd", s), across, x, hi)
            self.wait_low(("ul", s), x, lo)
            if s < 3:
                self.low(("ul", s + 1), up, x, lo)
            self.wait_low(("dl", s), x, hi)
            self.low(("dl", s + 1), down, x, hi)
            self.wait_low(("uq", s), 1 - x, lo)
            if s < 3:
                self.low(("uq", s + 1), up, 1 - x, lo)
            else:
                self.move(("uq", 4), up, 1 - x, lo, 0, self.mid)
            self.wait_low(("dq", s), 1 - x, hi)
            if s < 3:
                self.low(("dq", s + 1), down, 1 - x, hi)
            else:
                self.move(("dq", 4), down, 1 - x, hi, self.mid, self.cut)
            self.to_sibling(x, lo)
            self.to_sibling(x, hi)
            if s == 2 and not self.alone:
                self.from_x()
            if s > 1:
                self.crossed(s - 1)

        def crossed(self, s):
            lo, hi = (z + NZ - s) % NZ, (z + s) % NZ
            self.wait_high(("xu", s), 1 - x, lo)
            self.to_sibling(1 - x, lo)
            self.wait_high(("xd", s), 1 - x, hi)
            self.to_sibling(1 - x, hi)

        def last(self):
            far = (z + 4) % NZ
            self.wait_high(("uh", 4), x, far)
            self.high(("xu", 4), across, x, far)
            self.wait_low(("dl", 4), x, far)
            self.to_sibling(x, far)
            self.crossed(3)
            self.wait(("uq", 4), 1 - x, far, 0, self.mid)
            self.wait(("dq", 4), 1 - x, far, self.mid, self.cut)
            self.wait_high(("xu", 4), 1 - x, far)
            self.to_sibling(1 - x, far)

        def end(self):
            for m, ref, when in self.sib_waits:
                arrive(m, ref, sibling, when)

    def strip_at(bz, bc):
        return pl.ds(pl.multiple_of((bz * 2 + bc) * STRIP, PIECE), STRIP)

    def strip_of(bz):
        return pl.ds(pl.multiple_of(bz * STRIP, PIECE), STRIP)

    def at_z(bz):
        return pl.ds(pl.multiple_of(bz * 2 * STRIP, PIECE), 2 * STRIP)

    class Ring:
        def __init__(self, f):
            self.f = f
            self.m = {}
            self.m4 = [number() for _ in range(3)]

        def share(self, strip):
            self.f[x, strip_at(z, c), :] = strip[x * 2 + c]
            for n, (dx, dc) in enumerate(((1, 0), (1, 1), (0, 1))):
                bx, bc = (x + dx) % 2, (c + dc) % 2
                send(self.m4[n], strip.at[bx * 2 + bc], self.f.at[x, strip_at(z, c), :], dev(xh, y, bx, z, bc))

        def begin(self):
            for n, (dx, dc) in enumerate(((1, 0), (1, 1), (0, 1))):
                bx, bc = (x + dx) % 2, (c + dc) % 2
                arrive(self.m4[n], self.f.at[bx, strip_at(z, bc), :], sibling)
            for n in range(2):
                self.move("u", 1, n, up, z)
                self.move("d", 1, n, down, z)

        def move(self, way, s, n, target, bz):
            ref = self.f.at[n, at_z(bz), :]
            self.m[way, s, n] = number()
            send(self.m[way, s, n], ref, ref, target)

        def wait(self, way, s, n, bz):
            arrive(self.m[way, s, n], self.f.at[n, at_z(bz), :], sibling)

        def step(self, s):
            lo, hi = (z + NZ - s) % NZ, (z + s) % NZ
            for n in range(2):
                self.wait("u", s, n, lo)
                if s < 3 or n == 0:
                    self.move("u", s + 1, n, up, lo)
                self.wait("d", s, n, hi)
                if s < 3 or n == 1:
                    self.move("d", s + 1, n, down, hi)

        def last(self):
            far = (z + 4) % NZ
            self.wait("u", 4, 0, far)
            self.wait("d", 4, 1, far)

    def by_strips(bx, bz, bc, first, last):
        cols = pl.ds(pl.multiple_of(bc * HALF + first, LANES), last - first)
        return fq.at[:, bx, strip_of(bz), cols]

    def by_columns(bx, bz, bc, first, last):
        cols = pl.ds(pl.multiple_of(rank(bx, bz) * LANES, LANES), LANES)
        return out_ref.at[pl.ds(pl.multiple_of(bc * HALF + first, PIECE), last - first), cols]

    gg = Ring(fg)
    gq = Gather(by_strips, HALF, alone=True)
    go = Gather(by_columns, HALF, exists=lambda bx, bz: works(bx, bz))

    own = pl.ds(pl.multiple_of(dp * STRIP, PIECE), STRIP)

    for load in load_g:
        load.wait()
    gg.share(g)

    for load in load_a:
        load.wait()
    mine_a = x * 2 + c
    in_place = mine_a == y
    for n in range(4):
        started = pltpu.make_async_remote_copy(
            src_ref=av.at[n], dst_ref=aq.at[y], send_sem=ssem.at[number()], recv_sem=a_recv.at[y],
            device_id=(xh * 4 + mine_a, dp_of(n // 2, z, n % 2)), device_id_type=MESH,
        )
        there = jnp.logical_not(jnp.logical_and(in_place, y == n))
        pl.when(there)(started.start)
        pending.append((started, there))

    @pl.when(in_place)
    def _():
        aq[y] = av[y]

    for load in loads:
        load.wait()
    owner = owner_ref[xh]
    other = owner_ref[1 - xh]
    is_far = lax.bitwise_xor(lax.shift_right_logical(owner, 2), xh)
    owner_y = lax.bitwise_and(owner, 3)
    other_y = lax.bitwise_and(other, 3)
    load_q.wait()
    for layer in range(2):
        for slot in range(4):
            qsel[layer, slot] = qv[layer, assign_ref[layer, slot]]
    y_up, y_down = (xh * 4 + (y + 1) % 4, dp), (xh * 4 + (y + 3) % 4, dp)
    far, above, below = (y + 2) % 4, (y + 1) % 4, (y + 3) % 4
    m_q1, m_q2, m_q3 = ([number() for _ in range(2)] for _ in range(3))
    send(m_q1[0], qsel.at[:, far, :, :HALF], qr_low.at[:, 1], y_up)
    send(m_q1[1], qsel.at[:, far, :, HALF:], qr_high.at[:, 1], y_down)
    send(m_q3[0], qsel.at[:, above, :, HALF:], qt.at[:, 1, :, HALF:], y_up)
    send(m_q3[1], qsel.at[:, below, :, :HALF], qt.at[:, 2, :, :HALF], y_down)
    gg.begin()

    for layer in range(2):
        qr_low[layer, 0] = qsel[layer, above, :, :HALF]
        qr_high[layer, 0] = qsel[layer, below, :, HALF:]
        qt[layer, 0] = qsel[layer, y]
    owners_y = [lax.bitwise_and(owner_ref[layer], 3) for layer in range(2)]

    def one_if(condition):
        return jnp.where(condition, 1, 0)

    arrive(m_q1[0], qr_low.at[:, 1], y_down)
    for layer in range(2):
        qs[0, layer] = qr_low[layer, one_if(owners_y[layer] == below)]
    send(m_q2[0], qs.at[0], qt.at[:, 1, :, :HALF], y_up)
    arrive(m_q1[1], qr_high.at[:, 1], y_up)
    for layer in range(2):
        qs[1, layer] = qr_high[layer, one_if(owners_y[layer] == above)]
    send(m_q2[1], qs.at[1], qt.at[:, 2, :, HALF:], y_down)

    for k in range(1, 4):
        m_a = (y + k) % 4
        pltpu.make_async_remote_copy(
            src_ref=aq.at[m_a], dst_ref=aq.at[m_a], send_sem=ssem.at[0], recv_sem=a_recv.at[m_a],
            device_id=sibling, device_id_type=MESH,
        ).wait_recv()

    @pl.when(jnp.logical_not(in_place))
    def _():
        pltpu.make_async_remote_copy(
            src_ref=aq.at[y], dst_ref=aq.at[y], send_sem=ssem.at[0], recv_sem=a_recv.at[y],
            device_id=sibling, device_id_type=MESH,
        ).wait_recv()

    m_ax = number()
    ac[...] = aq[other_y, 1 - xh]
    send(m_ax, ac, ax.at[1], partner)
    ax[0] = aq[owner_y, xh]

    gg.step(1)
    m_vy = [number() for _ in range(3)]
    for layer in range(2):
        la_all = lav[...].astype(jnp.float32)[layer:layer + 1]
        lg_all = lgv[layer].astype(jnp.float32)
        at_row = lax.broadcasted_iota(jnp.int32, lg_all.shape, 0)
        for slot in range(4):
            lg = jnp.sum(jnp.where(at_row == assign_ref[layer, slot], lg_all, 0.0), axis=0, keepdims=True)
            for n in range(WIDTH // LANES):
                cols = slice(n * LANES, (n + 1) * LANES)
                vsel[slot, layer, 0, n:n + 1] = lg[:, cols]
                vsel[slot, layer, 1, n:n + 1] = la_all[:, cols]
    vsb[...] = vsel[...].astype(jnp.bfloat16)
    vy[y] = vsb[y]
    for k in range(1, 4):
        to = (y + k) % 4
        send(m_vy[k - 1], vsb.at[to], vy.at[y], (xh * 4 + to, dp))
    arrive(m_ax, ax.at[1], partner)
    fa[y // 2, z, y % 2] = ax[is_far]
    m_a = {}

    def ring_a(way, s, bz):
        ref = fa.at[y // 2, bz, y % 2]
        m_a[way, s] = number()
        send(m_a[way, s], ref, ref, up if way == "u" else down)

    def step_a(s):
        lo, hi = (z + NZ - s) % NZ, (z + s) % NZ
        arrive(m_a["u", s], fa.at[y // 2, lo, y % 2], sibling)
        if s < 4:
            ring_a("u", s + 1, lo)
            arrive(m_a["d", s], fa.at[y // 2, hi, y % 2], sibling)
        if s < 3:
            ring_a("d", s + 1, hi)

    def blocks_a(s):
        lo, hi = (z + NZ - s) % NZ, (z + s) % NZ
        return (lo,) if s in (0, 4) else (lo, hi)

    m_y = {}

    def move_y(name, s, n, target, ref):
        m_y[name, s, n] = number()
        send(m_y[name, s, n], ref, ref, target)

    def cross_y(s):
        for n, bz in enumerate(blocks_a(s)):
            ref = fa.at[y // 2, bz, y % 2]
            move_y("u", s, n, y_up, ref)
            move_y("d", s, n, y_down, ref)

    def relay_y(s):
        for n, bz in enumerate(blocks_a(s)):
            from_below, from_above = fa.at[below // 2, bz, below % 2], fa.at[above // 2, bz, above % 2]
            arrive(m_y["u", s, n], from_below, sibling)
            if n == 0:
                move_y("f", s, n, y_up, from_below)
            arrive(m_y["d", s, n], from_above, sibling)
            if n == 1:
                move_y("f", s, n, y_down, from_above)

    def finish_y(s):
        for n, bz in enumerate(blocks_a(s)):
            arrive(m_y["f", s, n], fa.at[far // 2, bz, far % 2], sibling)

    ring_a("u", 1, z)
    ring_a("d", 1, z)
    cross_y(0)
    gg.step(2)


    arrive(m_q3[0], qt.at[:, 1, :, HALF:], y_down)
    arrive(m_q3[1], qt.at[:, 2, :, :HALF], y_up)
    arrive(m_q2[0], qt.at[:, 1, :, :HALF], y_down)
    arrive(m_q2[1], qt.at[:, 2, :, HALF:], y_up)
    for k in range(1, 4):
        arrive(m_vy[k - 1], vy.at[(y + 4 - k) % 4], partner)

    def came(layer, column_half):
        away = lax.bitwise_and(lax.bitwise_and(owner_ref[layer], 3) + 4 - y, 3)
        by_below = (away >= 2) if column_half == 0 else (away == 3)
        return jnp.where(away == 0, 0, jnp.where(by_below, 1, 2))

    m_qx, m_vx = [number() for _ in range(2)], number()
    for n in range(2):
        half = slice(n * HALF, (n + 1) * HALF)
        qc[n] = qt[1 - xh, came(1 - xh, n), :, half]
        send(m_qx[n], qc.at[n], (qx_low, qx_high)[n].at[1], partner)
    vc[...] = vy[other_y, 1 - xh]
    send(m_vx, vc, vx.at[1], partner)
    for n in range(2):
        half = slice(n * HALF, (n + 1) * HALF)
        (qx_low, qx_high)[n][0] = qt[xh, came(xh, n), :, half]
    vx[0] = vy[owner_y, xh]
    step_a(1)
    cross_y(1)
    gg.step(3)
    relay_y(0)
    step_a(2)
    cross_y(2)
    relay_y(1)
    gg.last()
    m_s = [number() for _ in range(3)]
    for n, strip_half in enumerate((qx_low, qx_high)):
        arrive(m_qx[n], strip_half.at[1], partner)
        cols = slice(n * HALF, (n + 1) * HALF)
        fq[c, x, strip_of(z), cols] = strip_half[is_far]
        part = fq.at[c, x, strip_of(z), cols]
        send(m_s[n], part, part, sibling)
    for n in range(2):
        arrive(m_s[n], fq.at[1 - c, x, strip_of(z), n * HALF:(n + 1) * HALF], sibling)
    gq.begin_low()
    gq.begin_high()
    step_a(3)
    cross_y(3)
    gq.swap()
    step_a(4)
    cross_y(4)
    relay_y(2)
    gq.from_x()
    came_over = by_strips(1 - x, z, c, 0, HALF)
    send(m_s[2], came_over, came_over, sibling)
    relay_y(3)

    arrive(m_s[2], by_strips(1 - x, z, 1 - c, 0, HALF), sibling)

    def flat(value):
        return value.reshape((-1, value.shape[-1]))

    p[x * 2 + c] = jnp.dot(
        flat(fq[:, :, strip_of(z), :]), flat(fg[...]), preferred_element_type=jnp.float32
    ).astype(jnp.bfloat16)
    m_p = [number() for _ in range(3)]
    p_own, p_far = p.at[x * 2 + c], p.at[(1 - x) * 2 + c]
    send(m_p[0], p_own, p_own, across)
    send(m_p[1], p_own, p_own, sibling)
    gq.step(1)
    arrive(m_vx, vx.at[1], partner)
    vf[...] = vx[is_far].astype(jnp.float32)
    for n in range(WIDTH // LANES):
        lg_row = vf[0, n:n + 1, :]
        lgc[n * LANES:(n + 1) * LANES, :] = jnp.transpose(jnp.broadcast_to(lg_row, (LANES, LANES)))
    relay_y(4)
    arrive(m_p[0], p_far, across)
    send(m_p[2], p_far, p_far, sibling)
    gq.step(2)
    for s in range(5):
        finish_y(s)

    arrive(m_p[1], p.at[x * 2 + 1 - c], sibling)
    arrive(m_p[2], p.at[(1 - x) * 2 + 1 - c], sibling)
    eigen = sum(
        jnp.dot(p[n], flat(fa[n // 2, n % 2 * 4:n % 2 * 4 + 4]), preferred_element_type=jnp.float32)
        for n in range(4)
    )
    lg_col = jnp.concatenate([lgc[pl.ds(pl.multiple_of(bx * HALF + (z * 2 + bc) * STRIP, PIECE), STRIP), :]
                              for bc in range(2) for bx in range(2)])
    for n in range(QUARTER // LANES):
        la_row = vf[1, pl.ds((x * 2 + c) * (QUARTER // LANES) + n, 1), :]
        cols = slice(n * LANES, (n + 1) * LANES)
        sc[:, cols] = (eigen[:, cols] / (lg_col * la_row + DAMPING)).astype(jnp.bfloat16)

    for bx in range(2):
        for n in range(2):
            part = lax.dot_general(
                sc[...], flat(fa[bx, n * 4:n * 4 + 4]), (((1,), (1,)), ((), ())), preferred_element_type=jnp.float32
            ).reshape((2, 2, STRIP, QUARTER))
            cols = slice(bx * HALF + n * QUARTER, bx * HALF + (n + 1) * QUARTER)
            bp[:, :, :, cols] = part
            bo[:, :, :, cols] = part.astype(jnp.bfloat16)
    m_b = number()
    send(m_b, bo.at[1 - c], bi, sibling)
    gq.step(3)
    arrive(m_b, bi, sibling)
    done = (bp[c] + bi[...].astype(jnp.float32)).astype(jnp.bfloat16)
    for j in range(WIDTH // LANES):
        bk[j] = done[:, :, j * LANES:(j + 1) * LANES]

    for wx in range(2):
        for wz in range(NZ):
            if (wz + 2 * wx) % 4 == 3:
                continue
            part = bk.at[wx * 6 + wz - (wz + 2 * wx) // 4]
            to_self = jnp.logical_and(x == wx, z == wz)
            others = jnp.logical_not(to_self)
            started = pltpu.make_async_remote_copy(
                src_ref=part, dst_ref=bc.at[x, :, strip_of(z), :], send_sem=ssem.at[number()],
                recv_sem=b_recv.at[x * NZ + z], device_id=dev(xh, y, wx, wz, c), device_id_type=MESH,
            )
            pl.when(others)(started.start)
            pending.append((started, others))

            @pl.when(to_self)
            def _():
                bc[x, :, strip_of(z), :] = part[...]

    gq.last()
    is_worker = works(x, z)
    m_bt = number()

    @pl.when(is_worker)
    def _():
        def take(k, carry):
            n = (x * NZ + z + k) % 16
            block = bc.at[n // NZ, :, strip_of(n % NZ), :]
            pltpu.make_async_remote_copy(
                src_ref=block, dst_ref=block, send_sem=ssem.at[m_bt], recv_sem=b_recv.at[n],
                device_id=sibling, device_id_type=MESH,
            ).wait_recv()
            return carry

        lax.fori_loop(1, 16, take, 0)
        total = flat(bc[0].astype(jnp.float32) + bc[1].astype(jnp.float32))
        for n in range(HALF // LANES):
            cols = slice(n * LANES, (n + 1) * LANES)
            bt[c, :, cols] = jnp.transpose(total[cols, :]).astype(jnp.bfloat16)

    send(m_bt, bt.at[c], bt.at[c], sibling, is_worker)
    arrive(m_bt, bt.at[1 - c], sibling, is_worker)

    mine = pl.ds(pl.multiple_of(rank(x, z) * LANES, LANES), LANES)

    def finish(n):
        @pl.when(is_worker)
        def _():
            rows = pl.ds(pl.multiple_of(c * HALF + n * QUARTER, LANES), QUARTER)
            part = sum(
                jnp.dot(bt[k], flat(fq[k, :, :, rows]), preferred_element_type=jnp.float32) for k in range(2)
            )
            out_ref[rows, mine] = jnp.transpose(part).astype(jnp.bfloat16)

    finish(0)
    go.begin_low()
    finish(1)
    go.begin_high()
    drain()
    go.swap()
    go.step(1)
    early = len(pending)
    go.step(2)
    go.step(3)
    drain(early)
    go.last()
    go.end()
    drain()


def local(gradient_tiles, qa_basis, qg_basis, qa_values, qg_values, layer_owner, block_assign):
    strip = (STRIP, WIDTH)
    bf = jnp.bfloat16
    f32 = jnp.float32
    out = pl.pallas_call(
        kernel,
        out_shape=jax.ShapeDtypeStruct((WIDTH, WIDTH), bf),
        in_specs=[pl.BlockSpec(memory_space=pltpu.HBM)] * 7,
        out_specs=pl.BlockSpec(memory_space=pltpu.VMEM),
        scratch_shapes=[
            pltpu.SMEM((2,), jnp.int32),
            pltpu.SMEM((2, 4), jnp.int32),
            pltpu.VMEM((2, 16, WIDTH), bf),
            pltpu.VMEM((2, WIDTH), bf),
            pltpu.VMEM((4, STRIP, QUARTER), bf),
            pltpu.VMEM((4, 2, STRIP, QUARTER), bf),
            pltpu.VMEM((2, 16) + strip, bf),
            pltpu.VMEM((2, 4) + strip, bf),
            pltpu.VMEM((2, 2, STRIP, HALF), bf),
            pltpu.VMEM((2, 2, STRIP, HALF), bf),
            pltpu.VMEM((2, 2, STRIP, HALF), bf),
            pltpu.VMEM((2, 3) + strip, bf),
            pltpu.VMEM((2, STRIP, HALF), bf),
            pltpu.VMEM((2, STRIP, HALF), bf),
            pltpu.VMEM((2, STRIP, HALF), bf),
            pltpu.VMEM((4, 2, STRIP, QUARTER), bf),
            pltpu.VMEM((STRIP, QUARTER), bf),
            pltpu.VMEM((2, STRIP, QUARTER), bf),
            pltpu.VMEM((4, 2, 2, 16, LANES), f32),
            pltpu.VMEM((4, 2, 2, 16, LANES), bf),
            pltpu.VMEM((4, 2, 2, 16, LANES), bf),
            pltpu.VMEM((2, 2, 16, LANES), bf),
            pltpu.VMEM((2, 16, LANES), bf),
            pltpu.VMEM((2, 16, LANES), f32),
            pltpu.VMEM((2, HALF, QUARTER), bf),
            pltpu.VMEM((2, NZ, 2, STRIP, QUARTER), bf),
            pltpu.VMEM((2, 2, HALF // 2, WIDTH), bf),
            pltpu.VMEM((4, 4 * STRIP, QUARTER), bf),
            pltpu.VMEM((WIDTH, LANES), f32),
            pltpu.VMEM((4 * STRIP, QUARTER), bf),
            pltpu.VMEM((2, 2) + strip, f32),
            pltpu.VMEM((2, 2) + strip, bf),
            pltpu.VMEM((2,) + strip, bf),
            pltpu.VMEM((12, 2, STRIP, LANES), bf),
            pltpu.VMEM((2, 2, HALF // 2, LANES), bf),
            pltpu.VMEM((2, LANES, HALF), bf),
            pltpu.SemaphoreType.DMA((N_SEM,)),
            pltpu.SemaphoreType.DMA((N_SEM,)),
            pltpu.SemaphoreType.DMA((15,)),
            pltpu.SemaphoreType.DMA((4,)),
            pltpu.SemaphoreType.DMA((16,)),
        ],
        compiler_params=pltpu.CompilerParams(
            collective_id=0, has_side_effects=True, vmem_limit_bytes=48 * 1024 * 1024
        ),
        cost_estimate=pl.CostEstimate(flops=4 * 2 * 48 * 1536 * 1536, bytes_accessed=10_000_000, transcendentals=0),
    )(
        *(
            pltpu.with_memory_space_constraint(operand, pltpu.HBM)
            for operand in (
                layer_owner, block_assign, gradient_tiles[0], qa_basis[0], jnp.swapaxes(qg_basis[0], -1, -2),
                qg_values[0], qa_values[0],
            )
        )
    )
    return out[None]


def solution(mesh):
    in_specs = (
        P("grp", "dp", None),
        P("grp", None, "dp", None),
        P("grp", None, None, None, "dp"),
        P("grp", None, None),
        P("grp", None, None, None),
        P(),
        P(),
    )
    out_specs = P("grp", None, None)
    return jax.shard_map(local, mesh=mesh, in_specs=in_specs, out_specs=out_specs, check_vma=False)
```

```python
import functools

import jax
import jax.numpy as jnp
from jax import lax
from jax.experimental import pallas as pl
from jax.experimental.pallas import tpu as pltpu
from jax.sharding import PartitionSpec as P

MESH = pl.DeviceIdType.MESH
DAMPING = 0.1
NZ = 8
STRIP = 48
PIECE = 16
WIDTH = 1536
LANES = 128
N_DP = 32
HALF = WIDTH // 2
QUARTER = WIDTH // 4
TILE = 256
N_SEM = 320


def works(x, z):
    return (z + 2 * x) % 4 != 3


def rank(x, z):
    return x * 6 + z - (z + 2 * x) // 4


def kernel(
    owner_hbm, assign_hbm, g_hbm, a_hbm, q_hbm, lg_hbm, la_hbm, out_ref,
    owner_ref, assign_ref, lgv, lav, g, av, qv, qsel, qr_low, qr_high, qs, qt, qx_low, qx_high, qc, aq, ac, ax, vsel, vsb, vy, vx, vc, vf, fg, fa, fq, p, lgc, sc, bp, bo, bi, bk, bc, bt,
    ssem, rsem, lsem, a_recv, b_recv,
):
    member = lax.axis_index("grp")
    dp = lax.axis_index("dp")
    xh, y = member // 4, member % 4
    x, z, c = dp // 16, (dp // 2) % NZ, dp % 2

    load_g = [
        pltpu.make_async_copy(g_hbm.at[:, n * QUARTER:(n + 1) * QUARTER], g.at[n], lsem.at[7 + n]) for n in range(4)
    ]
    load_a = [
        pltpu.make_async_copy(a_hbm.at[:, :, n * QUARTER:(n + 1) * QUARTER], av.at[n], lsem.at[11 + n])
        for n in range(4)
    ]
    load_q = pltpu.make_async_copy(q_hbm, qv, lsem.at[2])
    loads = [
        pltpu.make_async_copy(src, dst, lsem.at[3 + n])
        for n, (src, dst) in enumerate(
            ((owner_hbm, owner_ref), (assign_hbm, assign_ref), (lg_hbm, lgv), (la_hbm, lav))
        )
    ]
    for load in load_a:
        load.start()
    for load in load_g:
        load.start()
    for load in loads:
        load.start()
    load_q.start()
    core0 = c == 0

    def dp_of(dx, dz, dc):
        return dx * 16 + dz * 2 + dc

    def dev(gx, gy, dx, dz, dc):
        return (gx * 4 + gy, dp_of(dx, dz, dc))

    sibling = dev(xh, y, x, z, 1 - c)
    across = dev(xh, y, 1 - x, z, c)
    up = dev(xh, y, x, (z + 1) % NZ, c)
    down = dev(xh, y, x, (z + NZ - 1) % NZ, c)
    partner = dev(1 - xh, y, x, z, c)

    barrier = pltpu.get_barrier_semaphore()

    near = [up, down, partner]
    near += [
        dev(xh, (y + k // 4) % 4, (x + k // 2) % 2, z, (c + k) % 2) for k in range(1, 16)
    ]
    for target in near:
        pl.semaphore_signal(barrier, inc=1, device_id=target, device_id_type=MESH)

    y_up, y_down = (xh * 4 + (y + 1) % 4, dp), (xh * 4 + (y + 3) % 4, dp)
    far, above, below = (y + 2) % 4, (y + 1) % 4, (y + 3) % 4
    for load in load_a:
        load.wait()
    for load in load_g:
        load.wait()
    for load in loads:
        load.wait()
    owner = owner_ref[xh]
    other = owner_ref[1 - xh]
    is_far = lax.bitwise_xor(lax.shift_right_logical(owner, 2), xh)
    owner_y = lax.bitwise_and(owner, 3)
    other_y = lax.bitwise_and(other, 3)
    load_q.wait()
    for layer in range(2):
        for slot in range(4):
            qsel[layer, slot] = qv[layer, assign_ref[layer, slot]]
    for layer in range(2):
        qr_low[layer, 0] = qsel[layer, above, :, :HALF]
        qr_high[layer, 0] = qsel[layer, below, :, HALF:]
        qt[layer, 0] = qsel[layer, y]
    for layer in range(2):
        la_all = lav[...].astype(jnp.float32)[layer:layer + 1]
        lg_all = lgv[layer].astype(jnp.float32)
        at_row = lax.broadcasted_iota(jnp.int32, lg_all.shape, 0)
        for slot in range(4):
            lg = jnp.sum(jnp.where(at_row == assign_ref[layer, slot], lg_all, 0.0), axis=0, keepdims=True)
            for n in range(WIDTH // LANES):
                cols = slice(n * LANES, (n + 1) * LANES)
                vsel[slot, layer, 0, n:n + 1] = lg[:, cols]
                vsel[slot, layer, 1, n:n + 1] = la_all[:, cols]
    vsb[...] = vsel[...].astype(jnp.bfloat16)
    vy[y] = vsb[y]

    pl.semaphore_wait(barrier, len(near))

    count = [0]
    pending = []

    def number():
        count[0] += 1
        assert count[0] <= N_SEM
        return count[0] - 1

    def copy(m, src, dst, target):
        return pltpu.make_async_remote_copy(
            src_ref=src, dst_ref=dst, send_sem=ssem.at[m], recv_sem=rsem.at[m],
            device_id=target, device_id_type=MESH,
        )

    def send(m, src, dst, target, when=None):
        started = copy(m, src, dst, target)
        pending.append((started, when))
        if when is None:
            started.start()
        else:
            pl.when(when)(started.start)

    def drain(until=None):
        for started, when in pending[:until]:
            if when is None:
                started.wait_send()
            else:
                pl.when(when)(started.wait_send)
        del pending[:until]

    def arrive(m, dst, target, when=None):
        landed = copy(m, dst, dst, target)
        if when is None:
            landed.wait_recv()
        else:
            pl.when(when)(landed.wait_recv)

    class Gather:
        def __init__(self, ref, full, exists=None, alone=False):
            self.ref, self.full, self.cut, self.mid = ref, full, full // 2, 2 * LANES if alone else full // 4
            self.alone = alone
            self.exists = exists or (lambda bx, bz: None)
            self.sib_waits = []
            self.m = {}

        def key(self, *name):
            if name not in self.m:
                self.m[name] = number()
            return self.m[name]

        def to_sibling(self, bx, bz):
            if self.alone:
                return
            m = number()
            ref = self.ref(bx, bz, c, 0, self.full)
            send(m, ref, ref, sibling, self.exists(bx, bz))
            self.sib_waits.append((m, self.ref(bx, bz, 1 - c, 0, self.full), self.exists(bx, bz)))

        def move(self, name, target, bx, bz, first, last):
            ref = self.ref(bx, bz, c, first, last)
            send(self.key(*name), ref, ref, target, self.exists(bx, bz))

        def wait(self, name, bx, bz, first, last, bc=c):
            arrive(self.key(*name), self.ref(bx, bz, bc, first, last), sibling, self.exists(bx, bz))

        def low(self, name, target, bx, bz):
            self.move(name, target, bx, bz, 0, self.cut)

        def high(self, name, target, bx, bz):
            self.move(name, target, bx, bz, self.cut, self.full)

        def wait_low(self, name, bx, bz):
            self.wait(name, bx, bz, 0, self.cut)

        def wait_high(self, name, bx, bz):
            self.wait(name, bx, bz, self.cut, self.full)

        def begin_low(self):
            self.low(("x", 0), across, x, z)
            self.low(("ul", 1), up, x, z)
            self.low(("dl", 1), down, x, z)

        def begin_high(self):
            self.high(("xh", 0), across, x, z)
            self.high(("uh", 1), up, x, z)
            self.high(("dh", 1), down, x, z)
            self.to_sibling(x, z)

        def swap(self):
            self.wait_low(("x", 0), 1 - x, z)
            self.low(("uq", 1), up, 1 - x, z)
            self.low(("dq", 1), down, 1 - x, z)

        def from_x(self):
            self.wait_high(("xh", 0), 1 - x, z)
            self.to_sibling(1 - x, z)

        def step(self, s):
            lo, hi = (z + NZ - s) % NZ, (z + s) % NZ
            self.wait_high(("uh", s), x, lo)
            self.high(("uh", s + 1), up, x, lo)
            self.high(("xu", s), across, x, lo)
            self.wait_high(("dh", s), x, hi)
            if s < 3:
                self.high(("dh", s + 1), down, x, hi)
            self.high(("xd", s), across, x, hi)
            self.wait_low(("ul", s), x, lo)
            if s < 3:
                self.low(("ul", s + 1), up, x, lo)
            self.wait_low(("dl", s), x, hi)
            self.low(("dl", s + 1), down, x, hi)
            self.wait_low(("uq", s), 1 - x, lo)
            if s < 3:
                self.low(("uq", s + 1), up, 1 - x, lo)
            else:
                self.move(("uq", 4), up, 1 - x, lo, 0, self.mid)
            self.wait_low(("dq", s), 1 - x, hi)
            if s < 3:
                self.low(("dq", s + 1), down, 1 - x, hi)
            else:
                self.move(("dq", 4), down, 1 - x, hi, self.mid, self.cut)
            self.to_sibling(x, lo)
            self.to_sibling(x, hi)
            if s == 2 and not self.alone:
                self.from_x()
            if s > 1:
                self.crossed(s - 1)

        def crossed(self, s):
            lo, hi = (z + NZ - s) % NZ, (z + s) % NZ
            self.wait_high(("xu", s), 1 - x, lo)
            self.to_sibling(1 - x, lo)
            self.wait_high(("xd", s), 1 - x, hi)
            self.to_sibling(1 - x, hi)

        def last(self):
            far = (z + 4) % NZ
            self.wait_high(("uh", 4), x, far)
            self.high(("xu", 4), across, x, far)
            self.wait_low(("dl", 4), x, far)
            self.to_sibling(x, far)
            self.crossed(3)
            self.wait(("uq", 4), 1 - x, far, 0, self.mid)
            self.wait(("dq", 4), 1 - x, far, self.mid, self.cut)
            self.wait_high(("xu", 4), 1 - x, far)
            self.to_sibling(1 - x, far)

        def end(self):
            for m, ref, when in self.sib_waits:
                arrive(m, ref, sibling, when)

    def strip_at(bz, bc):
        return pl.ds(pl.multiple_of((bz * 2 + bc) * STRIP, PIECE), STRIP)

    def strip_of(bz):
        return pl.ds(pl.multiple_of(bz * STRIP, PIECE), STRIP)

    def at_z(bz):
        return pl.ds(pl.multiple_of(bz * 2 * STRIP, PIECE), 2 * STRIP)

    class Ring:
        def __init__(self, f):
            self.f = f
            self.m = {}
            self.m4 = [number() for _ in range(3)]

        def share(self, strip):
            self.f[x, strip_at(z, c), :] = strip[x * 2 + c]
            for n, (dx, dc) in enumerate(((1, 0), (1, 1), (0, 1))):
                bx, bc = (x + dx) % 2, (c + dc) % 2
                send(self.m4[n], strip.at[bx * 2 + bc], self.f.at[x, strip_at(z, c), :], dev(xh, y, bx, z, bc))

        def begin(self):
            for n, (dx, dc) in enumerate(((1, 0), (1, 1), (0, 1))):
                bx, bc = (x + dx) % 2, (c + dc) % 2
                arrive(self.m4[n], self.f.at[bx, strip_at(z, bc), :], sibling)
            for n in range(2):
                self.move("u", 1, n, up, z)
                self.move("d", 1, n, down, z)

        def move(self, way, s, n, target, bz):
            ref = self.f.at[n, at_z(bz), :]
            self.m[way, s, n] = number()
            send(self.m[way, s, n], ref, ref, target)

        def wait(self, way, s, n, bz):
            arrive(self.m[way, s, n], self.f.at[n, at_z(bz), :], sibling)

        def step(self, s):
            lo, hi = (z + NZ - s) % NZ, (z + s) % NZ
            for n in range(2):
                self.wait("u", s, n, lo)
                if s < 3 or n == 0:
                    self.move("u", s + 1, n, up, lo)
                self.wait("d", s, n, hi)
                if s < 3 or n == 1:
                    self.move("d", s + 1, n, down, hi)

        def last(self):
            far = (z + 4) % NZ
            self.wait("u", 4, 0, far)
            self.wait("d", 4, 1, far)

    def by_strips(bx, bz, bc, first, last):
        cols = pl.ds(pl.multiple_of(bc * HALF + first, LANES), last - first)
        return fq.at[:, bx, strip_of(bz), cols]

    def by_columns(bx, bz, bc, first, last):
        cols = pl.ds(pl.multiple_of(rank(bx, bz) * LANES, LANES), LANES)
        return out_ref.at[pl.ds(pl.multiple_of(bc * HALF + first, PIECE), last - first), cols]

    gg = Ring(fg)
    gq = Gather(by_strips, HALF, alone=True)
    go = Gather(by_columns, HALF, exists=lambda bx, bz: works(bx, bz))

    own = pl.ds(pl.multiple_of(dp * STRIP, PIECE), STRIP)

    mine_a = x * 2 + c
    in_place = mine_a == y
    for n in range(4):
        started = pltpu.make_async_remote_copy(
            src_ref=av.at[n], dst_ref=aq.at[y], send_sem=ssem.at[number()], recv_sem=a_recv.at[y],
            device_id=(xh * 4 + mine_a, dp_of(n // 2, z, n % 2)), device_id_type=MESH,
        )
        there = jnp.logical_not(jnp.logical_and(in_place, y == n))
        pl.when(there)(started.start)
        pending.append((started, there))

    @pl.when(in_place)
    def _():
        aq[y] = av[y]

    gg.share(g)

    m_q1, m_q2, m_q3 = ([number() for _ in range(2)] for _ in range(3))
    send(m_q1[0], qsel.at[:, far, :, :HALF], qr_low.at[:, 1], y_up)
    send(m_q1[1], qsel.at[:, far, :, HALF:], qr_high.at[:, 1], y_down)
    send(m_q3[0], qsel.at[:, above, :, HALF:], qt.at[:, 1, :, HALF:], y_up)
    send(m_q3[1], qsel.at[:, below, :, :HALF], qt.at[:, 2, :, :HALF], y_down)
    gg.begin()

    owners_y = [lax.bitwise_and(owner_ref[layer], 3) for layer in range(2)]

    def one_if(condition):
        return jnp.where(condition, 1, 0)

    arrive(m_q1[0], qr_low.at[:, 1], y_down)
    for layer in range(2):
        qs[0, layer] = qr_low[layer, one_if(owners_y[layer] == below)]
    send(m_q2[0], qs.at[0], qt.at[:, 1, :, :HALF], y_up)
    arrive(m_q1[1], qr_high.at[:, 1], y_up)
    for layer in range(2):
        qs[1, layer] = qr_high[layer, one_if(owners_y[layer] == above)]
    send(m_q2[1], qs.at[1], qt.at[:, 2, :, HALF:], y_down)

    for k in range(1, 4):
        m_a = (y + k) % 4
        pltpu.make_async_remote_copy(
            src_ref=aq.at[m_a], dst_ref=aq.at[m_a], send_sem=ssem.at[0], recv_sem=a_recv.at[m_a],
            device_id=sibling, device_id_type=MESH,
        ).wait_recv()

    @pl.when(jnp.logical_not(in_place))
    def _():
        pltpu.make_async_remote_copy(
            src_ref=aq.at[y], dst_ref=aq.at[y], send_sem=ssem.at[0], recv_sem=a_recv.at[y],
            device_id=sibling, device_id_type=MESH,
        ).wait_recv()

    m_ax = number()
    ac[...] = aq[other_y, 1 - xh]
    send(m_ax, ac, ax.at[1], partner)
    ax[0] = aq[owner_y, xh]

    m_vy = [number() for _ in range(3)]
    for k in range(1, 4):
        to = (y + k) % 4
        send(m_vy[k - 1], vsb.at[to], vy.at[y], (xh * 4 + to, dp))
    gg.step(1)
    arrive(m_ax, ax.at[1], partner)
    fa[y // 2, z, y % 2] = ax[is_far]
    m_a = {}

    def ring_a(way, s, bz):
        ref = fa.at[y // 2, bz, y % 2]
        m_a[way, s] = number()
        send(m_a[way, s], ref, ref, up if way == "u" else down)

    def step_a(s):
        lo, hi = (z + NZ - s) % NZ, (z + s) % NZ
        arrive(m_a["u", s], fa.at[y // 2, lo, y % 2], sibling)
        if s < 4:
            ring_a("u", s + 1, lo)
            arrive(m_a["d", s], fa.at[y // 2, hi, y % 2], sibling)
        if s < 3:
            ring_a("d", s + 1, hi)

    def blocks_a(s):
        lo, hi = (z + NZ - s) % NZ, (z + s) % NZ
        return (lo,) if s in (0, 4) else (lo, hi)

    m_y = {}

    def move_y(name, s, n, target, ref):
        m_y[name, s, n] = number()
        send(m_y[name, s, n], ref, ref, target)

    def cross_y(s):
        for n, bz in enumerate(blocks_a(s)):
            ref = fa.at[y // 2, bz, y % 2]
            move_y("u", s, n, y_up, ref)
            move_y("d", s, n, y_down, ref)

    def relay_y(s):
        for n, bz in enumerate(blocks_a(s)):
            from_below, from_above = fa.at[below // 2, bz, below % 2], fa.at[above // 2, bz, above % 2]
            arrive(m_y["u", s, n], from_below, sibling)
            if n == 0:
                move_y("f", s, n, y_up, from_below)
            arrive(m_y["d", s, n], from_above, sibling)
            if n == 1:
                move_y("f", s, n, y_down, from_above)

    def finish_y(s):
        for n, bz in enumerate(blocks_a(s)):
            arrive(m_y["f", s, n], fa.at[far // 2, bz, far % 2], sibling)

    ring_a("u", 1, z)
    ring_a("d", 1, z)
    cross_y(0)

    arrive(m_q3[0], qt.at[:, 1, :, HALF:], y_down)
    arrive(m_q3[1], qt.at[:, 2, :, :HALF], y_up)
    arrive(m_q2[0], qt.at[:, 1, :, :HALF], y_down)
    arrive(m_q2[1], qt.at[:, 2, :, HALF:], y_up)
    for k in range(1, 4):
        arrive(m_vy[k - 1], vy.at[(y + 4 - k) % 4], partner)

    def came(layer, column_half):
        away = lax.bitwise_and(lax.bitwise_and(owner_ref[layer], 3) + 4 - y, 3)
        by_below = (away >= 2) if column_half == 0 else (away == 3)
        return jnp.where(away == 0, 0, jnp.where(by_below, 1, 2))

    m_qx, m_vx = [number() for _ in range(2)], number()
    for n in range(2):
        half = slice(n * HALF, (n + 1) * HALF)
        qc[n] = qt[1 - xh, came(1 - xh, n), :, half]
        send(m_qx[n], qc.at[n], (qx_low, qx_high)[n].at[1], partner)
    vc[...] = vy[other_y, 1 - xh]
    send(m_vx, vc, vx.at[1], partner)
    for n in range(2):
        half = slice(n * HALF, (n + 1) * HALF)
        (qx_low, qx_high)[n][0] = qt[xh, came(xh, n), :, half]
    vx[0] = vy[owner_y, xh]
    gg.step(2)

    step_a(1)
    cross_y(1)
    gg.step(3)
    relay_y(0)
    step_a(2)
    cross_y(2)
    relay_y(1)
    m_s = [number() for _ in range(3)]
    for n, strip_half in enumerate((qx_low, qx_high)):
        arrive(m_qx[n], strip_half.at[1], partner)
        cols = slice(n * HALF, (n + 1) * HALF)
        fq[c, x, strip_of(z), cols] = strip_half[is_far]
        part = fq.at[c, x, strip_of(z), cols]
        send(m_s[n], part, part, sibling)
    for n in range(2):
        arrive(m_s[n], fq.at[1 - c, x, strip_of(z), n * HALF:(n + 1) * HALF], sibling)
    gq.begin_low()
    gq.begin_high()
    step_a(3)
    cross_y(3)
    gq.swap()
    step_a(4)
    cross_y(4)
    relay_y(2)
    gq.from_x()
    came_over = by_strips(1 - x, z, c, 0, HALF)
    send(m_s[2], came_over, came_over, sibling)
    gg.last()
    relay_y(3)

    arrive(m_s[2], by_strips(1 - x, z, 1 - c, 0, HALF), sibling)

    def flat(value):
        return value.reshape((-1, value.shape[-1]))

    p[x * 2 + c] = jnp.dot(
        flat(fq[:, :, strip_of(z), :]), flat(fg[...]), preferred_element_type=jnp.float32
    ).astype(jnp.bfloat16)
    m_p = [number() for _ in range(3)]
    p_own, p_far = p.at[x * 2 + c], p.at[(1 - x) * 2 + c]
    send(m_p[0], p_own, p_own, across)
    send(m_p[1], p_own, p_own, sibling)
    gq.step(1)
    arrive(m_vx, vx.at[1], partner)
    vf[...] = vx[is_far].astype(jnp.float32)
    for n in range(WIDTH // LANES):
        lg_row = vf[0, n:n + 1, :]
        lgc[n * LANES:(n + 1) * LANES, :] = jnp.transpose(jnp.broadcast_to(lg_row, (LANES, LANES)))
    relay_y(4)
    arrive(m_p[0], p_far, across)
    send(m_p[2], p_far, p_far, sibling)
    gq.step(2)
    for s in range(5):
        finish_y(s)

    arrive(m_p[1], p.at[x * 2 + 1 - c], sibling)
    arrive(m_p[2], p.at[(1 - x) * 2 + 1 - c], sibling)
    eigen = sum(
        jnp.dot(p[n], flat(fa[n // 2, n % 2 * 4:n % 2 * 4 + 4]), preferred_element_type=jnp.float32)
        for n in range(4)
    )
    lg_col = jnp.concatenate([lgc[pl.ds(pl.multiple_of(bx * HALF + (z * 2 + bc) * STRIP, PIECE), STRIP), :]
                              for bc in range(2) for bx in range(2)])
    for n in range(QUARTER // LANES):
        la_row = vf[1, pl.ds((x * 2 + c) * (QUARTER // LANES) + n, 1), :]
        cols = slice(n * LANES, (n + 1) * LANES)
        sc[:, cols] = (eigen[:, cols] / (lg_col * la_row + DAMPING)).astype(jnp.bfloat16)

    for bx in range(2):
        for n in range(2):
            part = lax.dot_general(
                sc[...], flat(fa[bx, n * 4:n * 4 + 4]), (((1,), (1,)), ((), ())), preferred_element_type=jnp.float32
            ).reshape((2, 2, STRIP, QUARTER))
            cols = slice(bx * HALF + n * QUARTER, bx * HALF + (n + 1) * QUARTER)
            bp[:, :, :, cols] = part
            bo[:, :, :, cols] = part.astype(jnp.bfloat16)
    m_b = number()
    send(m_b, bo.at[1 - c], bi, sibling)
    gq.step(3)
    arrive(m_b, bi, sibling)
    done = (bp[c] + bi[...].astype(jnp.float32)).astype(jnp.bfloat16)
    for j in range(WIDTH // LANES):
        bk[j] = done[:, :, j * LANES:(j + 1) * LANES]

    for wx in range(2):
        for wz in range(NZ):
            if (wz + 2 * wx) % 4 == 3:
                continue
            part = bk.at[wx * 6 + wz - (wz + 2 * wx) // 4]
            to_self = jnp.logical_and(x == wx, z == wz)
            others = jnp.logical_not(to_self)
            started = pltpu.make_async_remote_copy(
                src_ref=part, dst_ref=bc.at[x, :, strip_of(z), :], send_sem=ssem.at[number()],
                recv_sem=b_recv.at[x * NZ + z], device_id=dev(xh, y, wx, wz, c), device_id_type=MESH,
            )
            pl.when(others)(started.start)
            pending.append((started, others))

            @pl.when(to_self)
            def _():
                bc[x, :, strip_of(z), :] = part[...]

    gq.last()
    is_worker = works(x, z)
    m_bt = number()

    @pl.when(is_worker)
    def _():
        def take(k, carry):
            n = (x * NZ + z + k) % 16
            block = bc.at[n // NZ, :, strip_of(n % NZ), :]
            pltpu.make_async_remote_copy(
                src_ref=block, dst_ref=block, send_sem=ssem.at[m_bt], recv_sem=b_recv.at[n],
                device_id=sibling, device_id_type=MESH,
            ).wait_recv()
            return carry

        lax.fori_loop(1, 16, take, 0)
        total = flat(bc[0].astype(jnp.float32) + bc[1].astype(jnp.float32))
        for n in range(HALF // LANES):
            cols = slice(n * LANES, (n + 1) * LANES)
            bt[c, :, cols] = jnp.transpose(total[cols, :]).astype(jnp.bfloat16)

    send(m_bt, bt.at[c], bt.at[c], sibling, is_worker)
    arrive(m_bt, bt.at[1 - c], sibling, is_worker)

    mine = pl.ds(pl.multiple_of(rank(x, z) * LANES, LANES), LANES)

    def finish(n):
        @pl.when(is_worker)
        def _():
            rows = pl.ds(pl.multiple_of(c * HALF + n * QUARTER, LANES), QUARTER)
            part = sum(
                jnp.dot(bt[k], flat(fq[k, :, :, rows]), preferred_element_type=jnp.float32) for k in range(2)
            )
            out_ref[rows, mine] = jnp.transpose(part).astype(jnp.bfloat16)

    finish(0)
    go.begin_low()
    finish(1)
    go.begin_high()
    drain()
    go.swap()
    go.step(1)
    early = len(pending)
    go.step(2)
    go.step(3)
    drain(early)
    go.last()
    go.end()
    drain()


def local(gradient_tiles, qa_basis, qg_basis, qa_values, qg_values, layer_owner, block_assign):
    strip = (STRIP, WIDTH)
    bf = jnp.bfloat16
    f32 = jnp.float32
    out = pl.pallas_call(
        kernel,
        out_shape=jax.ShapeDtypeStruct((WIDTH, WIDTH), bf),
        in_specs=[pl.BlockSpec(memory_space=pltpu.HBM)] * 7,
        out_specs=pl.BlockSpec(memory_space=pltpu.VMEM),
        scratch_shapes=[
            pltpu.SMEM((2,), jnp.int32),
            pltpu.SMEM((2, 4), jnp.int32),
            pltpu.VMEM((2, 16, WIDTH), bf),
            pltpu.VMEM((2, WIDTH), bf),
            pltpu.VMEM((4, STRIP, QUARTER), bf),
            pltpu.VMEM((4, 2, STRIP, QUARTER), bf),
            pltpu.VMEM((2, 16) + strip, bf),
            pltpu.VMEM((2, 4) + strip, bf),
            pltpu.VMEM((2, 2, STRIP, HALF), bf),
            pltpu.VMEM((2, 2, STRIP, HALF), bf),
            pltpu.VMEM((2, 2, STRIP, HALF), bf),
            pltpu.VMEM((2, 3) + strip, bf),
            pltpu.VMEM((2, STRIP, HALF), bf),
            pltpu.VMEM((2, STRIP, HALF), bf),
            pltpu.VMEM((2, STRIP, HALF), bf),
            pltpu.VMEM((4, 2, STRIP, QUARTER), bf),
            pltpu.VMEM((STRIP, QUARTER), bf),
            pltpu.VMEM((2, STRIP, QUARTER), bf),
            pltpu.VMEM((4, 2, 2, 16, LANES), f32),
            pltpu.VMEM((4, 2, 2, 16, LANES), bf),
            pltpu.VMEM((4, 2, 2, 16, LANES), bf),
            pltpu.VMEM((2, 2, 16, LANES), bf),
            pltpu.VMEM((2, 16, LANES), bf),
            pltpu.VMEM((2, 16, LANES), f32),
            pltpu.VMEM((2, HALF, QUARTER), bf),
            pltpu.VMEM((2, NZ, 2, STRIP, QUARTER), bf),
            pltpu.VMEM((2, 2, HALF // 2, WIDTH), bf),
            pltpu.VMEM((4, 4 * STRIP, QUARTER), bf),
            pltpu.VMEM((WIDTH, LANES), f32),
            pltpu.VMEM((4 * STRIP, QUARTER), bf),
            pltpu.VMEM((2, 2) + strip, f32),
            pltpu.VMEM((2, 2) + strip, bf),
            pltpu.VMEM((2,) + strip, bf),
            pltpu.VMEM((12, 2, STRIP, LANES), bf),
            pltpu.VMEM((2, 2, HALF // 2, LANES), bf),
            pltpu.VMEM((2, LANES, HALF), bf),
            pltpu.SemaphoreType.DMA((N_SEM,)),
            pltpu.SemaphoreType.DMA((N_SEM,)),
            pltpu.SemaphoreType.DMA((15,)),
            pltpu.SemaphoreType.DMA((4,)),
            pltpu.SemaphoreType.DMA((16,)),
        ],
        compiler_params=pltpu.CompilerParams(
            collective_id=0, has_side_effects=True, vmem_limit_bytes=48 * 1024 * 1024
        ),
        cost_estimate=pl.CostEstimate(flops=4 * 2 * 48 * 1536 * 1536, bytes_accessed=10_000_000, transcendentals=0),
    )(
        *(
            pltpu.with_memory_space_constraint(operand, pltpu.HBM)
            for operand in (
                layer_owner, block_assign, gradient_tiles[0], qa_basis[0], jnp.swapaxes(qg_basis[0], -1, -2),
                qg_values[0], qa_values[0],
            )
        )
    )
    return out[None]


def solution(mesh):
    in_specs = (
        P("grp", "dp", None),
        P("grp", None, "dp", None),
        P("grp", None, None, None, "dp"),
        P("grp", None, None),
        P("grp", None, None, None),
        P(),
        P(),
    )
    out_specs = P("grp", None, None)
    return jax.shard_map(local, mesh=mesh, in_specs=in_specs, out_specs=out_specs, check_vma=False)
```

```python
import functools

import jax
import jax.numpy as jnp
from jax import lax
from jax.experimental import pallas as pl
from jax.experimental.pallas import tpu as pltpu
from jax.sharding import PartitionSpec as P

MESH = pl.DeviceIdType.MESH
DAMPING = 0.1
NZ = 8
STRIP = 48
PIECE = 16
WIDTH = 1536
LANES = 128
N_DP = 32
HALF = WIDTH // 2
QUARTER = WIDTH // 4
TILE = 256
N_SEM = 320


def works(x, z):
    return (z + 2 * x) % 4 != 3


def rank(x, z):
    return x * 6 + z - (z + 2 * x) // 4


def kernel(
    owner_hbm, assign_hbm, g_hbm, a_hbm, q_hbm, lg_hbm, la_hbm, out_ref,
    owner_ref, assign_ref, lgv, lav, g, av, qv, qsel, qr_low, qr_high, qs, qt, qx_low, qx_high, qc, aq, ac, ax, vsel, vsb, vy, vx, vc, vf, fg, fa, fq, p, lgc, sc, bp, bo, bi, bk, bc, bt, acc,
    ssem, rsem, lsem, a_recv, b_recv,
):
    member = lax.axis_index("grp")
    dp = lax.axis_index("dp")
    xh, y = member // 4, member % 4
    x, z, c = dp // 16, (dp // 2) % NZ, dp % 2

    load_g = [
        pltpu.make_async_copy(g_hbm.at[:, n * QUARTER:(n + 1) * QUARTER], g.at[n], lsem.at[7 + n]) for n in range(4)
    ]
    load_a = [
        pltpu.make_async_copy(a_hbm.at[:, :, n * QUARTER:(n + 1) * QUARTER], av.at[n], lsem.at[11 + n])
        for n in range(4)
    ]
    load_q = pltpu.make_async_copy(q_hbm, qv, lsem.at[2])
    loads = [
        pltpu.make_async_copy(src, dst, lsem.at[3 + n])
        for n, (src, dst) in enumerate(
            ((owner_hbm, owner_ref), (assign_hbm, assign_ref), (lg_hbm, lgv), (la_hbm, lav))
        )
    ]
    for load in load_a:
        load.start()
    for load in load_g:
        load.start()
    for load in loads:
        load.start()
    load_q.start()
    core0 = c == 0

    def dp_of(dx, dz, dc):
        return dx * 16 + dz * 2 + dc

    def dev(gx, gy, dx, dz, dc):
        return (gx * 4 + gy, dp_of(dx, dz, dc))

    sibling = dev(xh, y, x, z, 1 - c)
    across = dev(xh, y, 1 - x, z, c)
    up = dev(xh, y, x, (z + 1) % NZ, c)
    down = dev(xh, y, x, (z + NZ - 1) % NZ, c)
    partner = dev(1 - xh, y, x, z, c)

    barrier = pltpu.get_barrier_semaphore()

    near = [up, down, partner]
    near += [
        dev(xh, (y + k // 4) % 4, (x + k // 2) % 2, z, (c + k) % 2) for k in range(1, 16)
    ]
    for target in near:
        pl.semaphore_signal(barrier, inc=1, device_id=target, device_id_type=MESH)

    y_up, y_down = (xh * 4 + (y + 1) % 4, dp), (xh * 4 + (y + 3) % 4, dp)
    far, above, below = (y + 2) % 4, (y + 1) % 4, (y + 3) % 4
    for load in load_a:
        load.wait()
    for load in load_g:
        load.wait()
    for load in loads:
        load.wait()
    owner = owner_ref[xh]
    other = owner_ref[1 - xh]
    is_far = lax.bitwise_xor(lax.shift_right_logical(owner, 2), xh)
    owner_y = lax.bitwise_and(owner, 3)
    other_y = lax.bitwise_and(other, 3)
    load_q.wait()
    for layer in range(2):
        for slot in range(4):
            qsel[layer, slot] = qv[layer, assign_ref[layer, slot]]
    for layer in range(2):
        qr_low[layer, 0] = qsel[layer, above, :, :HALF]
        qr_high[layer, 0] = qsel[layer, below, :, HALF:]
        qt[layer, 0] = qsel[layer, y]
    for layer in range(2):
        la_all = lav[...].astype(jnp.float32)[layer:layer + 1]
        lg_all = lgv[layer].astype(jnp.float32)
        at_row = lax.broadcasted_iota(jnp.int32, lg_all.shape, 0)
        for slot in range(4):
            lg = jnp.sum(jnp.where(at_row == assign_ref[layer, slot], lg_all, 0.0), axis=0, keepdims=True)
            for n in range(WIDTH // LANES):
                cols = slice(n * LANES, (n + 1) * LANES)
                vsel[slot, layer, 0, n:n + 1] = lg[:, cols]
                vsel[slot, layer, 1, n:n + 1] = la_all[:, cols]
    vsb[...] = vsel[...].astype(jnp.bfloat16)
    vy[y] = vsb[y]

    pl.semaphore_wait(barrier, len(near))

    count = [0]
    pending = []

    def number():
        count[0] += 1
        assert count[0] <= N_SEM
        return count[0] - 1

    def copy(m, src, dst, target):
        return pltpu.make_async_remote_copy(
            src_ref=src, dst_ref=dst, send_sem=ssem.at[m], recv_sem=rsem.at[m],
            device_id=target, device_id_type=MESH,
        )

    def send(m, src, dst, target, when=None):
        started = copy(m, src, dst, target)
        pending.append((started, when))
        if when is None:
            started.start()
        else:
            pl.when(when)(started.start)

    def drain(until=None):
        for started, when in pending[:until]:
            if when is None:
                started.wait_send()
            else:
                pl.when(when)(started.wait_send)
        del pending[:until]

    def arrive(m, dst, target, when=None):
        landed = copy(m, dst, dst, target)
        if when is None:
            landed.wait_recv()
        else:
            pl.when(when)(landed.wait_recv)

    class Gather:
        def __init__(self, ref, full, exists=None, alone=False):
            self.ref, self.full, self.cut, self.mid = ref, full, full // 2, 2 * LANES if alone else full // 4
            self.alone = alone
            self.exists = exists or (lambda bx, bz: None)
            self.sib_waits = []
            self.m = {}

        def key(self, *name):
            if name not in self.m:
                self.m[name] = number()
            return self.m[name]

        def to_sibling(self, bx, bz):
            if self.alone:
                return
            m = number()
            ref = self.ref(bx, bz, c, 0, self.full)
            send(m, ref, ref, sibling, self.exists(bx, bz))
            self.sib_waits.append((m, self.ref(bx, bz, 1 - c, 0, self.full), self.exists(bx, bz)))

        def move(self, name, target, bx, bz, first, last):
            ref = self.ref(bx, bz, c, first, last)
            send(self.key(*name), ref, ref, target, self.exists(bx, bz))

        def wait(self, name, bx, bz, first, last, bc=c):
            arrive(self.key(*name), self.ref(bx, bz, bc, first, last), sibling, self.exists(bx, bz))

        def low(self, name, target, bx, bz):
            self.move(name, target, bx, bz, 0, self.cut)

        def high(self, name, target, bx, bz):
            self.move(name, target, bx, bz, self.cut, self.full)

        def wait_low(self, name, bx, bz):
            self.wait(name, bx, bz, 0, self.cut)

        def wait_high(self, name, bx, bz):
            self.wait(name, bx, bz, self.cut, self.full)

        def begin_low(self):
            self.low(("x", 0), across, x, z)
            self.low(("ul", 1), up, x, z)
            self.low(("dl", 1), down, x, z)

        def begin_high(self):
            self.high(("xh", 0), across, x, z)
            self.high(("uh", 1), up, x, z)
            self.high(("dh", 1), down, x, z)
            self.to_sibling(x, z)

        def swap(self):
            self.wait_low(("x", 0), 1 - x, z)
            self.low(("uq", 1), up, 1 - x, z)
            self.low(("dq", 1), down, 1 - x, z)

        def from_x(self):
            self.wait_high(("xh", 0), 1 - x, z)
            self.to_sibling(1 - x, z)

        def step(self, s):
            lo, hi = (z + NZ - s) % NZ, (z + s) % NZ
            self.wait_high(("uh", s), x, lo)
            self.high(("uh", s + 1), up, x, lo)
            self.high(("xu", s), across, x, lo)
            self.wait_high(("dh", s), x, hi)
            if s < 3:
                self.high(("dh", s + 1), down, x, hi)
            self.high(("xd", s), across, x, hi)
            self.wait_low(("ul", s), x, lo)
            if s < 3:
                self.low(("ul", s + 1), up, x, lo)
            self.wait_low(("dl", s), x, hi)
            self.low(("dl", s + 1), down, x, hi)
            self.wait_low(("uq", s), 1 - x, lo)
            if s < 3:
                self.low(("uq", s + 1), up, 1 - x, lo)
            else:
                self.move(("uq", 4), up, 1 - x, lo, 0, self.mid)
            self.wait_low(("dq", s), 1 - x, hi)
            if s < 3:
                self.low(("dq", s + 1), down, 1 - x, hi)
            else:
                self.move(("dq", 4), down, 1 - x, hi, self.mid, self.cut)
            self.to_sibling(x, lo)
            self.to_sibling(x, hi)
            if s == 2 and not self.alone:
                self.from_x()
            if s > 1:
                self.crossed(s - 1)

        def crossed(self, s):
            lo, hi = (z + NZ - s) % NZ, (z + s) % NZ
            self.wait_high(("xu", s), 1 - x, lo)
            self.to_sibling(1 - x, lo)
            self.wait_high(("xd", s), 1 - x, hi)
            self.to_sibling(1 - x, hi)

        def last(self):
            far = (z + 4) % NZ
            self.wait_high(("uh", 4), x, far)
            self.high(("xu", 4), across, x, far)
            self.wait_low(("dl", 4), x, far)
            self.to_sibling(x, far)
            self.crossed(3)
            self.wait(("uq", 4), 1 - x, far, 0, self.mid)
            self.wait(("dq", 4), 1 - x, far, self.mid, self.cut)
            self.wait_high(("xu", 4), 1 - x, far)
            self.to_sibling(1 - x, far)

        def end(self):
            for m, ref, when in self.sib_waits:
                arrive(m, ref, sibling, when)

    def strip_at(bz, bc):
        return pl.ds(pl.multiple_of((bz * 2 + bc) * STRIP, PIECE), STRIP)

    def strip_of(bz):
        return pl.ds(pl.multiple_of(bz * STRIP, PIECE), STRIP)

    def at_z(bz):
        return pl.ds(pl.multiple_of(bz * 2 * STRIP, PIECE), 2 * STRIP)

    class Ring:
        def __init__(self, f):
            self.f = f
            self.m = {}
            self.m4 = [number() for _ in range(3)]

        def share(self, strip):
            self.f[x, strip_at(z, c), :] = strip[x * 2 + c]
            for n, (dx, dc) in enumerate(((1, 0), (1, 1), (0, 1))):
                bx, bc = (x + dx) % 2, (c + dc) % 2
                send(self.m4[n], strip.at[bx * 2 + bc], self.f.at[x, strip_at(z, c), :], dev(xh, y, bx, z, bc))

        def begin(self):
            for n, (dx, dc) in enumerate(((1, 0), (1, 1), (0, 1))):
                bx, bc = (x + dx) % 2, (c + dc) % 2
                arrive(self.m4[n], self.f.at[bx, strip_at(z, bc), :], sibling)
            for n in range(2):
                self.move("u", 1, n, up, z)
                self.move("d", 1, n, down, z)

        def move(self, way, s, n, target, bz):
            ref = self.f.at[n, at_z(bz), :]
            self.m[way, s, n] = number()
            send(self.m[way, s, n], ref, ref, target)

        def wait(self, way, s, n, bz):
            arrive(self.m[way, s, n], self.f.at[n, at_z(bz), :], sibling)

        def step(self, s):
            lo, hi = (z + NZ - s) % NZ, (z + s) % NZ
            for n in range(2):
                self.wait("u", s, n, lo)
                if s < 3 or n == 0:
                    self.move("u", s + 1, n, up, lo)
                self.wait("d", s, n, hi)
                if s < 3 or n == 1:
                    self.move("d", s + 1, n, down, hi)

        def last(self):
            far = (z + 4) % NZ
            self.wait("u", 4, 0, far)
            self.wait("d", 4, 1, far)

    def by_strips(bx, bz, bc, first, last):
        cols = pl.ds(pl.multiple_of(bc * HALF + first, LANES), last - first)
        return fq.at[:, bx, strip_of(bz), cols]

    def by_columns(bx, bz, bc, first, last):
        cols = pl.ds(pl.multiple_of(rank(bx, bz) * LANES, LANES), LANES)
        return out_ref.at[pl.ds(pl.multiple_of(bc * HALF + first, PIECE), last - first), cols]

    gg = Ring(fg)
    gq = Gather(by_strips, HALF, alone=True)
    go = Gather(by_columns, HALF, exists=lambda bx, bz: works(bx, bz))

    own = pl.ds(pl.multiple_of(dp * STRIP, PIECE), STRIP)

    mine_a = x * 2 + c
    in_place = mine_a == y
    for n in range(4):
        started = pltpu.make_async_remote_copy(
            src_ref=av.at[n], dst_ref=aq.at[y], send_sem=ssem.at[number()], recv_sem=a_recv.at[y],
            device_id=(xh * 4 + mine_a, dp_of(n // 2, z, n % 2)), device_id_type=MESH,
        )
        there = jnp.logical_not(jnp.logical_and(in_place, y == n))
        pl.when(there)(started.start)
        pending.append((started, there))

    @pl.when(in_place)
    def _():
        aq[y] = av[y]

    gg.share(g)

    m_q1, m_q2, m_q3 = ([number() for _ in range(2)] for _ in range(3))
    send(m_q1[0], qsel.at[:, far, :, :HALF], qr_low.at[:, 1], y_up)
    send(m_q1[1], qsel.at[:, far, :, HALF:], qr_high.at[:, 1], y_down)
    send(m_q3[0], qsel.at[:, above, :, HALF:], qt.at[:, 1, :, HALF:], y_up)
    send(m_q3[1], qsel.at[:, below, :, :HALF], qt.at[:, 2, :, :HALF], y_down)
    gg.begin()

    owners_y = [lax.bitwise_and(owner_ref[layer], 3) for layer in range(2)]

    def one_if(condition):
        return jnp.where(condition, 1, 0)

    arrive(m_q1[0], qr_low.at[:, 1], y_down)
    for layer in range(2):
        qs[0, layer] = qr_low[layer, one_if(owners_y[layer] == below)]
    send(m_q2[0], qs.at[0], qt.at[:, 1, :, :HALF], y_up)
    arrive(m_q1[1], qr_high.at[:, 1], y_up)
    for layer in range(2):
        qs[1, layer] = qr_high[layer, one_if(owners_y[layer] == above)]
    send(m_q2[1], qs.at[1], qt.at[:, 2, :, HALF:], y_down)

    for k in range(1, 4):
        m_a = (y + k) % 4
        pltpu.make_async_remote_copy(
            src_ref=aq.at[m_a], dst_ref=aq.at[m_a], send_sem=ssem.at[0], recv_sem=a_recv.at[m_a],
            device_id=sibling, device_id_type=MESH,
        ).wait_recv()

    @pl.when(jnp.logical_not(in_place))
    def _():
        pltpu.make_async_remote_copy(
            src_ref=aq.at[y], dst_ref=aq.at[y], send_sem=ssem.at[0], recv_sem=a_recv.at[y],
            device_id=sibling, device_id_type=MESH,
        ).wait_recv()

    m_ax = number()
    ac[...] = aq[other_y, 1 - xh]
    send(m_ax, ac, ax.at[1], partner)
    ax[0] = aq[owner_y, xh]

    m_vy = [number() for _ in range(3)]
    for k in range(1, 4):
        to = (y + k) % 4
        send(m_vy[k - 1], vsb.at[to], vy.at[y], (xh * 4 + to, dp))
    gg.step(1)
    arrive(m_ax, ax.at[1], partner)
    fa[y // 2, z, y % 2] = ax[is_far]
    m_a = {}

    def ring_a(way, s, bz):
        ref = fa.at[y // 2, bz, y % 2]
        m_a[way, s] = number()
        send(m_a[way, s], ref, ref, up if way == "u" else down)

    def step_a(s):
        lo, hi = (z + NZ - s) % NZ, (z + s) % NZ
        arrive(m_a["u", s], fa.at[y // 2, lo, y % 2], sibling)
        if s < 4:
            ring_a("u", s + 1, lo)
            arrive(m_a["d", s], fa.at[y // 2, hi, y % 2], sibling)
        if s < 3:
            ring_a("d", s + 1, hi)

    def blocks_a(s):
        lo, hi = (z + NZ - s) % NZ, (z + s) % NZ
        return (lo,) if s in (0, 4) else (lo, hi)

    m_y = {}

    def move_y(name, s, n, target, ref):
        m_y[name, s, n] = number()
        send(m_y[name, s, n], ref, ref, target)

    def cross_y(s):
        for n, bz in enumerate(blocks_a(s)):
            ref = fa.at[y // 2, bz, y % 2]
            move_y("u", s, n, y_up, ref)
            move_y("d", s, n, y_down, ref)

    def relay_y(s):
        for n, bz in enumerate(blocks_a(s)):
            from_below, from_above = fa.at[below // 2, bz, below % 2], fa.at[above // 2, bz, above % 2]
            arrive(m_y["u", s, n], from_below, sibling)
            if n == 0:
                move_y("f", s, n, y_up, from_below)
            arrive(m_y["d", s, n], from_above, sibling)
            if n == 1:
                move_y("f", s, n, y_down, from_above)

    def finish_y(s):
        for n, bz in enumerate(blocks_a(s)):
            arrive(m_y["f", s, n], fa.at[far // 2, bz, far % 2], sibling)

    ring_a("u", 1, z)
    ring_a("d", 1, z)
    cross_y(0)

    arrive(m_q3[0], qt.at[:, 1, :, HALF:], y_down)
    arrive(m_q3[1], qt.at[:, 2, :, :HALF], y_up)
    arrive(m_q2[0], qt.at[:, 1, :, :HALF], y_down)
    arrive(m_q2[1], qt.at[:, 2, :, HALF:], y_up)
    for k in range(1, 4):
        arrive(m_vy[k - 1], vy.at[(y + 4 - k) % 4], partner)

    def came(layer, column_half):
        away = lax.bitwise_and(lax.bitwise_and(owner_ref[layer], 3) + 4 - y, 3)
        by_below = (away >= 2) if column_half == 0 else (away == 3)
        return jnp.where(away == 0, 0, jnp.where(by_below, 1, 2))

    m_qx, m_vx = [number() for _ in range(2)], number()
    for n in range(2):
        half = slice(n * HALF, (n + 1) * HALF)
        qc[n] = qt[1 - xh, came(1 - xh, n), :, half]
        send(m_qx[n], qc.at[n], (qx_low, qx_high)[n].at[1], partner)
    vc[...] = vy[other_y, 1 - xh]
    send(m_vx, vc, vx.at[1], partner)
    for n in range(2):
        half = slice(n * HALF, (n + 1) * HALF)
        (qx_low, qx_high)[n][0] = qt[xh, came(xh, n), :, half]
    vx[0] = vy[owner_y, xh]
    gg.step(2)

    step_a(1)
    cross_y(1)
    gg.step(3)
    relay_y(0)
    step_a(2)
    cross_y(2)
    relay_y(1)
    m_s = [number() for _ in range(3)]
    for n, strip_half in enumerate((qx_low, qx_high)):
        arrive(m_qx[n], strip_half.at[1], partner)
        cols = slice(n * HALF, (n + 1) * HALF)
        fq[c, x, strip_of(z), cols] = strip_half[is_far]
        part = fq.at[c, x, strip_of(z), cols]
        send(m_s[n], part, part, sibling)
    for n in range(2):
        arrive(m_s[n], fq.at[1 - c, x, strip_of(z), n * HALF:(n + 1) * HALF], sibling)
    gq.begin_low()
    gq.begin_high()
    step_a(3)
    cross_y(3)
    gq.swap()
    step_a(4)
    cross_y(4)
    relay_y(2)
    gq.from_x()
    came_over = by_strips(1 - x, z, c, 0, HALF)
    send(m_s[2], came_over, came_over, sibling)
    gg.last()
    relay_y(3)

    arrive(m_s[2], by_strips(1 - x, z, 1 - c, 0, HALF), sibling)

    def flat(value):
        return value.reshape((-1, value.shape[-1]))

    p[x * 2 + c] = jnp.dot(
        flat(fq[:, :, strip_of(z), :]), flat(fg[...]), preferred_element_type=jnp.float32
    ).astype(jnp.bfloat16)
    m_p = [number() for _ in range(3)]
    p_own, p_far = p.at[x * 2 + c], p.at[(1 - x) * 2 + c]
    send(m_p[0], p_own, p_own, across)
    send(m_p[1], p_own, p_own, sibling)
    gq.step(1)
    arrive(m_vx, vx.at[1], partner)
    vf[...] = vx[is_far].astype(jnp.float32)
    for n in range(WIDTH // LANES):
        lg_row = vf[0, n:n + 1, :]
        lgc[n * LANES:(n + 1) * LANES, :] = jnp.transpose(jnp.broadcast_to(lg_row, (LANES, LANES)))
    relay_y(4)
    arrive(m_p[0], p_far, across)
    send(m_p[2], p_far, p_far, sibling)
    gq.step(2)
    for s in range(5):
        finish_y(s)

    arrive(m_p[1], p.at[x * 2 + 1 - c], sibling)
    arrive(m_p[2], p.at[(1 - x) * 2 + 1 - c], sibling)
    eigen = sum(
        jnp.dot(p[n], flat(fa[n // 2, n % 2 * 4:n % 2 * 4 + 4]), preferred_element_type=jnp.float32)
        for n in range(4)
    )
    lg_col = jnp.concatenate([lgc[pl.ds(pl.multiple_of(bx * HALF + (z * 2 + bc) * STRIP, PIECE), STRIP), :]
                              for bc in range(2) for bx in range(2)])
    for n in range(QUARTER // LANES):
        la_row = vf[1, pl.ds((x * 2 + c) * (QUARTER // LANES) + n, 1), :]
        cols = slice(n * LANES, (n + 1) * LANES)
        sc[:, cols] = (eigen[:, cols] / (lg_col * la_row + DAMPING)).astype(jnp.bfloat16)

    for bx in range(2):
        for n in range(2):
            part = lax.dot_general(
                sc[...], flat(fa[bx, n * 4:n * 4 + 4]), (((1,), (1,)), ((), ())), preferred_element_type=jnp.float32
            ).reshape((2, 2, STRIP, QUARTER))
            cols = slice(bx * HALF + n * QUARTER, bx * HALF + (n + 1) * QUARTER)
            bp[:, :, :, cols] = part
            bo[:, :, :, cols] = part.astype(jnp.bfloat16)
    m_b = number()
    send(m_b, bo.at[1 - c], bi, sibling)
    gq.step(3)
    arrive(m_b, bi, sibling)
    done = (bp[c] + bi[...].astype(jnp.float32)).astype(jnp.bfloat16)
    for j in range(WIDTH // LANES):
        bk[j] = done[:, :, j * LANES:(j + 1) * LANES]

    for wx in range(2):
        for wz in range(NZ):
            if (wz + 2 * wx) % 4 == 3:
                continue
            part = bk.at[wx * 6 + wz - (wz + 2 * wx) // 4]
            to_self = jnp.logical_and(x == wx, z == wz)
            others = jnp.logical_not(to_self)
            started = pltpu.make_async_remote_copy(
                src_ref=part, dst_ref=bc.at[x, :, strip_of(z), :], send_sem=ssem.at[number()],
                recv_sem=b_recv.at[x * NZ + z], device_id=dev(xh, y, wx, wz, c), device_id_type=MESH,
            )
            pl.when(others)(started.start)
            pending.append((started, others))

            @pl.when(to_self)
            def _():
                bc[x, :, strip_of(z), :] = part[...]

    gq.last()
    is_worker = works(x, z)
    m_bt = number()

    @pl.when(is_worker)
    def _():
        def take(k, carry):
            n = (x * NZ + z + k) % 16
            block = bc.at[n // NZ, :, strip_of(n % NZ), :]
            pltpu.make_async_remote_copy(
                src_ref=block, dst_ref=block, send_sem=ssem.at[m_bt], recv_sem=b_recv.at[n],
                device_id=sibling, device_id_type=MESH,
            ).wait_recv()
            return carry

        lax.fori_loop(1, 16, take, 0)
        total = flat(bc[0].astype(jnp.float32) + bc[1].astype(jnp.float32))
        for n in range(HALF // LANES):
            cols = slice(n * LANES, (n + 1) * LANES)
            bt[c, :, cols] = jnp.transpose(total[cols, :]).astype(jnp.bfloat16)

    send(m_bt, bt.at[c], bt.at[c], sibling, is_worker)

    def rows_at(n):
        return pl.ds(pl.multiple_of(c * HALF + n * QUARTER, LANES), QUARTER)

    @pl.when(is_worker)
    def _():
        for n in range(2):
            acc[n] = jnp.dot(bt[c], flat(fq[c, :, :, rows_at(n)]), preferred_element_type=jnp.float32)

    arrive(m_bt, bt.at[1 - c], sibling, is_worker)

    mine = pl.ds(pl.multiple_of(rank(x, z) * LANES, LANES), LANES)

    def finish(n):
        @pl.when(is_worker)
        def _():
            rows = rows_at(n)
            part = acc[n] + jnp.dot(bt[1 - c], flat(fq[1 - c, :, :, rows]), preferred_element_type=jnp.float32)
            out_ref[rows, mine] = jnp.transpose(part).astype(jnp.bfloat16)

    older = len(pending)
    finish(0)
    go.begin_low()
    finish(1)
    go.begin_high()
    drain(older)
    go.swap()
    go.step(1)
    early = len(pending)
    go.step(2)
    go.step(3)
    drain(early)
    go.last()
    go.end()
    drain()


def local(gradient_tiles, qa_basis, qg_basis, qa_values, qg_values, layer_owner, block_assign):
    strip = (STRIP, WIDTH)
    bf = jnp.bfloat16
    f32 = jnp.float32
    out = pl.pallas_call(
        kernel,
        out_shape=jax.ShapeDtypeStruct((WIDTH, WIDTH), bf),
        in_specs=[pl.BlockSpec(memory_space=pltpu.HBM)] * 7,
        out_specs=pl.BlockSpec(memory_space=pltpu.VMEM),
        scratch_shapes=[
            pltpu.SMEM((2,), jnp.int32),
            pltpu.SMEM((2, 4), jnp.int32),
            pltpu.VMEM((2, 16, WIDTH), bf),
            pltpu.VMEM((2, WIDTH), bf),
            pltpu.VMEM((4, STRIP, QUARTER), bf),
            pltpu.VMEM((4, 2, STRIP, QUARTER), bf),
            pltpu.VMEM((2, 16) + strip, bf),
            pltpu.VMEM((2, 4) + strip, bf),
            pltpu.VMEM((2, 2, STRIP, HALF), bf),
            pltpu.VMEM((2, 2, STRIP, HALF), bf),
            pltpu.VMEM((2, 2, STRIP, HALF), bf),
            pltpu.VMEM((2, 3) + strip, bf),
            pltpu.VMEM((2, STRIP, HALF), bf),
            pltpu.VMEM((2, STRIP, HALF), bf),
            pltpu.VMEM((2, STRIP, HALF), bf),
            pltpu.VMEM((4, 2, STRIP, QUARTER), bf),
            pltpu.VMEM((STRIP, QUARTER), bf),
            pltpu.VMEM((2, STRIP, QUARTER), bf),
            pltpu.VMEM((4, 2, 2, 16, LANES), f32),
            pltpu.VMEM((4, 2, 2, 16, LANES), bf),
            pltpu.VMEM((4, 2, 2, 16, LANES), bf),
            pltpu.VMEM((2, 2, 16, LANES), bf),
            pltpu.VMEM((2, 16, LANES), bf),
            pltpu.VMEM((2, 16, LANES), f32),
            pltpu.VMEM((2, HALF, QUARTER), bf),
            pltpu.VMEM((2, NZ, 2, STRIP, QUARTER), bf),
            pltpu.VMEM((2, 2, HALF // 2, WIDTH), bf),
            pltpu.VMEM((4, 4 * STRIP, QUARTER), bf),
            pltpu.VMEM((WIDTH, LANES), f32),
            pltpu.VMEM((4 * STRIP, QUARTER), bf),
            pltpu.VMEM((2, 2) + strip, f32),
            pltpu.VMEM((2, 2) + strip, bf),
            pltpu.VMEM((2,) + strip, bf),
            pltpu.VMEM((12, 2, STRIP, LANES), bf),
            pltpu.VMEM((2, 2, HALF // 2, LANES), bf),
            pltpu.VMEM((2, LANES, HALF), bf),
            pltpu.VMEM((2, LANES, QUARTER), f32),
            pltpu.SemaphoreType.DMA((N_SEM,)),
            pltpu.SemaphoreType.DMA((N_SEM,)),
            pltpu.SemaphoreType.DMA((15,)),
            pltpu.SemaphoreType.DMA((4,)),
            pltpu.SemaphoreType.DMA((16,)),
        ],
        compiler_params=pltpu.CompilerParams(
            collective_id=0, has_side_effects=True, vmem_limit_bytes=48 * 1024 * 1024
        ),
        cost_estimate=pl.CostEstimate(flops=4 * 2 * 48 * 1536 * 1536, bytes_accessed=10_000_000, transcendentals=0),
    )(
        *(
            pltpu.with_memory_space_constraint(operand, pltpu.HBM)
            for operand in (
                layer_owner, block_assign, gradient_tiles[0], qa_basis[0], jnp.swapaxes(qg_basis[0], -1, -2),
                qg_values[0], qa_values[0],
            )
        )
    )
    return out[None]


def solution(mesh):
    in_specs = (
        P("grp", "dp", None),
        P("grp", None, "dp", None),
        P("grp", None, None, None, "dp"),
        P("grp", None, None),
        P("grp", None, None, None),
        P(),
        P(),
    )
    out_specs = P("grp", None, None)
    return jax.shard_map(local, mesh=mesh, in_specs=in_specs, out_specs=out_specs, check_vma=False)
```

```python
import functools

import jax
import jax.numpy as jnp
from jax import lax
from jax.experimental import pallas as pl
from jax.experimental.pallas import tpu as pltpu
from jax.sharding import PartitionSpec as P

MESH = pl.DeviceIdType.MESH
DAMPING = 0.1
NZ = 8
STRIP = 48
PIECE = 16
WIDTH = 1536
LANES = 128
N_DP = 32
HALF = WIDTH // 2
QUARTER = WIDTH // 4
TILE = 256
N_SEM = 320


def works(x, z):
    return (z + 2 * x) % 4 != 3


def rank(x, z):
    return x * 6 + z - (z + 2 * x) // 4


def kernel(
    owner_hbm, assign_hbm, g_hbm, a_hbm, q_hbm, lg_hbm, la_hbm, out_ref,
    owner_ref, assign_ref, lgv, lav, g, av, qv, qsel, qr_low, qr_high, qs, qt, qx_low, qx_high, qc, aq, ac, ax, vsel, vsb, vy, vx, vc, vf, fg, fa, fq, p, lgc, sc, bp, bo, bi, bk, bc, bt,
    ssem, rsem, lsem, a_recv, b_recv,
):
    member = lax.axis_index("grp")
    dp = lax.axis_index("dp")
    xh, y = member // 4, member % 4
    x, z, c = dp // 16, (dp // 2) % NZ, dp % 2

    load_g = [
        pltpu.make_async_copy(g_hbm.at[:, n * QUARTER:(n + 1) * QUARTER], g.at[n], lsem.at[7 + n]) for n in range(4)
    ]
    load_a = [
        pltpu.make_async_copy(a_hbm.at[:, :, n * QUARTER:(n + 1) * QUARTER], av.at[n], lsem.at[11 + n])
        for n in range(4)
    ]
    load_q = pltpu.make_async_copy(q_hbm, qv, lsem.at[2])
    loads = [
        pltpu.make_async_copy(src, dst, lsem.at[3 + n])
        for n, (src, dst) in enumerate(
            ((owner_hbm, owner_ref), (assign_hbm, assign_ref), (lg_hbm, lgv), (la_hbm, lav))
        )
    ]
    for load in load_a:
        load.start()
    for load in load_g:
        load.start()
    for load in loads:
        load.start()
    load_q.start()
    core0 = c == 0

    def dp_of(dx, dz, dc):
        return dx * 16 + dz * 2 + dc

    def dev(gx, gy, dx, dz, dc):
        return (gx * 4 + gy, dp_of(dx, dz, dc))

    sibling = dev(xh, y, x, z, 1 - c)
    across = dev(xh, y, 1 - x, z, c)
    up = dev(xh, y, x, (z + 1) % NZ, c)
    down = dev(xh, y, x, (z + NZ - 1) % NZ, c)
    partner = dev(1 - xh, y, x, z, c)

    barrier = pltpu.get_barrier_semaphore()

    near = [up, down, partner]
    near += [
        dev(xh, (y + k // 4) % 4, (x + k // 2) % 2, z, (c + k) % 2) for k in range(1, 16)
    ]
    for target in near:
        pl.semaphore_signal(barrier, inc=1, device_id=target, device_id_type=MESH)

    y_up, y_down = (xh * 4 + (y + 1) % 4, dp), (xh * 4 + (y + 3) % 4, dp)
    far, above, below = (y + 2) % 4, (y + 1) % 4, (y + 3) % 4
    for load in load_a:
        load.wait()
    for load in load_g:
        load.wait()
    for load in loads:
        load.wait()
    owner = owner_ref[xh]
    other = owner_ref[1 - xh]
    is_far = lax.bitwise_xor(lax.shift_right_logical(owner, 2), xh)
    owner_y = lax.bitwise_and(owner, 3)
    other_y = lax.bitwise_and(other, 3)
    load_q.wait()
    for layer in range(2):
        for slot in range(4):
            qsel[layer, slot] = qv[layer, assign_ref[layer, slot]]
    for layer in range(2):
        qr_low[layer, 0] = qsel[layer, above, :, :HALF]
        qr_high[layer, 0] = qsel[layer, below, :, HALF:]
        qt[layer, 0] = qsel[layer, y]
    for layer in range(2):
        la_all = lav[...].astype(jnp.float32)[layer:layer + 1]
        lg_all = lgv[layer].astype(jnp.float32)
        at_row = lax.broadcasted_iota(jnp.int32, lg_all.shape, 0)
        for slot in range(4):
            lg = jnp.sum(jnp.where(at_row == assign_ref[layer, slot], lg_all, 0.0), axis=0, keepdims=True)
            for n in range(WIDTH // LANES):
                cols = slice(n * LANES, (n + 1) * LANES)
                vsel[slot, layer, 0, n:n + 1] = lg[:, cols]
                vsel[slot, layer, 1, n:n + 1] = la_all[:, cols]
    vsb[...] = vsel[...].astype(jnp.bfloat16)
    vy[y] = vsb[y]

    pl.semaphore_wait(barrier, len(near))

    count = [0]
    pending = []

    def number():
        count[0] += 1
        assert count[0] <= N_SEM
        return count[0] - 1

    def copy(m, src, dst, target):
        return pltpu.make_async_remote_copy(
            src_ref=src, dst_ref=dst, send_sem=ssem.at[m], recv_sem=rsem.at[m],
            device_id=target, device_id_type=MESH,
        )

    def send(m, src, dst, target, when=None):
        started = copy(m, src, dst, target)
        pending.append((started, when))
        if when is None:
            started.start()
        else:
            pl.when(when)(started.start)

    def drain(until=None):
        for started, when in pending[:until]:
            if when is None:
                started.wait_send()
            else:
                pl.when(when)(started.wait_send)
        del pending[:until]

    def arrive(m, dst, target, when=None):
        landed = copy(m, dst, dst, target)
        if when is None:
            landed.wait_recv()
        else:
            pl.when(when)(landed.wait_recv)

    class Gather:
        def __init__(self, ref, full, exists=None, alone=False):
            self.ref, self.full, self.cut, self.mid = ref, full, full // 2, 2 * LANES if alone else full // 4
            self.alone = alone
            self.exists = exists or (lambda bx, bz: None)
            self.sib_waits = []
            self.m = {}

        def key(self, *name):
            if name not in self.m:
                self.m[name] = number()
            return self.m[name]

        def to_sibling(self, bx, bz):
            if self.alone:
                return
            m = number()
            ref = self.ref(bx, bz, c, 0, self.full)
            send(m, ref, ref, sibling, self.exists(bx, bz))
            self.sib_waits.append((m, self.ref(bx, bz, 1 - c, 0, self.full), self.exists(bx, bz)))

        def move(self, name, target, bx, bz, first, last):
            ref = self.ref(bx, bz, c, first, last)
            send(self.key(*name), ref, ref, target, self.exists(bx, bz))

        def wait(self, name, bx, bz, first, last, bc=c):
            arrive(self.key(*name), self.ref(bx, bz, bc, first, last), sibling, self.exists(bx, bz))

        def low(self, name, target, bx, bz):
            self.move(name, target, bx, bz, 0, self.cut)

        def high(self, name, target, bx, bz):
            self.move(name, target, bx, bz, self.cut, self.full)

        def wait_low(self, name, bx, bz):
            self.wait(name, bx, bz, 0, self.cut)

        def wait_high(self, name, bx, bz):
            self.wait(name, bx, bz, self.cut, self.full)

        def begin_low(self):
            self.low(("x", 0), across, x, z)
            self.low(("ul", 1), up, x, z)
            self.low(("dl", 1), down, x, z)

        def begin_high(self):
            self.high(("xh", 0), across, x, z)
            self.high(("uh", 1), up, x, z)
            self.high(("dh", 1), down, x, z)
            self.to_sibling(x, z)

        def swap(self):
            self.wait_low(("x", 0), 1 - x, z)
            self.low(("uq", 1), up, 1 - x, z)
            self.low(("dq", 1), down, 1 - x, z)

        def from_x(self):
            self.wait_high(("xh", 0), 1 - x, z)
            self.to_sibling(1 - x, z)

        def step(self, s):
            lo, hi = (z + NZ - s) % NZ, (z + s) % NZ
            self.wait_high(("uh", s), x, lo)
            self.high(("uh", s + 1), up, x, lo)
            self.high(("xu", s), across, x, lo)
            self.wait_high(("dh", s), x, hi)
            if s < 3:
                self.high(("dh", s + 1), down, x, hi)
            self.high(("xd", s), across, x, hi)
            self.wait_low(("ul", s), x, lo)
            if s < 3:
                self.low(("ul", s + 1), up, x, lo)
            self.wait_low(("dl", s), x, hi)
            self.low(("dl", s + 1), down, x, hi)
            self.wait_low(("uq", s), 1 - x, lo)
            if s < 3:
                self.low(("uq", s + 1), up, 1 - x, lo)
            else:
                self.move(("uq", 4), up, 1 - x, lo, 0, self.mid)
            self.wait_low(("dq", s), 1 - x, hi)
            if s < 3:
                self.low(("dq", s + 1), down, 1 - x, hi)
            else:
                self.move(("dq", 4), down, 1 - x, hi, self.mid, self.cut)
            self.to_sibling(x, lo)
            self.to_sibling(x, hi)
            if s == 2 and not self.alone:
                self.from_x()
            if s > 1:
                self.crossed(s - 1)

        def crossed(self, s):
            lo, hi = (z + NZ - s) % NZ, (z + s) % NZ
            self.wait_high(("xu", s), 1 - x, lo)
            self.to_sibling(1 - x, lo)
            self.wait_high(("xd", s), 1 - x, hi)
            self.to_sibling(1 - x, hi)

        def last(self):
            far = (z + 4) % NZ
            self.wait_high(("uh", 4), x, far)
            self.high(("xu", 4), across, x, far)
            self.wait_low(("dl", 4), x, far)
            self.to_sibling(x, far)
            self.crossed(3)
            self.wait(("uq", 4), 1 - x, far, 0, self.mid)
            self.wait(("dq", 4), 1 - x, far, self.mid, self.cut)
            self.wait_high(("xu", 4), 1 - x, far)
            self.to_sibling(1 - x, far)

        def end(self):
            for m, ref, when in self.sib_waits:
                arrive(m, ref, sibling, when)

    def strip_at(bz, bc):
        return pl.ds(pl.multiple_of((bz * 2 + bc) * STRIP, PIECE), STRIP)

    def strip_of(bz):
        return pl.ds(pl.multiple_of(bz * STRIP, PIECE), STRIP)

    def at_z(bz):
        return pl.ds(pl.multiple_of(bz * 2 * STRIP, PIECE), 2 * STRIP)

    class Ring:
        def __init__(self, f):
            self.f = f
            self.m = {}
            self.m4 = [number() for _ in range(3)]

        def share(self, strip):
            self.f[x, strip_at(z, c), :] = strip[x * 2 + c]
            for n, (dx, dc) in enumerate(((1, 0), (1, 1), (0, 1))):
                bx, bc = (x + dx) % 2, (c + dc) % 2
                send(self.m4[n], strip.at[bx * 2 + bc], self.f.at[x, strip_at(z, c), :], dev(xh, y, bx, z, bc))

        def begin(self):
            for n, (dx, dc) in enumerate(((1, 0), (1, 1), (0, 1))):
                bx, bc = (x + dx) % 2, (c + dc) % 2
                arrive(self.m4[n], self.f.at[bx, strip_at(z, bc), :], sibling)
            for n in range(2):
                self.move("u", 1, n, up, z)
                self.move("d", 1, n, down, z)

        def move(self, way, s, n, target, bz):
            ref = self.f.at[n, at_z(bz), :]
            self.m[way, s, n] = number()
            send(self.m[way, s, n], ref, ref, target)

        def wait(self, way, s, n, bz):
            arrive(self.m[way, s, n], self.f.at[n, at_z(bz), :], sibling)

        def step(self, s):
            lo, hi = (z + NZ - s) % NZ, (z + s) % NZ
            for n in range(2):
                self.wait("u", s, n, lo)
                if s < 3 or n == 0:
                    self.move("u", s + 1, n, up, lo)
                self.wait("d", s, n, hi)
                if s < 3 or n == 1:
                    self.move("d", s + 1, n, down, hi)

        def last(self):
            far = (z + 4) % NZ
            self.wait("u", 4, 0, far)
            self.wait("d", 4, 1, far)

    def by_strips(bx, bz, bc, first, last):
        cols = pl.ds(pl.multiple_of(bc * HALF + first, LANES), last - first)
        return fq.at[:, bx, strip_of(bz), cols]

    def by_columns(bx, bz, bc, first, last):
        cols = pl.ds(pl.multiple_of(rank(bx, bz) * LANES, LANES), LANES)
        return out_ref.at[pl.ds(pl.multiple_of(bc * HALF + first, PIECE), last - first), cols]

    gg = Ring(fg)
    gq = Gather(by_strips, HALF, alone=True)
    go = Gather(by_columns, HALF, exists=lambda bx, bz: works(bx, bz))

    own = pl.ds(pl.multiple_of(dp * STRIP, PIECE), STRIP)

    mine_a = x * 2 + c
    in_place = mine_a == y
    for n in range(4):
        started = pltpu.make_async_remote_copy(
            src_ref=av.at[n], dst_ref=aq.at[y], send_sem=ssem.at[number()], recv_sem=a_recv.at[y],
            device_id=(xh * 4 + mine_a, dp_of(n // 2, z, n % 2)), device_id_type=MESH,
        )
        there = jnp.logical_not(jnp.logical_and(in_place, y == n))
        pl.when(there)(started.start)
        pending.append((started, there))

    @pl.when(in_place)
    def _():
        aq[y] = av[y]

    gg.share(g)

    m_q1, m_q2, m_q3 = ([number() for _ in range(2)] for _ in range(3))
    send(m_q1[0], qsel.at[:, far, :, :HALF], qr_low.at[:, 1], y_up)
    send(m_q1[1], qsel.at[:, far, :, HALF:], qr_high.at[:, 1], y_down)
    send(m_q3[0], qsel.at[:, above, :, HALF:], qt.at[:, 1, :, HALF:], y_up)
    send(m_q3[1], qsel.at[:, below, :, :HALF], qt.at[:, 2, :, :HALF], y_down)
    gg.begin()

    owners_y = [lax.bitwise_and(owner_ref[layer], 3) for layer in range(2)]

    def one_if(condition):
        return jnp.where(condition, 1, 0)

    arrive(m_q1[0], qr_low.at[:, 1], y_down)
    for layer in range(2):
        qs[0, layer] = qr_low[layer, one_if(owners_y[layer] == below)]
    send(m_q2[0], qs.at[0], qt.at[:, 1, :, :HALF], y_up)
    arrive(m_q1[1], qr_high.at[:, 1], y_up)
    for layer in range(2):
        qs[1, layer] = qr_high[layer, one_if(owners_y[layer] == above)]
    send(m_q2[1], qs.at[1], qt.at[:, 2, :, HALF:], y_down)

    for k in range(1, 4):
        m_a = (y + k) % 4
        pltpu.make_async_remote_copy(
            src_ref=aq.at[m_a], dst_ref=aq.at[m_a], send_sem=ssem.at[0], recv_sem=a_recv.at[m_a],
            device_id=sibling, device_id_type=MESH,
        ).wait_recv()

    @pl.when(jnp.logical_not(in_place))
    def _():
        pltpu.make_async_remote_copy(
            src_ref=aq.at[y], dst_ref=aq.at[y], send_sem=ssem.at[0], recv_sem=a_recv.at[y],
            device_id=sibling, device_id_type=MESH,
        ).wait_recv()

    m_ax = number()
    ac[...] = aq[other_y, 1 - xh]
    send(m_ax, ac, ax.at[1], partner)
    ax[0] = aq[owner_y, xh]

    m_vy = [number() for _ in range(3)]
    for k in range(1, 4):
        to = (y + k) % 4
        send(m_vy[k - 1], vsb.at[to], vy.at[y], (xh * 4 + to, dp))
    gg.step(1)
    arrive(m_ax, ax.at[1], partner)
    fa[y // 2, z, y % 2] = ax[is_far]
    m_a = {}

    def ring_a(way, s, bz):
        ref = fa.at[y // 2, bz, y % 2]
        m_a[way, s] = number()
        send(m_a[way, s], ref, ref, up if way == "u" else down)

    def step_a(s):
        lo, hi = (z + NZ - s) % NZ, (z + s) % NZ
        arrive(m_a["u", s], fa.at[y // 2, lo, y % 2], sibling)
        if s < 4:
            ring_a("u", s + 1, lo)
            arrive(m_a["d", s], fa.at[y // 2, hi, y % 2], sibling)
        if s < 3:
            ring_a("d", s + 1, hi)

    def blocks_a(s):
        lo, hi = (z + NZ - s) % NZ, (z + s) % NZ
        return (lo,) if s in (0, 4) else (lo, hi)

    m_y = {}

    def move_y(name, s, n, target, ref):
        m_y[name, s, n] = number()
        send(m_y[name, s, n], ref, ref, target)

    def cross_y(s):
        for n, bz in enumerate(blocks_a(s)):
            ref = fa.at[y // 2, bz, y % 2]
            move_y("u", s, n, y_up, ref)
            move_y("d", s, n, y_down, ref)

    def relay_y(s):
        for n, bz in enumerate(blocks_a(s)):
            from_below, from_above = fa.at[below // 2, bz, below % 2], fa.at[above // 2, bz, above % 2]
            arrive(m_y["u", s, n], from_below, sibling)
            if n == 0:
                move_y("f", s, n, y_up, from_below)
            arrive(m_y["d", s, n], from_above, sibling)
            if n == 1:
                move_y("f", s, n, y_down, from_above)

    def finish_y(s):
        for n, bz in enumerate(blocks_a(s)):
            arrive(m_y["f", s, n], fa.at[far // 2, bz, far % 2], sibling)

    ring_a("u", 1, z)
    ring_a("d", 1, z)
    cross_y(0)

    arrive(m_q3[0], qt.at[:, 1, :, HALF:], y_down)
    arrive(m_q3[1], qt.at[:, 2, :, :HALF], y_up)
    arrive(m_q2[0], qt.at[:, 1, :, :HALF], y_down)
    arrive(m_q2[1], qt.at[:, 2, :, HALF:], y_up)
    for k in range(1, 4):
        arrive(m_vy[k - 1], vy.at[(y + 4 - k) % 4], partner)

    def came(layer, column_half):
        away = lax.bitwise_and(lax.bitwise_and(owner_ref[layer], 3) + 4 - y, 3)
        by_below = (away >= 2) if column_half == 0 else (away == 3)
        return jnp.where(away == 0, 0, jnp.where(by_below, 1, 2))

    m_qx, m_vx = [number() for _ in range(2)], number()
    for n in range(2):
        half = slice(n * HALF, (n + 1) * HALF)
        qc[n] = qt[1 - xh, came(1 - xh, n), :, half]
        send(m_qx[n], qc.at[n], (qx_low, qx_high)[n].at[1], partner)
    vc[...] = vy[other_y, 1 - xh]
    send(m_vx, vc, vx.at[1], partner)
    for n in range(2):
        half = slice(n * HALF, (n + 1) * HALF)
        (qx_low, qx_high)[n][0] = qt[xh, came(xh, n), :, half]
    vx[0] = vy[owner_y, xh]
    gg.step(2)

    step_a(1)
    cross_y(1)
    gg.step(3)
    relay_y(0)
    step_a(2)
    cross_y(2)
    relay_y(1)
    m_s = [number() for _ in range(3)]
    for n, strip_half in enumerate((qx_low, qx_high)):
        arrive(m_qx[n], strip_half.at[1], partner)
        cols = slice(n * HALF, (n + 1) * HALF)
        fq[c, x, strip_of(z), cols] = strip_half[is_far]
        part = fq.at[c, x, strip_of(z), cols]
        send(m_s[n], part, part, sibling)
    for n in range(2):
        arrive(m_s[n], fq.at[1 - c, x, strip_of(z), n * HALF:(n + 1) * HALF], sibling)
    gq.begin_low()
    gq.begin_high()
    step_a(3)
    cross_y(3)
    gq.swap()
    step_a(4)
    cross_y(4)
    relay_y(2)
    gq.from_x()
    came_over = by_strips(1 - x, z, c, 0, HALF)
    send(m_s[2], came_over, came_over, sibling)
    gg.last()
    relay_y(3)

    arrive(m_s[2], by_strips(1 - x, z, 1 - c, 0, HALF), sibling)

    def flat(value):
        return value.reshape((-1, value.shape[-1]))

    p[x * 2 + c] = jnp.dot(
        flat(fq[:, :, strip_of(z), :]), flat(fg[...]), preferred_element_type=jnp.float32
    ).astype(jnp.bfloat16)
    m_p = [number() for _ in range(3)]
    p_own, p_far = p.at[x * 2 + c], p.at[(1 - x) * 2 + c]
    send(m_p[0], p_own, p_own, across)
    send(m_p[1], p_own, p_own, sibling)
    gq.step(1)
    arrive(m_vx, vx.at[1], partner)
    vf[...] = vx[is_far].astype(jnp.float32)
    for n in range(WIDTH // LANES):
        lg_row = vf[0, n:n + 1, :]
        lgc[n * LANES:(n + 1) * LANES, :] = jnp.transpose(jnp.broadcast_to(lg_row, (LANES, LANES)))
    relay_y(4)
    arrive(m_p[0], p_far, across)
    send(m_p[2], p_far, p_far, sibling)
    gq.step(2)
    for s in range(5):
        finish_y(s)

    arrive(m_p[1], p.at[x * 2 + 1 - c], sibling)
    arrive(m_p[2], p.at[(1 - x) * 2 + 1 - c], sibling)
    eigen = sum(
        jnp.dot(p[n], flat(fa[n // 2, n % 2 * 4:n % 2 * 4 + 4]), preferred_element_type=jnp.float32)
        for n in range(4)
    )
    lg_col = jnp.concatenate([lgc[pl.ds(pl.multiple_of(bx * HALF + (z * 2 + bc) * STRIP, PIECE), STRIP), :]
                              for bc in range(2) for bx in range(2)])
    for n in range(QUARTER // LANES):
        la_row = vf[1, pl.ds((x * 2 + c) * (QUARTER // LANES) + n, 1), :]
        cols = slice(n * LANES, (n + 1) * LANES)
        sc[:, cols] = (eigen[:, cols] / (lg_col * la_row + DAMPING)).astype(jnp.bfloat16)

    for bx in range(2):
        for n in range(2):
            part = lax.dot_general(
                sc[...], flat(fa[bx, n * 4:n * 4 + 4]), (((1,), (1,)), ((), ())), preferred_element_type=jnp.float32
            ).reshape((2, 2, STRIP, QUARTER))
            cols = slice(bx * HALF + n * QUARTER, bx * HALF + (n + 1) * QUARTER)
            bp[:, :, :, cols] = part
            bo[:, :, :, cols] = part.astype(jnp.bfloat16)
    m_b = number()
    send(m_b, bo.at[1 - c], bi, sibling)
    arrive(m_b, bi, sibling)
    done = (bp[c] + bi[...].astype(jnp.float32)).astype(jnp.bfloat16)
    for j in range(WIDTH // LANES):
        bk[j] = done[:, :, j * LANES:(j + 1) * LANES]

    for wx in range(2):
        for wz in range(NZ):
            if (wz + 2 * wx) % 4 == 3:
                continue
            part = bk.at[wx * 6 + wz - (wz + 2 * wx) // 4]
            to_self = jnp.logical_and(x == wx, z == wz)
            others = jnp.logical_not(to_self)
            started = pltpu.make_async_remote_copy(
                src_ref=part, dst_ref=bc.at[x, :, strip_of(z), :], send_sem=ssem.at[number()],
                recv_sem=b_recv.at[x * NZ + z], device_id=dev(xh, y, wx, wz, c), device_id_type=MESH,
            )
            pl.when(others)(started.start)
            pending.append((started, others))

            @pl.when(to_self)
            def _():
                bc[x, :, strip_of(z), :] = part[...]

    gq.step(3)
    gq.last()
    is_worker = works(x, z)
    m_bt = number()

    @pl.when(is_worker)
    def _():
        def take(k, carry):
            n = (x * NZ + z + k) % 16
            block = bc.at[n // NZ, :, strip_of(n % NZ), :]
            pltpu.make_async_remote_copy(
                src_ref=block, dst_ref=block, send_sem=ssem.at[m_bt], recv_sem=b_recv.at[n],
                device_id=sibling, device_id_type=MESH,
            ).wait_recv()
            return carry

        lax.fori_loop(1, 16, take, 0)
        total = flat(bc[0].astype(jnp.float32) + bc[1].astype(jnp.float32))
        for n in range(HALF // LANES):
            cols = slice(n * LANES, (n + 1) * LANES)
            bt[c, :, cols] = jnp.transpose(total[cols, :]).astype(jnp.bfloat16)

    send(m_bt, bt.at[c], bt.at[c], sibling, is_worker)
    arrive(m_bt, bt.at[1 - c], sibling, is_worker)

    mine = pl.ds(pl.multiple_of(rank(x, z) * LANES, LANES), LANES)

    def finish(n):
        @pl.when(is_worker)
        def _():
            rows = pl.ds(pl.multiple_of(c * HALF + n * QUARTER, LANES), QUARTER)
            part = sum(
                jnp.dot(bt[k], flat(fq[k, :, :, rows]), preferred_element_type=jnp.float32) for k in range(2)
            )
            out_ref[rows, mine] = jnp.transpose(part).astype(jnp.bfloat16)

    finish(0)
    go.begin_low()
    finish(1)
    go.begin_high()
    drain()
    go.swap()
    go.step(1)
    early = len(pending)
    go.step(2)
    go.step(3)
    drain(early)
    go.last()
    go.end()
    drain()


def local(gradient_tiles, qa_basis, qg_basis, qa_values, qg_values, layer_owner, block_assign):
    strip = (STRIP, WIDTH)
    bf = jnp.bfloat16
    f32 = jnp.float32
    out = pl.pallas_call(
        kernel,
        out_shape=jax.ShapeDtypeStruct((WIDTH, WIDTH), bf),
        in_specs=[pl.BlockSpec(memory_space=pltpu.HBM)] * 7,
        out_specs=pl.BlockSpec(memory_space=pltpu.VMEM),
        scratch_shapes=[
            pltpu.SMEM((2,), jnp.int32),
            pltpu.SMEM((2, 4), jnp.int32),
            pltpu.VMEM((2, 16, WIDTH), bf),
            pltpu.VMEM((2, WIDTH), bf),
            pltpu.VMEM((4, STRIP, QUARTER), bf),
            pltpu.VMEM((4, 2, STRIP, QUARTER), bf),
            pltpu.VMEM((2, 16) + strip, bf),
            pltpu.VMEM((2, 4) + strip, bf),
            pltpu.VMEM((2, 2, STRIP, HALF), bf),
            pltpu.VMEM((2, 2, STRIP, HALF), bf),
            pltpu.VMEM((2, 2, STRIP, HALF), bf),
            pltpu.VMEM((2, 3) + strip, bf),
            pltpu.VMEM((2, STRIP, HALF), bf),
            pltpu.VMEM((2, STRIP, HALF), bf),
            pltpu.VMEM((2, STRIP, HALF), bf),
            pltpu.VMEM((4, 2, STRIP, QUARTER), bf),
            pltpu.VMEM((STRIP, QUARTER), bf),
            pltpu.VMEM((2, STRIP, QUARTER), bf),
            pltpu.VMEM((4, 2, 2, 16, LANES), f32),
            pltpu.VMEM((4, 2, 2, 16, LANES), bf),
            pltpu.VMEM((4, 2, 2, 16, LANES), bf),
            pltpu.VMEM((2, 2, 16, LANES), bf),
            pltpu.VMEM((2, 16, LANES), bf),
            pltpu.VMEM((2, 16, LANES), f32),
            pltpu.VMEM((2, HALF, QUARTER), bf),
            pltpu.VMEM((2, NZ, 2, STRIP, QUARTER), bf),
            pltpu.VMEM((2, 2, HALF // 2, WIDTH), bf),
            pltpu.VMEM((4, 4 * STRIP, QUARTER), bf),
            pltpu.VMEM((WIDTH, LANES), f32),
            pltpu.VMEM((4 * STRIP, QUARTER), bf),
            pltpu.VMEM((2, 2) + strip, f32),
            pltpu.VMEM((2, 2) + strip, bf),
            pltpu.VMEM((2,) + strip, bf),
            pltpu.VMEM((12, 2, STRIP, LANES), bf),
            pltpu.VMEM((2, 2, HALF // 2, LANES), bf),
            pltpu.VMEM((2, LANES, HALF), bf),
            pltpu.SemaphoreType.DMA((N_SEM,)),
            pltpu.SemaphoreType.DMA((N_SEM,)),
            pltpu.SemaphoreType.DMA((15,)),
            pltpu.SemaphoreType.DMA((4,)),
            pltpu.SemaphoreType.DMA((16,)),
        ],
        compiler_params=pltpu.CompilerParams(
            collective_id=0, has_side_effects=True, vmem_limit_bytes=48 * 1024 * 1024
        ),
        cost_estimate=pl.CostEstimate(flops=4 * 2 * 48 * 1536 * 1536, bytes_accessed=10_000_000, transcendentals=0),
    )(
        *(
            pltpu.with_memory_space_constraint(operand, pltpu.HBM)
            for operand in (
                layer_owner, block_assign, gradient_tiles[0], qa_basis[0], jnp.swapaxes(qg_basis[0], -1, -2),
                qg_values[0], qa_values[0],
            )
        )
    )
    return out[None]


def solution(mesh):
    in_specs = (
        P("grp", "dp", None),
        P("grp", None, "dp", None),
        P("grp", None, None, None, "dp"),
        P("grp", None, None),
        P("grp", None, None, None),
        P(),
        P(),
    )
    out_specs = P("grp", None, None)
    return jax.shard_map(local, mesh=mesh, in_specs=in_specs, out_specs=out_specs, check_vma=False)
```

```python
import functools

import jax
import jax.numpy as jnp
from jax import lax
from jax.experimental import pallas as pl
from jax.experimental.pallas import tpu as pltpu
from jax.sharding import PartitionSpec as P

MESH = pl.DeviceIdType.MESH
DAMPING = 0.1
NZ = 8
STRIP = 48
PIECE = 16
WIDTH = 1536
LANES = 128
N_DP = 32
HALF = WIDTH // 2
QUARTER = WIDTH // 4
TILE = 256
N_SEM = 320


def works(x, z):
    return (z + 2 * x) % 4 != 3


def rank(x, z):
    return x * 6 + z - (z + 2 * x) // 4


def kernel(
    owner_hbm, assign_hbm, g_hbm, a_hbm, q_hbm, lg_hbm, la_hbm, out_ref,
    owner_ref, assign_ref, lgv, lav, g, av, qv, qsel, qr_low, qr_high, qs, qt, qx_low, qx_high, qc, aq, ac, ax, vsel, vsb, vy, vx, vc, vf, fg, fa, fq, p, lgc, sc, bp, bo, bi, bk, bc, bt,
    ssem, rsem, lsem, a_recv, b_recv,
):
    member = lax.axis_index("grp")
    dp = lax.axis_index("dp")
    xh, y = member // 4, member % 4
    x, z, c = dp // 16, (dp // 2) % NZ, dp % 2

    load_g = [
        pltpu.make_async_copy(g_hbm.at[:, n * QUARTER:(n + 1) * QUARTER], g.at[n], lsem.at[7 + n]) for n in range(4)
    ]
    load_a = [
        pltpu.make_async_copy(a_hbm.at[:, :, n * QUARTER:(n + 1) * QUARTER], av.at[n], lsem.at[11 + n])
        for n in range(4)
    ]
    load_q = pltpu.make_async_copy(q_hbm, qv, lsem.at[2])
    loads = [
        pltpu.make_async_copy(src, dst, lsem.at[3 + n])
        for n, (src, dst) in enumerate(
            ((owner_hbm, owner_ref), (assign_hbm, assign_ref), (lg_hbm, lgv), (la_hbm, lav))
        )
    ]
    for load in load_a:
        load.start()
    for load in load_g:
        load.start()
    for load in loads:
        load.start()
    load_q.start()
    core0 = c == 0

    def dp_of(dx, dz, dc):
        return dx * 16 + dz * 2 + dc

    def dev(gx, gy, dx, dz, dc):
        return (gx * 4 + gy, dp_of(dx, dz, dc))

    sibling = dev(xh, y, x, z, 1 - c)
    across = dev(xh, y, 1 - x, z, c)
    up = dev(xh, y, x, (z + 1) % NZ, c)
    down = dev(xh, y, x, (z + NZ - 1) % NZ, c)
    partner = dev(1 - xh, y, x, z, c)

    barrier = pltpu.get_barrier_semaphore()

    near = [up, down, partner]
    near += [
        dev(xh, (y + k // 4) % 4, (x + k // 2) % 2, z, (c + k) % 2) for k in range(1, 16)
    ]
    for target in near:
        pl.semaphore_signal(barrier, inc=1, device_id=target, device_id_type=MESH)

    y_up, y_down = (xh * 4 + (y + 1) % 4, dp), (xh * 4 + (y + 3) % 4, dp)
    far, above, below = (y + 2) % 4, (y + 1) % 4, (y + 3) % 4
    for load in load_a:
        load.wait()
    for load in load_g:
        load.wait()
    for load in loads:
        load.wait()
    owner = owner_ref[xh]
    other = owner_ref[1 - xh]
    is_far = lax.bitwise_xor(lax.shift_right_logical(owner, 2), xh)
    owner_y = lax.bitwise_and(owner, 3)
    other_y = lax.bitwise_and(other, 3)
    load_q.wait()
    for layer in range(2):
        for slot in range(4):
            qsel[layer, slot] = qv[layer, assign_ref[layer, slot]]
    for layer in range(2):
        qr_low[layer, 0] = qsel[layer, above, :, :HALF]
        qr_high[layer, 0] = qsel[layer, below, :, HALF:]
        qt[layer, 0] = qsel[layer, y]
    for layer in range(2):
        la_all = lav[...].astype(jnp.float32)[layer:layer + 1]
        lg_all = lgv[layer].astype(jnp.float32)
        at_row = lax.broadcasted_iota(jnp.int32, lg_all.shape, 0)
        for slot in range(4):
            lg = jnp.sum(jnp.where(at_row == assign_ref[layer, slot], lg_all, 0.0), axis=0, keepdims=True)
            for n in range(WIDTH // LANES):
                cols = slice(n * LANES, (n + 1) * LANES)
                vsel[slot, layer, 0, n:n + 1] = lg[:, cols]
                vsel[slot, layer, 1, n:n + 1] = la_all[:, cols]
    vsb[...] = vsel[...].astype(jnp.bfloat16)
    vy[y] = vsb[y]

    pl.semaphore_wait(barrier, len(near))

    count = [0]
    pending = []

    def number():
        count[0] += 1
        assert count[0] <= N_SEM
        return count[0] - 1

    def copy(m, src, dst, target):
        return pltpu.make_async_remote_copy(
            src_ref=src, dst_ref=dst, send_sem=ssem.at[m], recv_sem=rsem.at[m],
            device_id=target, device_id_type=MESH,
        )

    def send(m, src, dst, target, when=None):
        started = copy(m, src, dst, target)
        pending.append((started, when))
        if when is None:
            started.start()
        else:
            pl.when(when)(started.start)

    def drain(until=None):
        for started, when in pending[:until]:
            if when is None:
                started.wait_send()
            else:
                pl.when(when)(started.wait_send)
        del pending[:until]

    def arrive(m, dst, target, when=None):
        landed = copy(m, dst, dst, target)
        if when is None:
            landed.wait_recv()
        else:
            pl.when(when)(landed.wait_recv)

    class Gather:
        def __init__(self, ref, full, exists=None, alone=False):
            self.ref, self.full, self.cut, self.mid = ref, full, full // 2, 2 * LANES if alone else full // 4
            self.alone = alone
            self.exists = exists or (lambda bx, bz: None)
            self.sib_waits = []
            self.m = {}

        def key(self, *name):
            if name not in self.m:
                self.m[name] = number()
            return self.m[name]

        def to_sibling(self, bx, bz):
            if self.alone:
                return
            m = number()
            ref = self.ref(bx, bz, c, 0, self.full)
            send(m, ref, ref, sibling, self.exists(bx, bz))
            self.sib_waits.append((m, self.ref(bx, bz, 1 - c, 0, self.full), self.exists(bx, bz)))

        def move(self, name, target, bx, bz, first, last):
            ref = self.ref(bx, bz, c, first, last)
            send(self.key(*name), ref, ref, target, self.exists(bx, bz))

        def wait(self, name, bx, bz, first, last, bc=c):
            arrive(self.key(*name), self.ref(bx, bz, bc, first, last), sibling, self.exists(bx, bz))

        def low(self, name, target, bx, bz):
            self.move(name, target, bx, bz, 0, self.cut)

        def high(self, name, target, bx, bz):
            self.move(name, target, bx, bz, self.cut, self.full)

        def wait_low(self, name, bx, bz):
            self.wait(name, bx, bz, 0, self.cut)

        def wait_high(self, name, bx, bz):
            self.wait(name, bx, bz, self.cut, self.full)

        def begin_low(self):
            self.low(("x", 0), across, x, z)
            self.low(("ul", 1), up, x, z)
            self.low(("dl", 1), down, x, z)

        def begin_high(self):
            self.high(("xh", 0), across, x, z)
            self.high(("uh", 1), up, x, z)
            self.high(("dh", 1), down, x, z)
            self.to_sibling(x, z)

        def swap(self):
            self.wait_low(("x", 0), 1 - x, z)
            self.low(("uq", 1), up, 1 - x, z)
            self.low(("dq", 1), down, 1 - x, z)

        def from_x(self):
            self.wait_high(("xh", 0), 1 - x, z)
            self.to_sibling(1 - x, z)

        def step(self, s):
            lo, hi = (z + NZ - s) % NZ, (z + s) % NZ
            self.wait_high(("uh", s), x, lo)
            self.high(("uh", s + 1), up, x, lo)
            self.high(("xu", s), across, x, lo)
            self.wait_high(("dh", s), x, hi)
            if s < 3:
                self.high(("dh", s + 1), down, x, hi)
            self.high(("xd", s), across, x, hi)
            self.wait_low(("ul", s), x, lo)
            if s < 3:
                self.low(("ul", s + 1), up, x, lo)
            self.wait_low(("dl", s), x, hi)
            self.low(("dl", s + 1), down, x, hi)
            self.wait_low(("uq", s), 1 - x, lo)
            if s < 3:
                self.low(("uq", s + 1), up, 1 - x, lo)
            else:
                self.move(("uq", 4), up, 1 - x, lo, 0, self.mid)
            self.wait_low(("dq", s), 1 - x, hi)
            if s < 3:
                self.low(("dq", s + 1), down, 1 - x, hi)
            else:
                self.move(("dq", 4), down, 1 - x, hi, self.mid, self.cut)
            self.to_sibling(x, lo)
            self.to_sibling(x, hi)
            if s == 2 and not self.alone:
                self.from_x()
            if s > 1:
                self.crossed(s - 1)

        def crossed(self, s):
            lo, hi = (z + NZ - s) % NZ, (z + s) % NZ
            self.wait_high(("xu", s), 1 - x, lo)
            self.to_sibling(1 - x, lo)
            self.wait_high(("xd", s), 1 - x, hi)
            self.to_sibling(1 - x, hi)

        def last(self):
            far = (z + 4) % NZ
            self.wait_high(("uh", 4), x, far)
            self.high(("xu", 4), across, x, far)
            self.wait_low(("dl", 4), x, far)
            self.to_sibling(x, far)
            self.crossed(3)
            self.wait(("uq", 4), 1 - x, far, 0, self.mid)
            self.wait(("dq", 4), 1 - x, far, self.mid, self.cut)
            self.wait_high(("xu", 4), 1 - x, far)
            self.to_sibling(1 - x, far)

        def end(self):
            for m, ref, when in self.sib_waits:
                arrive(m, ref, sibling, when)

    def strip_at(bz, bc):
        return pl.ds(pl.multiple_of((bz * 2 + bc) * STRIP, PIECE), STRIP)

    def strip_of(bz):
        return pl.ds(pl.multiple_of(bz * STRIP, PIECE), STRIP)

    def at_z(bz):
        return pl.ds(pl.multiple_of(bz * 2 * STRIP, PIECE), 2 * STRIP)

    class Ring:
        def __init__(self, f):
            self.f = f
            self.m = {}
            self.m4 = [number() for _ in range(3)]

        def share(self, strip):
            self.f[x, strip_at(z, c), :] = strip[x * 2 + c]
            for n, (dx, dc) in enumerate(((1, 0), (1, 1), (0, 1))):
                bx, bc = (x + dx) % 2, (c + dc) % 2
                send(self.m4[n], strip.at[bx * 2 + bc], self.f.at[x, strip_at(z, c), :], dev(xh, y, bx, z, bc))

        def begin(self):
            for n, (dx, dc) in enumerate(((1, 0), (1, 1), (0, 1))):
                bx, bc = (x + dx) % 2, (c + dc) % 2
                arrive(self.m4[n], self.f.at[bx, strip_at(z, bc), :], sibling)
            for n in range(2):
                self.move("u", 1, n, up, z)
                self.move("d", 1, n, down, z)

        def move(self, way, s, n, target, bz):
            ref = self.f.at[n, at_z(bz), :]
            self.m[way, s, n] = number()
            send(self.m[way, s, n], ref, ref, target)

        def wait(self, way, s, n, bz):
            arrive(self.m[way, s, n], self.f.at[n, at_z(bz), :], sibling)

        def step(self, s):
            lo, hi = (z + NZ - s) % NZ, (z + s) % NZ
            for n in range(2):
                self.wait("u", s, n, lo)
                if s < 3 or n == 0:
                    self.move("u", s + 1, n, up, lo)
                self.wait("d", s, n, hi)
                if s < 3 or n == 1:
                    self.move("d", s + 1, n, down, hi)

        def last(self):
            far = (z + 4) % NZ
            self.wait("u", 4, 0, far)
            self.wait("d", 4, 1, far)

    def by_strips(bx, bz, bc, first, last):
        cols = pl.ds(pl.multiple_of(bc * HALF + first, LANES), last - first)
        return fq.at[:, bx, strip_of(bz), cols]

    def by_columns(bx, bz, bc, first, last):
        cols = pl.ds(pl.multiple_of(rank(bx, bz) * LANES, LANES), LANES)
        return out_ref.at[pl.ds(pl.multiple_of(bc * HALF + first, PIECE), last - first), cols]

    gg = Ring(fg)
    gq = Gather(by_strips, HALF, alone=True)
    go = Gather(by_columns, HALF, exists=lambda bx, bz: works(bx, bz))

    own = pl.ds(pl.multiple_of(dp * STRIP, PIECE), STRIP)

    mine_a = x * 2 + c
    in_place = mine_a == y
    for n in range(4):
        started = pltpu.make_async_remote_copy(
            src_ref=av.at[n], dst_ref=aq.at[y], send_sem=ssem.at[number()], recv_sem=a_recv.at[y],
            device_id=(xh * 4 + mine_a, dp_of(n // 2, z, n % 2)), device_id_type=MESH,
        )
        there = jnp.logical_not(jnp.logical_and(in_place, y == n))
        pl.when(there)(started.start)
        pending.append((started, there))

    @pl.when(in_place)
    def _():
        aq[y] = av[y]

    gg.share(g)

    m_q1, m_q2, m_q3 = ([number() for _ in range(2)] for _ in range(3))
    send(m_q1[0], qsel.at[:, far, :, :HALF], qr_low.at[:, 1], y_up)
    send(m_q1[1], qsel.at[:, far, :, HALF:], qr_high.at[:, 1], y_down)
    send(m_q3[0], qsel.at[:, above, :, HALF:], qt.at[:, 1, :, HALF:], y_up)
    send(m_q3[1], qsel.at[:, below, :, :HALF], qt.at[:, 2, :, :HALF], y_down)
    gg.begin()

    owners_y = [lax.bitwise_and(owner_ref[layer], 3) for layer in range(2)]

    def one_if(condition):
        return jnp.where(condition, 1, 0)

    arrive(m_q1[0], qr_low.at[:, 1], y_down)
    for layer in range(2):
        qs[0, layer] = qr_low[layer, one_if(owners_y[layer] == below)]
    send(m_q2[0], qs.at[0], qt.at[:, 1, :, :HALF], y_up)
    arrive(m_q1[1], qr_high.at[:, 1], y_up)
    for layer in range(2):
        qs[1, layer] = qr_high[layer, one_if(owners_y[layer] == above)]
    send(m_q2[1], qs.at[1], qt.at[:, 2, :, HALF:], y_down)

    for k in range(1, 4):
        m_a = (y + k) % 4
        pltpu.make_async_remote_copy(
            src_ref=aq.at[m_a], dst_ref=aq.at[m_a], send_sem=ssem.at[0], recv_sem=a_recv.at[m_a],
            device_id=sibling, device_id_type=MESH,
        ).wait_recv()

    @pl.when(jnp.logical_not(in_place))
    def _():
        pltpu.make_async_remote_copy(
            src_ref=aq.at[y], dst_ref=aq.at[y], send_sem=ssem.at[0], recv_sem=a_recv.at[y],
            device_id=sibling, device_id_type=MESH,
        ).wait_recv()

    m_ax = number()
    ac[...] = aq[other_y, 1 - xh]
    send(m_ax, ac, ax.at[1], partner)
    ax[0] = aq[owner_y, xh]

    m_vy = [number() for _ in range(3)]
    for k in range(1, 4):
        to = (y + k) % 4
        send(m_vy[k - 1], vsb.at[to], vy.at[y], (xh * 4 + to, dp))
    gg.step(1)
    arrive(m_ax, ax.at[1], partner)
    fa[y // 2, z, y % 2] = ax[is_far]
    m_a = {}

    def ring_a(way, s, bz):
        ref = fa.at[y // 2, bz, y % 2]
        m_a[way, s] = number()
        send(m_a[way, s], ref, ref, up if way == "u" else down)

    def step_a(s):
        lo, hi = (z + NZ - s) % NZ, (z + s) % NZ
        arrive(m_a["u", s], fa.at[y // 2, lo, y % 2], sibling)
        if s < 4:
            ring_a("u", s + 1, lo)
            arrive(m_a["d", s], fa.at[y // 2, hi, y % 2], sibling)
        if s < 3:
            ring_a("d", s + 1, hi)

    def blocks_a(s):
        lo, hi = (z + NZ - s) % NZ, (z + s) % NZ
        return (lo,) if s in (0, 4) else (lo, hi)

    m_y = {}

    def move_y(name, s, n, target, ref):
        m_y[name, s, n] = number()
        send(m_y[name, s, n], ref, ref, target)

    def cross_y(s):
        for n, bz in enumerate(blocks_a(s)):
            ref = fa.at[y // 2, bz, y % 2]
            move_y("u", s, n, y_up, ref)
            move_y("d", s, n, y_down, ref)

    def relay_y(s):
        for n, bz in enumerate(blocks_a(s)):
            from_below, from_above = fa.at[below // 2, bz, below % 2], fa.at[above // 2, bz, above % 2]
            arrive(m_y["u", s, n], from_below, sibling)
            if n == 0:
                move_y("f", s, n, y_up, from_below)
            arrive(m_y["d", s, n], from_above, sibling)
            if n == 1:
                move_y("f", s, n, y_down, from_above)

    def finish_y(s):
        for n, bz in enumerate(blocks_a(s)):
            arrive(m_y["f", s, n], fa.at[far // 2, bz, far % 2], sibling)

    ring_a("u", 1, z)
    ring_a("d", 1, z)
    cross_y(0)

    arrive(m_q3[0], qt.at[:, 1, :, HALF:], y_down)
    arrive(m_q3[1], qt.at[:, 2, :, :HALF], y_up)
    arrive(m_q2[0], qt.at[:, 1, :, :HALF], y_down)
    arrive(m_q2[1], qt.at[:, 2, :, HALF:], y_up)
    for k in range(1, 4):
        arrive(m_vy[k - 1], vy.at[(y + 4 - k) % 4], partner)

    def came(layer, column_half):
        away = lax.bitwise_and(lax.bitwise_and(owner_ref[layer], 3) + 4 - y, 3)
        by_below = (away >= 2) if column_half == 0 else (away == 3)
        return jnp.where(away == 0, 0, jnp.where(by_below, 1, 2))

    m_qx, m_vx = [number() for _ in range(2)], number()
    for n in range(2):
        half = slice(n * HALF, (n + 1) * HALF)
        qc[n] = qt[1 - xh, came(1 - xh, n), :, half]
        send(m_qx[n], qc.at[n], (qx_low, qx_high)[n].at[1], partner)
    vc[...] = vy[other_y, 1 - xh]
    send(m_vx, vc, vx.at[1], partner)
    for n in range(2):
        half = slice(n * HALF, (n + 1) * HALF)
        (qx_low, qx_high)[n][0] = qt[xh, came(xh, n), :, half]
    vx[0] = vy[owner_y, xh]
    gg.step(2)

    step_a(1)
    cross_y(1)
    gg.step(3)
    relay_y(0)
    step_a(2)
    cross_y(2)
    relay_y(1)
    m_s = [number() for _ in range(3)]
    for n, strip_half in enumerate((qx_low, qx_high)):
        arrive(m_qx[n], strip_half.at[1], partner)
        cols = slice(n * HALF, (n + 1) * HALF)
        fq[c, x, strip_of(z), cols] = strip_half[is_far]
        part = fq.at[c, x, strip_of(z), cols]
        send(m_s[n], part, part, sibling)
    for n in range(2):
        arrive(m_s[n], fq.at[1 - c, x, strip_of(z), n * HALF:(n + 1) * HALF], sibling)
    gq.begin_low()
    gq.begin_high()
    step_a(3)
    cross_y(3)
    gq.swap()
    step_a(4)
    cross_y(4)
    relay_y(2)
    gq.from_x()
    came_over = by_strips(1 - x, z, c, 0, HALF)
    send(m_s[2], came_over, came_over, sibling)
    gg.last()
    relay_y(3)
    gq.step(1)

    arrive(m_s[2], by_strips(1 - x, z, 1 - c, 0, HALF), sibling)

    def flat(value):
        return value.reshape((-1, value.shape[-1]))

    p[x * 2 + c] = jnp.dot(
        flat(fq[:, :, strip_of(z), :]), flat(fg[...]), preferred_element_type=jnp.float32
    ).astype(jnp.bfloat16)
    m_p = [number() for _ in range(3)]
    p_own, p_far = p.at[x * 2 + c], p.at[(1 - x) * 2 + c]
    send(m_p[0], p_own, p_own, across)
    send(m_p[1], p_own, p_own, sibling)
    arrive(m_vx, vx.at[1], partner)
    vf[...] = vx[is_far].astype(jnp.float32)
    for n in range(WIDTH // LANES):
        lg_row = vf[0, n:n + 1, :]
        lgc[n * LANES:(n + 1) * LANES, :] = jnp.transpose(jnp.broadcast_to(lg_row, (LANES, LANES)))
    relay_y(4)
    arrive(m_p[0], p_far, across)
    send(m_p[2], p_far, p_far, sibling)
    gq.step(2)
    for s in range(5):
        finish_y(s)

    arrive(m_p[1], p.at[x * 2 + 1 - c], sibling)
    arrive(m_p[2], p.at[(1 - x) * 2 + 1 - c], sibling)
    eigen = sum(
        jnp.dot(p[n], flat(fa[n // 2, n % 2 * 4:n % 2 * 4 + 4]), preferred_element_type=jnp.float32)
        for n in range(4)
    )
    lg_col = jnp.concatenate([lgc[pl.ds(pl.multiple_of(bx * HALF + (z * 2 + bc) * STRIP, PIECE), STRIP), :]
                              for bc in range(2) for bx in range(2)])
    for n in range(QUARTER // LANES):
        la_row = vf[1, pl.ds((x * 2 + c) * (QUARTER // LANES) + n, 1), :]
        cols = slice(n * LANES, (n + 1) * LANES)
        sc[:, cols] = (eigen[:, cols] / (lg_col * la_row + DAMPING)).astype(jnp.bfloat16)

    for bx in range(2):
        for n in range(2):
            part = lax.dot_general(
                sc[...], flat(fa[bx, n * 4:n * 4 + 4]), (((1,), (1,)), ((), ())), preferred_element_type=jnp.float32
            ).reshape((2, 2, STRIP, QUARTER))
            cols = slice(bx * HALF + n * QUARTER, bx * HALF + (n + 1) * QUARTER)
            bp[:, :, :, cols] = part
            bo[:, :, :, cols] = part.astype(jnp.bfloat16)
    m_b = number()
    send(m_b, bo.at[1 - c], bi, sibling)
    gq.step(3)
    arrive(m_b, bi, sibling)
    done = (bp[c] + bi[...].astype(jnp.float32)).astype(jnp.bfloat16)
    for j in range(WIDTH // LANES):
        bk[j] = done[:, :, j * LANES:(j + 1) * LANES]

    for wx in range(2):
        for wz in range(NZ):
            if (wz + 2 * wx) % 4 == 3:
                continue
            part = bk.at[wx * 6 + wz - (wz + 2 * wx) // 4]
            to_self = jnp.logical_and(x == wx, z == wz)
            others = jnp.logical_not(to_self)
            started = pltpu.make_async_remote_copy(
                src_ref=part, dst_ref=bc.at[x, :, strip_of(z), :], send_sem=ssem.at[number()],
                recv_sem=b_recv.at[x * NZ + z], device_id=dev(xh, y, wx, wz, c), device_id_type=MESH,
            )
            pl.when(others)(started.start)
            pending.append((started, others))

            @pl.when(to_self)
            def _():
                bc[x, :, strip_of(z), :] = part[...]

    gq.last()
    is_worker = works(x, z)
    m_bt = number()

    @pl.when(is_worker)
    def _():
        def take(k, carry):
            n = (x * NZ + z + k) % 16
            block = bc.at[n // NZ, :, strip_of(n % NZ), :]
            pltpu.make_async_remote_copy(
                src_ref=block, dst_ref=block, send_sem=ssem.at[m_bt], recv_sem=b_recv.at[n],
                device_id=sibling, device_id_type=MESH,
            ).wait_recv()
            return carry

        lax.fori_loop(1, 16, take, 0)
        total = flat(bc[0].astype(jnp.float32) + bc[1].astype(jnp.float32))
        for n in range(HALF // LANES):
            cols = slice(n * LANES, (n + 1) * LANES)
            bt[c, :, cols] = jnp.transpose(total[cols, :]).astype(jnp.bfloat16)

    send(m_bt, bt.at[c], bt.at[c], sibling, is_worker)
    arrive(m_bt, bt.at[1 - c], sibling, is_worker)

    mine = pl.ds(pl.multiple_of(rank(x, z) * LANES, LANES), LANES)

    def finish(n):
        @pl.when(is_worker)
        def _():
            rows = pl.ds(pl.multiple_of(c * HALF + n * QUARTER, LANES), QUARTER)
            part = sum(
                jnp.dot(bt[k], flat(fq[k, :, :, rows]), preferred_element_type=jnp.float32) for k in range(2)
            )
            out_ref[rows, mine] = jnp.transpose(part).astype(jnp.bfloat16)

    finish(0)
    go.begin_low()
    finish(1)
    go.begin_high()
    drain()
    go.swap()
    go.step(1)
    early = len(pending)
    go.step(2)
    go.step(3)
    drain(early)
    go.last()
    go.end()
    drain()


def local(gradient_tiles, qa_basis, qg_basis, qa_values, qg_values, layer_owner, block_assign):
    strip = (STRIP, WIDTH)
    bf = jnp.bfloat16
    f32 = jnp.float32
    out = pl.pallas_call(
        kernel,
        out_shape=jax.ShapeDtypeStruct((WIDTH, WIDTH), bf),
        in_specs=[pl.BlockSpec(memory_space=pltpu.HBM)] * 7,
        out_specs=pl.BlockSpec(memory_space=pltpu.VMEM),
        scratch_shapes=[
            pltpu.SMEM((2,), jnp.int32),
            pltpu.SMEM((2, 4), jnp.int32),
            pltpu.VMEM((2, 16, WIDTH), bf),
            pltpu.VMEM((2, WIDTH), bf),
            pltpu.VMEM((4, STRIP, QUARTER), bf),
            pltpu.VMEM((4, 2, STRIP, QUARTER), bf),
            pltpu.VMEM((2, 16) + strip, bf),
            pltpu.VMEM((2, 4) + strip, bf),
            pltpu.VMEM((2, 2, STRIP, HALF), bf),
            pltpu.VMEM((2, 2, STRIP, HALF), bf),
            pltpu.VMEM((2, 2, STRIP, HALF), bf),
            pltpu.VMEM((2, 3) + strip, bf),
            pltpu.VMEM((2, STRIP, HALF), bf),
            pltpu.VMEM((2, STRIP, HALF), bf),
            pltpu.VMEM((2, STRIP, HALF), bf),
            pltpu.VMEM((4, 2, STRIP, QUARTER), bf),
            pltpu.VMEM((STRIP, QUARTER), bf),
            pltpu.VMEM((2, STRIP, QUARTER), bf),
            pltpu.VMEM((4, 2, 2, 16, LANES), f32),
            pltpu.VMEM((4, 2, 2, 16, LANES), bf),
            pltpu.VMEM((4, 2, 2, 16, LANES), bf),
            pltpu.VMEM((2, 2, 16, LANES), bf),
            pltpu.VMEM((2, 16, LANES), bf),
            pltpu.VMEM((2, 16, LANES), f32),
            pltpu.VMEM((2, HALF, QUARTER), bf),
            pltpu.VMEM((2, NZ, 2, STRIP, QUARTER), bf),
            pltpu.VMEM((2, 2, HALF // 2, WIDTH), bf),
            pltpu.VMEM((4, 4 * STRIP, QUARTER), bf),
            pltpu.VMEM((WIDTH, LANES), f32),
            pltpu.VMEM((4 * STRIP, QUARTER), bf),
            pltpu.VMEM((2, 2) + strip, f32),
            pltpu.VMEM((2, 2) + strip, bf),
            pltpu.VMEM((2,) + strip, bf),
            pltpu.VMEM((12, 2, STRIP, LANES), bf),
            pltpu.VMEM((2, 2, HALF // 2, LANES), bf),
            pltpu.VMEM((2, LANES, HALF), bf),
            pltpu.SemaphoreType.DMA((N_SEM,)),
            pltpu.SemaphoreType.DMA((N_SEM,)),
            pltpu.SemaphoreType.DMA((15,)),
            pltpu.SemaphoreType.DMA((4,)),
            pltpu.SemaphoreType.DMA((16,)),
        ],
        compiler_params=pltpu.CompilerParams(
            collective_id=0, has_side_effects=True, vmem_limit_bytes=48 * 1024 * 1024
        ),
        cost_estimate=pl.CostEstimate(flops=4 * 2 * 48 * 1536 * 1536, bytes_accessed=10_000_000, transcendentals=0),
    )(
        *(
            pltpu.with_memory_space_constraint(operand, pltpu.HBM)
            for operand in (
                layer_owner, block_assign, gradient_tiles[0], qa_basis[0], jnp.swapaxes(qg_basis[0], -1, -2),
                qg_values[0], qa_values[0],
            )
        )
    )
    return out[None]


def solution(mesh):
    in_specs = (
        P("grp", "dp", None),
        P("grp", None, "dp", None),
        P("grp", None, None, None, "dp"),
        P("grp", None, None),
        P("grp", None, None, None),
        P(),
        P(),
    )
    out_specs = P("grp", None, None)
    return jax.shard_map(local, mesh=mesh, in_specs=in_specs, out_specs=out_specs, check_vma=False)
```
